128 devices in a mesh: blk: 32 (over y, x, core), head: 4 (over z).
Axes of the slice: x: 4, y: 4, z: 4, core: 2. Of those that a mesh axis runs over, the one named last changes fastest.
Arguments:
- tokens: bfloat16 [16384, 1536], P(('blk', 'head')), may hold values from -6 to 6
- seq_bounds: int32 [2], replicated, may hold values from 1 to 16383, as said below
- expert_ids: int32 [16384, 6], P(('blk', 'head')), may hold values from 0 to 7, all different within a row
- attn_gain: float32 [1536], P(('blk', 'head')), may hold values from 0.25 to 1.75
- qkv_weight: float32 [1536, 2560], P(('blk', 'head')), may hold values from -0.21875 to 0.21875
- out_weight: float32 [1536, 1536], P(None, ('blk', 'head')), may hold values from -1 to 1
- mlp_gain: float32 [1536], P(('blk', 'head')), may hold values from 0.25 to 1.75
- router_weight: float32 [1536, 8], P(('blk', 'head')), may hold values from -0.078125 to 0.078125
- expert_gate_up: float32 [8, 1536, 1024], P(None, ('blk', 'head')), may hold values from -0.15625 to 0.15625
- expert_down: float32 [8, 512, 1536], P(None, None, ('blk', 'head')), may hold values from -0.5 to 0.5
- shared_gate_up: float32 [1536, 2048], P(('blk', 'head')), may hold values from -0.15625 to 0.15625
- shared_down: float32 [1024, 1536], P(None, ('blk', 'head')), may hold values from -0.375 to 0.375
- out_cotangent: bfloat16 [16384, 1536], P(('blk', 'head')), may hold values from -6 to 6
Outputs:
- output: bfloat16 [16384, 1536], P(('blk', 'head'))
- tokens_grad: float32 [16384, 1536], P(('blk', 'head'))
- attn_gain_grad: float32 [1536], P(('blk', 'head'))
- qkv_weight_grad: float32 [1536, 2560], P(('blk', 'head'))
- out_weight_grad: float32 [1536, 1536], P(None, ('blk', 'head'))
- mlp_gain_grad: float32 [1536], P(('blk', 'head'))
- router_weight_grad: float32 [1536, 8], P(('blk', 'head'))
- expert_gate_up_grad: float32 [8, 1536, 1024], P(None, ('blk', 'head'))
- expert_down_grad: float32 [8, 512, 1536], P(None, None, ('blk', 'head'))
- shared_gate_up_grad: float32 [1536, 2048], P(('blk', 'head'))
- shared_down_grad: float32 [1024, 1536], P(None, ('blk', 'head'))
The draws below stay inside these ranges and needn't reach their ends.
Inputs may be any that keep to these rules, and one draw needn't show every extreme that they name: `seq_bounds`: the second sequence begins within the first 512 positions, and the third begins as many positions before the end as the second begins after the start. `expert_ids`: each row names 6 different experts; every expert is named by some row.
All inputs are finite; a program needn't handle non-finite values.
Results may differ from the reference program's by a relative error of at most 0.03.
Values may be sent and summed in bfloat16 or wider, within the bound.
A program may use at most 320 MiB of HBM per device.

```python
import jax
import jax.numpy as jnp
from jax import lax

D = 1536
HQ = 12
HK = 4
HD = 128
FE = 512
FS = 1024
EXPERTS = 8
TOPK = 6
QPG = 3
GROUP_W = 640
QKV = 2560
CYCLE_TOK = 512
TOKENS = 16384


def draw_seq_bounds(key, part):
    key = jax.random.fold_in(key, 7)
    opening = jax.random.randint(key, (1,), 1, CYCLE_TOK, dtype=jnp.int32)
    closing = TOKENS - opening
    return jnp.concatenate([opening, closing]).astype(jnp.int32)


def level_of(own_key, extent, shards, least, top_value):
    factor_of, own = 1.0, jax.random.fold_in(own_key, 6)
    for axis_at, shards_of in shards:
        heights = jnp.exp(jax.random.uniform(jax.random.fold_in(own, axis_at), (shards_of,), jnp.float32, least / len(shards), top_value / len(shards)))
        factor_of = factor_of * jnp.repeat(heights, extent[axis_at] // shards_of).reshape([-1 if axis == axis_at else 1 for axis in range(len(extent))])
    return factor_of


def distinct(stream_key, rows, number_of, top, lift):
    ranking = jax.random.permutation(jax.random.fold_in(stream_key, 1), number_of)
    boost = ranking
    for power in range(3):
        boost = boost * boost // number_of
    boost = boost * lift // number_of
    chance = jax.random.randint(jax.random.fold_in(stream_key, 2), (rows, number_of), 0, 4096) + boost
    fixed_rows = jax.random.permutation(jax.random.fold_in(stream_key, 3), rows)[jnp.arange(number_of) % rows]
    chance = jnp.where(jnp.arange(rows)[:, None] == fixed_rows[None, :], 1 << 14, chance)
    priority = chance * number_of + jnp.arange(number_of)
    return lax.top_k(priority.astype(jnp.int32), top)[1].astype(jnp.int32)


def normal_values(key, shape, width, bound, cuts=(), kind=jnp.bfloat16):
    factor_of = level_of(key, shape, cuts, -0.22, 0.18) if cuts else 1.0
    array = jax.random.normal(key, shape, jnp.float32) * width * factor_of
    return jnp.minimum(jnp.maximum(array, -bound), bound).astype(kind)


def setup_inputs(seed: int = 0) -> dict:
    seeds = jax.random.split(jax.random.key(seed), 14)
    tokens = normal_values(seeds[0], (TOKENS, D), 1.0, 6.0, ((0, 128),))
    seq_bounds = draw_seq_bounds(jax.random.fold_in(seeds[13], 71), 0)
    expert_ids = distinct(seeds[2], TOKENS, EXPERTS, TOPK, 6144)
    attn_gain = jnp.clip(1.0 + 0.15 * jax.random.normal(seeds[3], (D,), jnp.float32), 0.25, 1.75)
    qkv_weight = normal_values(seeds[4], (D, QKV), (D // 2) ** -0.5, 0.21875, ((0, 128),), jnp.float32)
    out_weight = normal_values(seeds[5], (HQ * HD, D), (HD // 4) ** -0.5, 1.0, ((1, 128),), jnp.float32)
    mlp_gain = jnp.clip(1.0 + 0.15 * jax.random.normal(seeds[6], (D,), jnp.float32), 0.25, 1.75)
    router_weight = normal_values(seeds[7], (D, EXPERTS), (4 * D) ** -0.5, 0.078125, ((0, 128),), jnp.float32)
    expert_gate_up = normal_values(seeds[8], (EXPERTS, D, 2 * FE), D ** -0.5, 0.15625, ((1, 128),), jnp.float32)
    expert_down = normal_values(seeds[9], (EXPERTS, FE, D), (FE // 4) ** -0.5, 0.5, ((2, 128),), jnp.float32)
    shared_gate_up = normal_values(seeds[10], (D, 2 * FS), D ** -0.5, 0.15625, ((0, 128),), jnp.float32)
    shared_down = normal_values(seeds[11], (FS, D), (FS // 4) ** -0.5, 0.375, ((1, 128),), jnp.float32)
    out_cotangent = normal_values(seeds[12], (TOKENS, D), 1.0, 6.0, ((0, 128),))
    return dict(tokens=tokens, seq_bounds=seq_bounds, expert_ids=expert_ids, attn_gain=attn_gain, qkv_weight=qkv_weight, out_weight=out_weight, mlp_gain=mlp_gain, router_weight=router_weight, expert_gate_up=expert_gate_up, expert_down=expert_down, shared_gate_up=shared_gate_up, shared_down=shared_down, out_cotangent=out_cotangent)


epsilon = 1e-05
masked_score = -1e+30
highest = lax.Precision.HIGHEST

@jax.custom_vjp
def low(v):
    return lax.optimization_barrier(v.astype(jnp.bfloat16)).astype(jnp.float32)

@jax.custom_vjp
def low_back(v):
    return v

def low_keep(v):
    return (low(v), None)

def low_pass(kept, grad):
    return (grad,)

def back_keep(v):
    return (v, None)

def back_low(kept, grad):
    return (low(grad),)
low.defvjp(low_keep, low_pass)
low_back.defvjp(back_keep, back_low)

def rms_scale(values, gain_row):
    return values * lax.rsqrt(lax.optimization_barrier(jnp.mean(values * values, axis=-1, keepdims=True)) + epsilon) * gain_row

def swiglu_half(gate_up):
    half_width = gate_up.shape[-1] // 2
    return jax.nn.silu(gate_up[..., :half_width]) * gate_up[..., half_width:]

def route_table(logits, expert_ids):
    picked_marks = (expert_ids[:, :, None] == jnp.arange(EXPERTS, dtype=jnp.int32)[None, None, :]).astype(jnp.float32)
    picked = lax.optimization_barrier(jnp.sum(logits[:, None, :] * picked_marks, axis=-1))
    gate_values = jax.nn.softmax(picked, axis=-1)
    return lax.optimization_barrier(jnp.sum(gate_values[:, :, None] * picked_marks, axis=1))

def matmul_high(left, right):
    return jnp.dot(left, right, precision=highest, preferred_element_type=jnp.float32)

def attention(queries, key_rows, value_rows, segments):
    block_len = min(256, TOKENS)
    score_scale = HD ** (-0.5)
    positions = jnp.arange(TOKENS, dtype=jnp.int32)
    query_blocks = queries.reshape(TOKENS // block_len, block_len, HK, QPG, HD)
    block_starts = jnp.arange(TOKENS // block_len, dtype=jnp.int32) * block_len

    def one_block(pieces):
        query_block, block_start = pieces
        rows_here = block_start + jnp.arange(block_len, dtype=jnp.int32)
        segments_here = lax.dynamic_slice_in_dim(segments, block_start, block_len)
        raw_scores = low_back(score_scale * jnp.einsum('igqd,jgd->gqij', query_block, key_rows, precision=highest))
        allowed = (positions[None, :] <= rows_here[:, None]) & (segments[None, :] == segments_here[:, None])
        scores = jnp.where(allowed, raw_scores, masked_score)
        row_max = lax.optimization_barrier(jnp.max(scores, axis=-1, keepdims=True))
        weights = jnp.exp(scores - row_max)
        row_sum = lax.optimization_barrier(jnp.sum(weights, axis=-1, keepdims=True))
        mixed_block = jnp.einsum('gqij,jgd->gqid', low(weights), value_rows, precision=highest) / row_sum
        return jnp.transpose(mixed_block, (2, 0, 1, 3))
    blocks_out = lax.map(jax.checkpoint(one_block), (query_blocks, block_starts))
    return blocks_out.reshape(TOKENS, HQ * HD)

def reference(tokens, seq_bounds, expert_ids, attn_gain, qkv_weight, out_weight, mlp_gain, router_weight, expert_gate_up, expert_down, shared_gate_up, shared_down, out_cotangent):
    positions = jnp.arange(TOKENS, dtype=jnp.int32)
    segments = (positions >= seq_bounds[0]).astype(jnp.int32) + (positions >= seq_bounds[1]).astype(jnp.int32)

    def layer(token_rows, gain_attn, w_qkv, w_out, gain_mlp, w_router, w_experts, w_down, w_shared, w_sdown):
        normed = low(rms_scale(token_rows, low(gain_attn)))
        joined = low(low_back(matmul_high(normed, low(w_qkv))))
        groups = joined.reshape(TOKENS, HK, GROUP_W)
        queries = groups[:, :, :QPG * HD].reshape(TOKENS, HK, QPG, HD)
        key_rows = groups[:, :, QPG * HD:(QPG + 1) * HD]
        value_rows = groups[:, :, (QPG + 1) * HD:]
        mixed = low(low_back(attention(queries, key_rows, value_rows, segments)))
        hidden = token_rows + low_back(matmul_high(mixed, low(w_out)))
        normed_mlp = low(rms_scale(hidden, low(gain_mlp)))
        logits = low_back(matmul_high(normed_mlp, low(w_router)))
        route_weights = route_table(logits, expert_ids)

        def one_expert(running, pieces):
            gate_up, down_proj, share_col = pieces
            pre_act = low_back(matmul_high(normed_mlp, low(gate_up)))
            inner_act = low(swiglu_half(pre_act))
            result = low_back(matmul_high(inner_act, low(down_proj)))
            return (running + share_col[:, None] * result, None)
        expert_sum, _ = lax.scan(jax.checkpoint(one_expert), jnp.zeros((TOKENS, D), jnp.float32), (w_experts, w_down, jnp.transpose(route_weights)))
        shared_pre = low_back(matmul_high(normed_mlp, low(w_shared)))
        shared_out = low_back(matmul_high(low(swiglu_half(shared_pre)), low(w_sdown)))
        return hidden + expert_sum + shared_out
    primal, pullback = jax.vjp(layer, tokens.astype(jnp.float32), attn_gain, qkv_weight, out_weight, mlp_gain, router_weight, expert_gate_up, expert_down, shared_gate_up, shared_down)
    gradients = pullback(out_cotangent.astype(jnp.float32))
    return (primal.astype(jnp.bfloat16), gradients[0], gradients[1], gradients[2], gradients[3], gradients[4], gradients[5], gradients[6], gradients[7], gradients[8], gradients[9])
```

```python
import functools

import jax
import jax.numpy as jnp
from jax import lax
from jax.experimental import pallas as pl
from jax.experimental.pallas import tpu as pltpu
from jax.sharding import PartitionSpec as P

D = 1536
HQ = 12
HK = 4
HD = 128
FE = 512
FS = 1024
EXPERTS = 8
QPG = 3
GROUP_W = 640
QKV = 2560
ROWS = 128
BLK = 512
HALF = 256
QW = 384
SMALL = 128
WQ = GROUP_W + SMALL
GQ = GROUP_W + QW + SMALL
FSL = FS // 8
UP = FE + FSL
WE = 3 * UP
NBLK = 32
MESH = pl.DeviceIdType.MESH
BF = jnp.bfloat16
F32 = jnp.float32
epsilon = 1e-05
LOW = -1e30
LOG2E = 1.4426950408889634
SCALE = HD**-0.5
VMEM_LIMIT = 60 * 1024 * 1024

ANY = pl.BlockSpec(memory_space=pl.ANY)
VM = pl.BlockSpec(memory_space=pltpu.VMEM)


def position():
    b = lax.axis_index("blk")
    z = lax.axis_index("head")
    return b // 8, lax.rem(b // 2, 4), lax.rem(b, 2), z


def device(y, x, c, z):
    return ((lax.rem(y, 4) * 4 + lax.rem(x, 4)) * 2 + lax.rem(c, 2), lax.rem(z, 4))


def mirror(pos):
    y, x, c, z = pos
    return 3 - y, 3 - x, 1 - c, z


def greet(targets):
    barrier = pltpu.get_barrier_semaphore()
    for target in targets:
        pl.semaphore_signal(barrier, inc=1, device_id=target, device_id_type=MESH)
    pl.semaphore_wait(barrier, len(targets))


def z_peers(pos):
    y, x, c, z = pos
    return [device(y, x, c, z + d) for d in (1, 2, 3)]


def xy_peers(pos):
    y, x, c, z = pos
    return [device(y, x + d, c, z) for d in (1, 2, 3)] + [
        device(y + d, x, c, z) for d in (1, 2, 3)
    ]


def sibling(pos):
    y, x, c, z = pos
    return device(y, x, c + 1, z)


def other_column(pos):
    y, x, c, z = pos
    return [device(y, x, c + 1, z + d) for d in (0, 1, 2, 3)]


class Net:
    def __init__(self, send_sems, recv_sems, local_sems):
        self.send_sems, self.recv_sems, self.local_sems = send_sems, recv_sems, local_sems
        self.count = 0
        self.locals = 0
        self.started = []

    def put(self, src, dst, target):
        k = self.count
        self.count += 1
        copy = pltpu.make_async_remote_copy(
            src_ref=src,
            dst_ref=dst,
            send_sem=self.send_sems.at[k],
            recv_sem=self.recv_sems.at[k],
            device_id=target,
            device_id_type=MESH,
        )
        copy.start()
        self.started.append(copy)
        return copy

    def reserve(self, count):
        k = self.count
        self.count += count
        return k

    def put_at(self, k, src, dst, target):
        copy = self.copy_at(k, src, dst, target)
        copy.start()

    def copy_at(self, k, src, dst, target):
        return pltpu.make_async_remote_copy(
            src_ref=src,
            dst_ref=dst,
            send_sem=self.send_sems.at[k],
            recv_sem=self.recv_sems.at[k],
            device_id=target,
            device_id_type=MESH,
        )

    def arrived(self, k, ref):
        pltpu.make_async_copy(ref, ref, self.recv_sems.at[k]).wait()

    def left(self, k, ref):
        pltpu.make_async_copy(ref, ref, self.send_sems.at[k]).wait()

    def keep(self, src, dst):
        k = self.locals
        self.locals += 1
        copy = pltpu.make_async_copy(src, dst, self.local_sems.at[k])
        copy.start()
        return copy

    def finish(self):
        for copy in self.started:
            copy.wait_send()


def sems(remote, local):
    return [
        pltpu.SemaphoreType.DMA((remote,)),
        pltpu.SemaphoreType.DMA((remote,)),
        pltpu.SemaphoreType.DMA((local,)),
    ]


def run_jobs(jobs):
    live = list(jobs)
    while live:
        still = []
        for job in live:
            try:
                next(job)
                still.append(job)
            except StopIteration:
                pass
        live = still


def all_of(start, length):
    return pl.ds(start, length)


def gather_xy(net, land, own, cut, pos, with_core):
    y, x, c, z = pos
    width = own.shape[-1]
    first, second = pl.ds(0, cut), pl.ds(cut, width - cut)

    def place(yy, xx, columns):
        if with_core:
            return land.at[yy, xx, c, :, columns]
        return land.at[yy, xx, :, columns]

    whole = slice(None)
    mine = land.at[y, x, c] if with_core else land.at[y, x]
    kept = net.keep(own, mine)
    along_x = [
        net.put(own.at[:, first], place(y, x, first), device(y, x + d, c, z)) for d in (1, 3, 2)
    ]
    along_y = [
        net.put(own.at[:, second], place(y, x, second), device(y + d, x, c, z)) for d in (1, 3, 2)
    ]
    yield
    kept.wait()
    for copy in along_x:
        copy.wait_recv()
    row = place(y, whole, first)
    then_y = [(d, net.put(row, row, device(y + d, x, c, z))) for d in (1, 3, 2)]
    passed = []
    if with_core:
        passed.append(net.put(row, row, sibling(pos)))
    for copy in along_y:
        copy.wait_recv()
    column = place(whole, x, second)
    then_x = [(d, net.put(column, column, device(y, x + d, c, z))) for d in (1, 3, 2)]
    if with_core:
        passed.append(net.put(column, column, sibling(pos)))
    yield
    for d, copy in then_y:
        copy.wait_recv()
        if with_core:
            got = place(lax.rem(y + 4 - d, 4), whole, first)
            passed.append(net.put(got, got, sibling(pos)))
    for d, copy in then_x:
        copy.wait_recv()
        if with_core:
            got = place(whole, lax.rem(x + 4 - d, 4), second)
            passed.append(net.put(got, got, sibling(pos)))
    yield
    for copy in passed:
        copy.wait_recv()


def pick_rows(groups):
    rows = lax.broadcasted_iota(jnp.int32, (12 * groups, 16 * groups), 0)
    cols = lax.broadcasted_iota(jnp.int32, (12 * groups, 16 * groups), 1)
    piece = cols // 16
    within = cols - piece * 16
    return jnp.where((rows == piece * 12 + within) & (within < 12), 1.0, 0.0).astype(BF)


def squeeze_rows(pieces, groups):
    flat = pieces.reshape(groups * 16, pieces.shape[-1])
    return jnp.dot(pick_rows(groups), flat, preferred_element_type=F32).astype(BF)


def spread_rows(rows, groups):
    wide = lax.dot_general(
        pick_rows(groups), rows, (((0,), (0,)), ((), ())), preferred_element_type=F32
    )
    return wide.astype(BF).reshape(groups, 16, rows.shape[-1])


def mult(value, of):
    return pl.multiple_of(value, of)


def transposed(value):
    return jnp.transpose(value.astype(F32), (1, 0)).astype(BF)


SM = pl.BlockSpec(memory_space=pltpu.SMEM)


def home_block(pos, z):
    y, x, c, _ = pos
    b = (y * 4 + x) * 2 + c
    return jnp.where(z < 2, b, NBLK - 1 - b)


RW = D + SMALL
FLOOR = -1e29
ROW_ROW = (((1,), (1,)), ((), ()))
COL_COL = (((0,), (0,)), ((), ()))
EXP_SCALE = SCALE * LOG2E


def exchange_heads(to_tokens, pos, src_at, dst_at, ss, rs):
    y, x, c, z = pos
    b = (y * 4 + x) * 2 + c

    def ends(k):
        target = (home_block(pos, k if to_tokens else z), k)
        return src_at(k), dst_at(z), target, (target[0] == b) & (k == z)

    def remote(k):
        part, slot, target, _ = ends(k)
        return pltpu.make_async_remote_copy(
            src_ref=part,
            dst_ref=slot,
            send_sem=ss.at[k],
            recv_sem=rs.at[z],
            device_id=target,
            device_id_type=MESH,
        )

    def start(k):
        part, slot, _, stays = ends(k)

        @pl.when(stays)
        def _():
            pltpu.make_async_copy(part, slot, rs.at[z]).start()

        @pl.when(jnp.logical_not(stays))
        def _():
            remote(k).start()

    def wait():
        for k in range(4):
            pltpu.make_async_copy(dst_at(k), dst_at(k), rs.at[k]).wait()
        for k in range(4):

            @pl.when(jnp.logical_not(ends(k)[3]))
            def _():
                remote(k).wait_send()

    return start, wait


def turn(n):
    return jnp.where(n == 2, 3, jnp.where(n == 3, 2, n))


def forward_kernel(
    bounds, tok, wq, wo, we, gy, used,
    wo_out, wq_out, kv_out, q_out, o_out, lse_out, tok_out,
    hidden_out, hidden_grad_out, hidden_low_out, gains_out, small_out, do_out, out_parts, dwe_out,
    wq_z, wq_slab, wq_land, wo_z, wo_slab, wo_land, we_z, we_slab, we_land, tok_all, kv_land, q_in,
    qt, m_ref, l_ref, acc, mixed, own_rows, rows_all, gy_all, inner_all, pre_all, parts, out_stage,
    core_land, both, z_land, dwe_stage, mixed_grad, do_in, ss, rs, ls, hs, hr, gs, gr, hs2, hr2,
):
    pos = position()
    y, x, c, z = pos
    b = (y * 4 + x) * 2 + c
    my, mx, mc, _ = mirror(pos)
    greet(
        z_peers(pos)
        + xy_peers(pos)
        + [device(my, mx, mc, d) for d in range(4)]
        + other_column(pos)
    )
    net = Net(ss, rs, ls)

    wq_pieces = [
        net.put(wq.at[lax.rem(z + d, 4)], wq_z.at[z], device(y, x, c, z + d)) for d in (1, 3, 2)
    ]
    wq_kept = net.keep(wq.at[z], wq_z.at[z])

    def out_weights():
        pieces = [net.put(wo, wo_z.at[z], device(y, x, c, z + d)) for d in (1, 3, 2)]
        kept = net.keep(wo, wo_z.at[z])
        yield
        kept.wait()
        for copy in pieces:
            copy.wait_recv()
        wo_slab[...] = squeeze_rows(wo_z[...], 4)
        yield from gather_xy(net, wo_land, wo_slab, D // 2, pos, True)

    def expert_weights():
        me = c * 4 + z
        pieces = []
        for dc in (0, 1):
            for d in (0, 1, 3, 2):
                if (dc, d) == (0, 0):
                    continue
                cc, zz = lax.rem(c + dc, 2), lax.rem(z + d, 4)
                pieces.append(net.put(we.at[cc * 4 + zz], we_z.at[me], device(y, x, cc, zz)))
        kept = net.keep(we.at[me], we_z.at[me])
        yield
        kept.wait()
        for copy in pieces:
            copy.wait_recv()
        we_slab[...] = squeeze_rows(we_z[...], 8)
        yield from gather_xy(net, we_land, we_slab, 1024, pos, False)

    def cotangent():
        mine = gy_all.at[z, c]
        kept = net.keep(gy, mine)
        copies = [(d, net.put(gy, mine, device(y, x, c, z + d))) for d in (1, 3, 2)]
        passed = [net.put(gy, mine, sibling(pos))]
        yield
        for d, copy in copies:
            copy.wait_recv()
            got = gy_all.at[lax.rem(z + 4 - d, 4), c]
            passed.append(net.put(got, got, sibling(pos)))
        yield
        kept.wait()
        for copy in passed:
            copy.wait_recv()

    def pump(job):
        try:
            next(job)
        except StopIteration:
            pass

    wo_job, we_job, gy_job = out_weights(), expert_weights(), cotangent()
    pump(wo_job)
    tok_copies = [net.put(tok, tok_all.at[z], device(y, x, c, z + d)) for d in (1, 3, 2)]
    tok_kept = net.keep(tok, tok_all.at[z])
    pump(we_job)
    pump(gy_job)

    wq_kept.wait()
    for copy in wq_pieces:
        copy.wait_recv()
    wq_slab[...] = squeeze_rows(wq_z[...], 4)
    wq_job = gather_xy(net, wq_land, wq_slab, QW, pos, True)
    pump(wq_job)
    pump(wo_job)
    pump(wq_job)
    pump(wo_job)
    pump(wq_job)
    pump(wq_job)
    wq_saved = net.keep(wq_land, wq_out)

    for i in range(4):
        part = wq_land[i, :, :, :, GROUP_W:].reshape(QW, SMALL)
        one_hot = (
            lax.broadcasted_iota(jnp.int32, (16, SMALL), 0)
            == lax.broadcasted_iota(jnp.int32, (16, SMALL), 1)
        ).astype(BF)
        gains_out[:, i * QW : (i + 1) * QW] = lax.dot_general(
            one_hot, part, (((1,), (1,)), ((), ())), preferred_element_type=F32
        )
    tok_kept.wait()
    for copy in tok_copies:
        copy.wait_recv()
    tok_saved = net.keep(tok_all, tok_out)
    gain_attn = gains_out[EXPERTS + 1 : EXPERTS + 2, :]

    def project(i, carried):
        rows = tok_all[i].astype(F32)
        unit = rows * lax.rsqrt(jnp.mean(rows * rows, axis=-1, keepdims=True) + epsilon)
        low = (unit * gain_attn).astype(BF)
        weights = wq_land[...].reshape(D, WQ)[:, :GROUP_W]
        joined = jnp.dot(low, weights, preferred_element_type=F32).astype(BF)
        half, place = i // 2, pl.ds(mult(lax.rem(i, 2) * ROWS, ROWS), ROWS)
        q_out[half, place, :] = joined[:, :QW]
        kv_land[y, x, c, half, place, :] = joined[:, QW:]
        return carried

    lax.fori_loop(0, 4, project, 0)

    swapped = net.put(q_out.at[1], q_in, device(my, mx, mc, z))
    whole = slice(None)
    along_x, along_y = [], []
    even, odd = kv_land.at[y, x, c, 0], kv_land.at[y, x, c, 1]
    for d in (1, 3, 2):
        along_x.append(net.put(even, even, device(y, x + d, c, z)))
        along_y.append(net.put(odd, odd, device(y + d, x, c, z)))
    m_ref[...] = jnp.full_like(m_ref, FLOOR)
    l_ref[...] = jnp.zeros_like(l_ref)
    acc[...] = jnp.zeros_like(acc)
    lo, hi = 2 * b, 2 * (NBLK - b) - 1
    starts = []
    for chunk in (lo, hi):
        at = chunk * HALF + lax.broadcasted_iota(jnp.int32, (1, HALF), 1)
        first = jnp.where(at >= bounds[1], bounds[1], jnp.where(at >= bounds[0], bounds[0], 0))
        starts.append((at, first))
    for copy in along_x:
        copy.wait_recv()
    row = kv_land.at[y, whole, c, 0]
    from_y, crossed_y, crossed_x = net.reserve(4), net.reserve(4), net.reserve(4)
    for d in (1, 3, 2):
        net.put_at(from_y + d, row, row, device(y + d, x, c, z))
    net.put_at(crossed_y, row, row, sibling(pos))
    for copy in along_y:
        copy.wait_recv()
    column = kv_land.at[whole, x, c, 1]
    from_x = net.reserve(4)
    for d in (1, 3, 2):
        net.put_at(from_x + d, column, column, device(y, x + d, c, z))
    net.put_at(crossed_x, column, column, sibling(pos))
    pump(wo_job)
    swapped.wait_recv()
    for h in range(QPG):
        qt[0, h] = transposed(q_out[0, :, h * HD : (h + 1) * HD])
        qt[1, h] = transposed(q_in[:, h * HD : (h + 1) * HD])
    q_out[2] = q_in[...]

    def update(ids, yy, xx, cc, half, masked):
        k_rows = kv_land[yy, xx, cc, half, :, :HD]
        v_rows = kv_land[yy, xx, cc, half, :, HD:]
        work = [(i, h) for i in ids for h in range(QPG)]
        scores = [jnp.dot(k_rows, qt[i, h], preferred_element_type=F32) for i, h in work]
        if masked:
            chunk = ((yy * 4 + xx) * 2 + cc) * 2 + half
            key_at = chunk * HALF + lax.broadcasted_iota(jnp.int32, (HALF, HALF), 0)
            allowed = {i: (key_at >= starts[i][1]) & (key_at <= starts[i][0]) for i in ids}
            scores = [jnp.where(allowed[i], s, LOW) for (i, _), s in zip(work, scores)]
        m_old = [m_ref[i, h] for i, h in work]
        l_old = [l_ref[i, h] for i, h in work]
        a_old = [acc[i, h] for i, h in work]
        m_new = [jnp.maximum(m, jnp.max(s, axis=0, keepdims=True)) for m, s in zip(m_old, scores)]
        p = [jnp.exp2((s - m) * EXP_SCALE) for s, m in zip(scores, m_new)]
        alpha = [jnp.exp2((m - n) * EXP_SCALE) for m, n in zip(m_old, m_new)]
        pv = [
            lax.dot_general(
                v_rows, w.astype(BF), (((0,), (0,)), ((), ())), preferred_element_type=F32
            )
            for w in p
        ]
        for n, (i, h) in enumerate(work):
            m_ref[i, h] = m_new[n]
            l_ref[i, h] = l_old[n] * alpha[n] + jnp.sum(p[n], axis=0, keepdims=True)
            acc[i, h] = a_old[n] * alpha[n] + pv[n]

    late = 2 * NBLK - 2

    def chunk_step(yy, xx, cc, half):
        chunk = ((yy * 4 + xx) * 2 + cc) * 2 + half
        in_lo, in_hi = chunk <= lo, chunk <= hi
        masked = (chunk <= 1) | (chunk == lo) | (chunk == hi)
        early = chunk < late
        plain = early & jnp.logical_not(masked)

        @pl.when(plain & in_lo & in_hi)
        def _():
            update((0, 1), yy, xx, cc, half, False)

        @pl.when(plain & in_lo & jnp.logical_not(in_hi))
        def _():
            update((0,), yy, xx, cc, half, False)

        @pl.when(plain & in_hi & jnp.logical_not(in_lo))
        def _():
            update((1,), yy, xx, cc, half, False)

        @pl.when(early & masked)
        def _():
            update((0, 1), yy, xx, cc, half, True)

    def stage(n, carried):
        d = turn(n)
        yy, xx = lax.rem(y + 4 - d, 4), lax.rem(x + 4 - d, 4)
        row, column = kv_land.at[yy, whole, c, 0], kv_land.at[whole, xx, c, 1]

        @pl.when(n > 0)
        def _():
            net.arrived(from_y + d, row)
            net.put_at(crossed_y + d, row, row, sibling(pos))
            net.arrived(from_x + d, column)
            net.put_at(crossed_x + d, column, column, sibling(pos))

        net.arrived(crossed_y + d, kv_land.at[yy, whole, 1 - c, 0])
        net.arrived(crossed_x + d, kv_land.at[whole, xx, 1 - c, 1])

        def step(t, carried):
            half = t // 8
            chunk_step(
                jnp.where(half == 0, yy, (t - 8) // 2),
                jnp.where(half == 0, t // 2, xx),
                lax.rem(t, 2),
                half,
            )
            return carried

        lax.fori_loop(0, 16, step, 0)
        return carried

    lax.fori_loop(0, 3, stage, 0)
    pump(we_job)
    lax.fori_loop(3, 4, stage, 0)
    pump(we_job)
    for n in range(4):
        for k in (crossed_y, crossed_x):
            net.left(k + n, row)
        if n:
            net.left(from_y + n, row)
            net.left(from_x + n, column)
    kv_saved = net.keep(kv_land, kv_out)

    for i, chunk in enumerate((lo, hi)):

        @pl.when(chunk >= late)
        def _():
            third = starts[i][0] >= bounds[1]
            for h in range(QPG):
                m_ref[i, h] = jnp.where(third, FLOOR, m_ref[i, h])
                l_ref[i, h] = jnp.where(third, 0.0, l_ref[i, h])
                acc[i, h] = jnp.where(third, 0.0, acc[i, h])
            lax.fori_loop(0, 2, lambda half, _: update((i,), 3, 3, 1, half, True), None)

    start, wait_mixed = exchange_heads(
        True, pos, lambda k: o_out.at[k], lambda g: mixed.at[:, pl.ds(mult(g * QW, QW), QW)], hs, hr
    )
    for i in range(2):
        for h in range(QPG):
            total = l_ref[i, h]
            lse_out[i, h] = m_ref[i, h] * EXP_SCALE + jnp.log(total) * LOG2E
            value = jnp.transpose(acc[i, h] / total, (1, 0)).astype(BF)
            o_out[2 * i, :, h * HD : (h + 1) * HD] = value[:ROWS]
            o_out[2 * i + 1, :, h * HD : (h + 1) * HD] = value[ROWS:]
        start(2 * i)
        start(2 * i + 1)

    pump(wo_job)
    pump(wo_job)
    wo_saved = net.keep(wo_land, wo_out)
    wait_mixed()

    def add_hidden(i, carried):
        columns = pl.ds(mult(i * QW, QW), QW)
        hidden_out[:, columns] = tok[:, columns].astype(F32) + lax.dot_general(
            mixed[...], wo_land[i].reshape(QW, D), ROW_ROW, preferred_element_type=F32
        )
        return carried

    lax.fori_loop(0, 4, add_hidden, 0)
    hidden = hidden_out[...]
    unit = hidden * lax.rsqrt(jnp.mean(hidden * hidden, axis=-1, keepdims=True) + epsilon)
    low = (unit * gains_out[EXPERTS : EXPERTS + 1, :]).astype(BF)
    own_rows[:, :D] = low
    small_weights = wq_land[:, :, :, :, GROUP_W:].reshape(D, SMALL)
    logits = jnp.dot(low, small_weights, preferred_element_type=F32)
    is_used = used[...] > 0.0
    top = jnp.max(jnp.where(is_used, logits, LOW), axis=-1, keepdims=True)
    raised = jnp.where(is_used, jnp.exp(logits - top), 0.0)
    route = raised / jnp.sum(raised, axis=-1, keepdims=True)
    coarse = route.astype(BF).astype(F32)
    own_rows[:, D:] = (coarse + pltpu.roll(route - coarse, EXPERTS, 1)).astype(BF)

    mine = rows_all.at[z, c]
    rows_kept = net.keep(own_rows, mine)
    from_z, crossed_z = net.reserve(4), net.reserve(4)
    for d in (1, 3, 2):
        net.put_at(from_z + d, own_rows, mine, device(y, x, c, z + d))
    net.put_at(crossed_z, own_rows, mine, sibling(pos))
    for job in (gy_job, we_job, wo_job, wq_job):
        for _ in job:
            pass
    rows_kept.wait()
    to_core, to_z = net.reserve(4), net.reserve(4)
    me = c * 4 + z
    gate_columns, up_columns, down_columns = (slice(i * UP, (i + 1) * UP) for i in range(3))

    def weights(columns):
        return we_land[:, :, :, columns].reshape(D, UP)

    def finish_block(n):
        d, slot = turn(n), lax.rem(n, 2)
        zz = lax.rem(z + 4 - d, 4)
        net.arrived(to_core + n, core_land.at[n])
        both[n] = (parts[slot, c].astype(F32) + core_land[n].astype(F32)).astype(BF)
        net.left(to_core + n, parts.at[slot, 1 - c])

        @pl.when(n > 0)
        def _():
            net.put_at(to_z + d, both.at[n], z_land.at[d], device(y, x, c, zz))

    def expert_block(n, carried):
        d, slot = turn(n), lax.rem(n, 2)
        zz = lax.rem(z + 4 - d, 4)
        got = rows_all.at[zz, c]

        @pl.when(n > 0)
        def _():
            net.arrived(from_z + d, got)
            net.put_at(crossed_z + d, got, got, sibling(pos))

        net.arrived(crossed_z + d, rows_all.at[zz, 1 - c])

        @pl.when(n > 1)
        def _():
            pltpu.make_async_copy(out_stage.at[slot], out_stage.at[slot], gs.at[slot]).wait()

        rows = rows_all[zz].reshape(2 * ROWS, RW)
        x_rows, lanes = rows[:, :D], rows[:, D:].astype(F32)
        lane = lax.broadcasted_iota(jnp.int32, lanes.shape, 1)
        route = jnp.sum(
            jnp.where((lane == me) | (lane == me + EXPERTS), lanes, 0.0), axis=-1, keepdims=True
        )
        gy_rows = gy_all[zz].reshape(2 * ROWS, D)
        gate = jnp.dot(x_rows, weights(gate_columns), preferred_element_type=F32)
        up = jnp.dot(x_rows, weights(up_columns), preferred_element_type=F32)
        raw = jnp.dot(gy_rows, weights(down_columns), preferred_element_type=F32)
        unit_lane = lax.broadcasted_iota(jnp.int32, gate.shape, 1)
        share = jnp.where(unit_lane < FE, route, 1.0)
        sig = 1.0 / (1.0 + jnp.exp(-gate))
        silu = gate * sig
        inner = silu * up
        scaled = (inner * share).astype(BF)
        inner_all[zz] = scaled
        route_grad = jnp.sum(inner[:, :FE] * raw[:, :FE], axis=-1, keepdims=True)
        inner_grad = raw * share
        pre_grad = jnp.concatenate(
            [inner_grad * up * (sig + silu * (1.0 - sig)), inner_grad * silu], axis=-1
        ).astype(BF)
        pre_all[zz] = pre_grad
        out_stage[slot] = (
            lax.dot_general(scaled, weights(down_columns), ROW_ROW, preferred_element_type=F32)
            .astype(BF)
            .reshape(2, ROWS, D)
        )
        pltpu.make_async_copy(out_stage.at[slot], out_parts.at[zz], gs.at[slot]).start()
        rows_grad = lax.dot_general(
            pre_grad[:, :UP], weights(gate_columns), ROW_ROW, preferred_element_type=F32
        ) + lax.dot_general(
            pre_grad[:, UP:], weights(up_columns), ROW_ROW, preferred_element_type=F32
        )
        parts[slot, :, :, :D] = rows_grad.astype(BF).reshape(2, ROWS, D)
        high = route_grad.astype(BF).astype(F32)
        parts[slot, :, :, D:] = (
            jnp.where(lane == me, high, 0.0) + jnp.where(lane == me + EXPERTS, route_grad - high, 0.0)
        ).astype(BF).reshape(2, ROWS, SMALL)
        net.put_at(to_core + n, parts.at[slot, 1 - c], core_land.at[n], sibling(pos))

        @pl.when(n > 0)
        def _():
            finish_block(n - 1)

        return carried

    lax.fori_loop(0, 4, expert_block, 0)
    finish_block(3)
    for slot in range(2):
        pltpu.make_async_copy(out_stage.at[slot], out_stage.at[slot], gs.at[slot]).wait()

    def weight_grads(t, carried):
        slot = lax.rem(t, 2)

        @pl.when(t > 1)
        def _():
            pltpu.make_async_copy(dwe_stage.at[slot], dwe_stage.at[slot], gr.at[slot]).wait()

        columns = pl.ds(mult(t * QW, QW), QW)
        for i in range(3):
            value = jnp.zeros((QW, UP), F32)
            for k in range(4):
                left = (rows_all if i < 2 else gy_all)[k, :, :, columns].reshape(2 * ROWS, QW)
                right = pre_all[k, :, i * UP : (i + 1) * UP] if i < 2 else inner_all[k]
                value = value + lax.dot_general(left, right, COL_COL, preferred_element_type=F32)
            dwe_stage[slot, :, :, i * UP : (i + 1) * UP] = value.astype(BF).reshape(4, 96, UP)
        pltpu.make_async_copy(dwe_stage.at[slot], dwe_out.at[t], gr.at[slot]).start()
        return carried

    lax.fori_loop(0, 4, weight_grads, 0)

    for d in (1, 2, 3):
        net.arrived(to_z + d, z_land.at[d])

    def total(columns):
        value = both[0, :, columns].astype(F32)
        for d in (1, 2, 3):
            value = value + z_land[d, :, columns].astype(F32)
        return value

    lane = lax.broadcasted_iota(jnp.int32, (ROWS, SMALL), 1)
    route_grads = total(slice(D, RW))
    route_grads = route_grads + pltpu.roll(route_grads, SMALL - EXPERTS, 1)
    logits_grad = (
        route * (route_grads - jnp.sum(route * route_grads, axis=-1, keepdims=True))
    ).astype(BF)
    normed_grad = total(slice(0, D)) + lax.dot_general(
        logits_grad, small_weights, ROW_ROW, preferred_element_type=F32
    )
    hidden = hidden_out[...]
    scale = lax.rsqrt(jnp.mean(hidden * hidden, axis=-1, keepdims=True) + epsilon)
    unit = hidden * scale
    dn = normed_grad * gains_out[EXPERTS : EXPERTS + 1, :]
    hidden_grad = gy_all[z, c].astype(F32) + scale * (
        dn - unit * jnp.mean(dn * unit, axis=-1, keepdims=True)
    )
    hidden_grad_out[...] = hidden_grad
    hidden_low = hidden_grad.astype(BF)
    hidden_low_out[...] = hidden_low
    total_grad = jnp.zeros((ROWS, D), F32)
    for i in range(4):
        total_grad = total_grad + jnp.dot(
            hidden_low[:, i * QW : (i + 1) * QW],
            wo_land[i].reshape(QW, D),
            preferred_element_type=F32,
        )
    start, wait_heads = exchange_heads(
        False, pos, lambda g: mixed_grad.at[g], lambda k: do_in.at[k], hs2, hr2
    )
    for g in range(4):
        mixed_grad[g] = total_grad[:, g * QW : (g + 1) * QW].astype(BF)
        start(g)
    gain_column = jnp.where(lane == EXPERTS, 1.0, 0.0).astype(BF)
    small_out[...] = (
        lax.dot_general(own_rows[:, :D], logits_grad, COL_COL, preferred_element_type=F32)
        + lax.dot_general(
            (normed_grad * unit).astype(BF), gain_column, COL_COL, preferred_element_type=F32
        )
    ).astype(BF)
    for n in range(4):
        net.left(crossed_z + n, own_rows)
        if n:
            net.left(from_z + n, own_rows)
            net.left(to_z + n, both.at[n])
    for slot in range(2):
        pltpu.make_async_copy(dwe_stage.at[slot], dwe_stage.at[slot], gr.at[slot]).wait()
    wait_heads()
    do_out[...] = do_in[...]
    for copy in (wq_saved, tok_saved, kv_saved, wo_saved):
        copy.wait()
    net.finish()


def forward(bounds, tok, wq, wo, we, gy, used):
    outs = {
        "wo": ((4, 4, 2, 48, D), BF, ANY),
        "wq": ((4, 4, 2, 48, WQ), BF, ANY),
        "kv": ((4, 4, 2, 2, HALF, 2 * HD), BF, ANY),
        "q": ((3, HALF, QW), BF, VM),
        "o": ((4, ROWS, QW), BF, VM),
        "lse": ((2, QPG, 1, HALF), F32, VM),
        "tok": ((4, ROWS, D), BF, ANY),
        "hidden": ((ROWS, D), F32, VM),
        "hidden_grad": ((ROWS, D), F32, VM),
        "hidden_low": ((ROWS, D), BF, VM),
        "gains": ((16, D), F32, VM),
        "small": ((D, SMALL), BF, VM),
        "do": ((4, ROWS, QW), BF, VM),
        "out_parts": ((4, 2, ROWS, D), BF, ANY),
        "dwe": ((4, 4, 96, WE), BF, ANY),
    }
    values = pl.pallas_call(
        forward_kernel,
        name="forward",
        out_shape=tuple(jax.ShapeDtypeStruct(s, t) for s, t, _ in outs.values()),
        in_specs=[SM, VM, ANY, ANY, ANY, ANY, VM],
        out_specs=tuple(m for _, _, m in outs.values()),
        scratch_shapes=[
            pltpu.VMEM((4, 16, WQ), BF),
            pltpu.VMEM((48, WQ), BF),
            pltpu.VMEM((4, 4, 2, 48, WQ), BF),
            pltpu.VMEM((4, 16, D), BF),
            pltpu.VMEM((48, D), BF),
            pltpu.VMEM((4, 4, 2, 48, D), BF),
            pltpu.VMEM((8, 16, WE), BF),
            pltpu.VMEM((96, WE), BF),
            pltpu.VMEM((4, 4, 96, WE), BF),
            pltpu.VMEM((4, ROWS, D), BF),
            pltpu.VMEM((4, 4, 2, 2, HALF, 2 * HD), BF),
            pltpu.VMEM((HALF, QW), BF),
            pltpu.VMEM((2, QPG, HD, HALF), BF),
            pltpu.VMEM((2, QPG, 1, HALF), F32),
            pltpu.VMEM((2, QPG, 1, HALF), F32),
            pltpu.VMEM((2, QPG, HD, HALF), F32),
            pltpu.VMEM((ROWS, D), BF),
            pltpu.VMEM((ROWS, RW), BF),
            pltpu.VMEM((4, 2, ROWS, RW), BF),
            pltpu.VMEM((4, 2, ROWS, D), BF),
            pltpu.VMEM((4, 2 * ROWS, UP), BF),
            pltpu.VMEM((4, 2 * ROWS, 2 * UP), BF),
            pltpu.VMEM((2, 2, ROWS, RW), BF),
            pltpu.VMEM((2, 2, ROWS, D), BF),
            pltpu.VMEM((4, ROWS, RW), BF),
            pltpu.VMEM((4, ROWS, RW), BF),
            pltpu.VMEM((4, ROWS, RW), BF),
            pltpu.VMEM((2, 4, 96, WE), BF),
            pltpu.VMEM((4, ROWS, QW), BF),
            pltpu.VMEM((4, ROWS, QW), BF),
        ]
        + sems(128, 32)
        + [pltpu.SemaphoreType.DMA((4,))] * 6,
        compiler_params=pltpu.CompilerParams(
            collective_id=1, has_side_effects=True, vmem_limit_bytes=VMEM_LIMIT
        ),
    )(bounds, tok, wq, wo, we, gy, used)
    return dict(zip(outs, values))


def add_into(dst, left, right, rows):
    step = 32

    def body(i, carried):
        place = pl.ds(mult(i * step, step), step)
        dst[place, :] = (left[place, :].astype(F32) + right[place, :].astype(F32)).astype(
            dst.dtype
        )
        return carried

    lax.fori_loop(0, rows // step, body, 0)


def add_four(dst, parts, rows, step):
    def body(i, carried):
        place = pl.ds(mult(i * step, step), step)
        total = parts[0][place, :].astype(F32)
        for part in parts[1:]:
            total = total + part[place, :].astype(F32)
        dst[place, :] = total.astype(dst.dtype)
        return carried

    lax.fori_loop(0, rows // step, body, 0)


def sum_group(net, parts, pos, core_land, own, both, z_land, out):
    y, x, c, z = pos
    order = (0, 1, 3, 2)
    crossing, kept = [], []
    for d in order:
        zz = lax.rem(z + d, 4)
        crossing.append(net.put(parts.at[zz, 1 - c], core_land.at[zz], sibling(pos)))
        kept.append(net.keep(parts.at[zz, c], own.at[zz]))
    yield
    arriving = []
    for n, d in enumerate(order):
        zz = lax.rem(z + d, 4)
        crossing[n].wait_recv()
        kept[n].wait()
        add_into(both.at[zz], own.at[zz], core_land.at[zz], ROWS)
        if d:
            arriving.append(net.put(both.at[zz], z_land.at[d - 1], device(y, x, c, zz)))
    yield
    for copy in arriving:
        copy.wait_recv()
    add_four(out, [both.at[z]] + [z_land.at[d] for d in range(3)], ROWS, 32)


def group_scratch(width):
    return [
        pltpu.VMEM((4, ROWS, width), BF),
        pltpu.VMEM((4, ROWS, width), BF),
        pltpu.VMEM((4, ROWS, width), BF),
        pltpu.VMEM((3, ROWS, width), BF),
    ]


def scatter_xy(net, src, pos, cut, a_own, a_land, a_sum, a_last, b_own, b_land, b_sum, b_last, out):
    y, x, c, z = pos
    rows, width = src.shape[2], src.shape[3]
    first, second = pl.ds(0, cut), pl.ds(cut, width - cut)
    whole = slice(None)
    keep_a = net.keep(src.at[whole, x, whole, first], a_own)
    keep_b = net.keep(src.at[y, whole, whole, second], b_own)
    to_x, to_y = [], []
    for d in (1, 3, 2):
        xx, yy = lax.rem(x + d, 4), lax.rem(y + d, 4)
        to_x.append(
            net.put(src.at[whole, xx, whole, first], a_land.at[d - 1], device(y, xx, c, z))
        )
        to_y.append(
            net.put(src.at[yy, whole, whole, second], b_land.at[d - 1], device(yy, x, c, z))
        )
    yield
    keep_a.wait()
    for copy in to_x:
        copy.wait_recv()
    step = 16

    def fold(own, land, total):
        def body(i, carried):
            q = i // (rows // step)
            place = pl.ds(mult(lax.rem(i, rows // step) * step, step), step)
            value = own[q, place, :].astype(F32)
            for d in range(3):
                value = value + land[d, q, place, :].astype(F32)
            total[q, place, :] = value.astype(BF)
            return carried

        lax.fori_loop(0, 4 * (rows // step), body, 0)

    fold(a_own, a_land, a_sum)
    last_y, last_x = [], []
    for d in (1, 3, 2):
        yy = lax.rem(y + d, 4)
        last_y.append(net.put(a_sum.at[yy], a_last.at[d - 1], device(yy, x, c, z)))
    keep_b.wait()
    for copy in to_y:
        copy.wait_recv()
    fold(b_own, b_land, b_sum)
    for d in (1, 3, 2):
        xx = lax.rem(x + d, 4)
        last_x.append(net.put(b_sum.at[xx], b_last.at[d - 1], device(y, xx, c, z)))
    yield
    for copy in last_y:
        copy.wait_recv()
    for copy in last_x:
        copy.wait_recv()

    def final(i, carried):
        place = pl.ds(mult(i * step, step), step)
        for at, own, last, columns in ((y, a_sum, a_last, first), (x, b_sum, b_last, second)):
            value = own[at, place, :].astype(F32)
            for d in range(3):
                value = value + last[d, place, :].astype(F32)
            out[place, columns] = value.astype(BF)
        return carried

    lax.fori_loop(0, rows // step, final, 0)


def scatter_scratch(rows, width, cut):
    shapes = []
    for w in (cut, width - cut):
        shapes += [
            pltpu.VMEM((4, rows, w), BF),
            pltpu.VMEM((3, 4, rows, w), BF),
            pltpu.VMEM((4, rows, w), BF),
            pltpu.VMEM((3, rows, w), BF),
        ]
    return shapes


def fold_cores(net, src, pos, own, land, both):
    y, x, c, z = pos
    crossing = net.put(src.at[:, :, 1 - c], land, sibling(pos))
    kept = net.keep(src.at[:, :, c], own)
    yield
    kept.wait()
    crossing.wait_recv()
    rows = own.shape[2]
    step = 16

    def body(i, carried):
        n = i // (rows // step)
        yy, xx = n // 4, lax.rem(n, 4)
        place = pl.ds(mult(lax.rem(i, rows // step) * step, step), step)
        both[yy, xx, place, :] = (
            own[yy, xx, place, :].astype(F32) + land[yy, xx, place, :].astype(F32)
        ).astype(BF)
        return carried

    lax.fori_loop(0, 16 * (rows // step), body, 0)


def backward_kernel(
    bounds, q, o, do, lse, kv_in, dwe, hg, out_parts,
    dkv_out, dq_out, o_out, dwe_out, hg_all, out_sum,
    kv, o_in, dq_own, dq_in, qt, dot_t, delta, late_lse, dqt, part, core_land, both, a_land, b_land,
    a_sum, b_sum, a_last, b_last, *scratch,
):
    we_s = scratch[:8]
    we_rows, we_pieces = scratch[8:10]
    group_s = scratch[10:14]
    ss, rs, ls = scratch[14:]
    pos = position()
    y, x, c, z = pos
    b = (y * 4 + x) * 2 + c
    net = Net(ss, rs, ls)
    kv_kept = net.keep(kv_in, kv)
    greet(z_peers(pos) + xy_peers(pos) + [device(*mirror(pos))] + other_column(pos))
    o_swap = net.put(o.at[pl.ds(2, 2)], o_in, device(*mirror(pos)))
    whole = slice(None)

    def experts():
        yield from scatter_xy(net, dwe, pos, 1024, *we_s, we_rows)
        we_pieces[...] = spread_rows(we_rows[...], 8)
        me = c * 4 + z
        pieces = []
        for dc in (0, 1):
            for d in (0, 1, 3, 2):
                if (dc, d) == (0, 0):
                    continue
                cc, zz = lax.rem(c + dc, 2), lax.rem(z + d, 4)
                pieces.append(
                    net.put(we_pieces.at[cc * 4 + zz], dwe_out.at[me], device(y, x, cc, zz))
                )
        kept = net.keep(we_pieces.at[me], dwe_out.at[me])
        yield
        kept.wait()
        for copy in pieces:
            copy.wait_recv()

    def rows_of_group():
        mine = hg_all.at[z]
        kept = net.keep(hg, mine)
        copies = [net.put(hg, mine, device(y, x, c, z + d)) for d in (1, 3, 2)]
        yield
        kept.wait()
        for copy in copies:
            copy.wait_recv()

    def pump(job):
        try:
            next(job)
        except StopIteration:
            pass

    we_job = experts()
    out_job = sum_group(net, out_parts, pos, *group_s, out_sum)
    hg_job = rows_of_group()
    pump(out_job)
    pump(we_job)
    pump(hg_job)

    lo, hi = 2 * b, 2 * (NBLK - b) - 1
    late = 2 * NBLK - 2
    starts = []
    for i, chunk in enumerate((lo, hi)):
        at = chunk * HALF + lax.broadcasted_iota(jnp.int32, (1, HALF), 1)
        first = jnp.where(at >= bounds[1], bounds[1], jnp.where(at >= bounds[0], bounds[0], 0))
        starts.append((at, first))
        third = at >= bounds[1]
        for h in range(QPG):
            columns = slice(h * HD, (h + 1) * HD)
            qt[i, h] = transposed(q[2 * i, :, columns])
            do_t = jnp.transpose(
                do[2 * i : 2 * i + 2, :, columns].reshape(HALF, HD).astype(F32), (1, 0)
            )
            o_t = jnp.transpose(
                o[2 * i : 2 * i + 2, :, columns].reshape(HALF, HD).astype(F32), (1, 0)
            )
            dot_t[i, h] = do_t.astype(BF)
            delta[i, h] = jnp.sum(do_t * o_t, axis=0, keepdims=True)
            late_lse[i, h] = jnp.where(third, -LOW, lse[i, h])
    dqt[...] = jnp.zeros_like(dqt)
    kv_kept.wait()
    pump(out_job)

    def pairs(ids, yy, xx, cc, half, slot, masked):
        k_rows = kv[yy, xx, cc, half, :, :HD]
        v_rows = kv[yy, xx, cc, half, :, HD:]
        work = [(i, h) for i in ids for h in range(QPG)]
        scores = [jnp.dot(k_rows, qt[i, h], preferred_element_type=F32) for i, h in work]
        dp = [jnp.dot(v_rows, dot_t[i, h], preferred_element_type=F32) for i, h in work]
        if masked:
            chunk = ((yy * 4 + xx) * 2 + cc) * 2 + half
            key_at = chunk * HALF + lax.broadcasted_iota(jnp.int32, (HALF, HALF), 0)
            allowed = {i: (key_at >= starts[i][1]) & (key_at <= starts[i][0]) for i in ids}
            p = [
                jnp.where(allowed[i], jnp.exp2(s * EXP_SCALE - lse[i, h]), 0.0)
                for (i, h), s in zip(work, scores)
            ]
        else:
            p = [
                jnp.exp2(s * EXP_SCALE - late_lse[i, h]) for (i, h), s in zip(work, scores)
            ]
        ds = [(w * (g - delta[i, h])).astype(BF) for (i, h), w, g in zip(work, p, dp)]
        dk = jnp.zeros((HALF, HD), F32)
        dv = jnp.zeros((HALF, HD), F32)
        dq = []
        for n, (i, h) in enumerate(work):
            columns = slice(h * HD, (h + 1) * HD)
            do_rows = do[2 * i : 2 * i + 2, :, columns].reshape(HALF, HD)
            dv = dv + jnp.dot(p[n].astype(BF), do_rows, preferred_element_type=F32)
            dk = dk + jnp.dot(ds[n], q[2 * i, :, columns], preferred_element_type=F32)
            dq.append(lax.dot_general(k_rows, ds[n], COL_COL, preferred_element_type=F32))
        for n, (i, h) in enumerate(work):
            dqt[i, h] += dq[n]
        part[slot, cc, half, :, :HD] = (dk * SCALE).astype(BF)
        part[slot, cc, half, :, HD:] = dv.astype(BF)

    def chunk_step(yy, xx, cc, half, slot):
        chunk = ((yy * 4 + xx) * 2 + cc) * 2 + half
        in_lo, in_hi = chunk <= lo, chunk <= hi
        special = (chunk <= 1) | (chunk == lo) | (chunk == hi) | (chunk >= late)
        masked = special & (in_lo | in_hi)
        plain = jnp.logical_not(special)

        @pl.when(plain & in_lo & in_hi)
        def _():
            pairs((0, 1), yy, xx, cc, half, slot, False)

        @pl.when(plain & in_lo & jnp.logical_not(in_hi))
        def _():
            pairs((0,), yy, xx, cc, half, slot, False)

        @pl.when(plain & in_hi & jnp.logical_not(in_lo))
        def _():
            pairs((1,), yy, xx, cc, half, slot, False)

        @pl.when(masked)
        def _():
            pairs((0, 1), yy, xx, cc, half, slot, True)

        @pl.when(jnp.logical_not(in_lo | in_hi))
        def _():
            part[slot, cc, half] = jnp.zeros((HALF, 2 * HD), BF)

    def chip(t):
        dy = jnp.where(
            t < 4,
            t,
            jnp.where(
                t < 7,
                1,
                jnp.where(
                    t < 10,
                    jnp.where(t == 7, 0, t - 6),
                    jnp.where(
                        t < 12, 3, jnp.where(t < 14, 2 * (t - 12), 2 * (15 - t))
                    ),
                ),
            ),
        )
        dx = jnp.where(
            t < 4,
            1,
            jnp.where(
                t < 7,
                jnp.where(t == 4, 0, t - 3),
                jnp.where(
                    t < 10,
                    3,
                    jnp.where(t < 12, 2 * (t - 10), jnp.where(t < 14, 2, 0)),
                ),
            ),
        )
        return lax.rem(y + dy, 4), lax.rem(x + dx, 4)

    to_core, to_x, to_y = net.reserve(16), net.reserve(4), net.reserve(4)

    def fold_chip(t):
        yy, xx = chip(t)
        slot = lax.rem(t, 2)
        net.arrived(to_core + t, core_land.at[yy, xx])
        both[yy, xx] = (part[slot, c].astype(F32) + core_land[yy, xx].astype(F32)).astype(BF)
        net.left(to_core + t, part.at[slot, 1 - c])

    def send_lines(d):
        xx, yy = lax.rem(x + d, 4), lax.rem(y + d, 4)
        net.put_at(to_x + d, both.at[whole, xx, 0], a_land.at[d], device(y, xx, c, z))
        net.put_at(to_y + d, both.at[yy, whole, 1], b_land.at[d], device(yy, x, c, z))

    def chip_step(t, carried):
        yy, xx = chip(t)
        slot = lax.rem(t, 2)

        def step(n, carried):
            chunk_step(yy, xx, n // 2, lax.rem(n, 2), slot)
            return carried

        lax.fori_loop(0, 4, step, 0)
        net.put_at(to_core + t, part.at[slot, 1 - c], core_land.at[yy, xx], sibling(pos))

        @pl.when(t > 0)
        def _():
            fold_chip(t - 1)

        for at, d in ((7, 1), (12, 3), (15, 2)):

            @pl.when(t == at)
            def _():
                send_lines(d)

        return carried

    lax.fori_loop(0, 16, chip_step, 0)
    for i in range(2):
        for h in range(QPG):
            dq_own[i, :, h * HD : (h + 1) * HD] = jnp.transpose(dqt[i, h] * SCALE, (1, 0)).astype(
                BF
            )
    dq_swap = net.put(dq_own.at[1], dq_in, device(*mirror(pos)))
    lax.fori_loop(15, 16, lambda t, _: fold_chip(t), None)

    def fold_lines(own_at, land, total):
        def body(n, carried):
            q_at, place = n // 8, pl.ds(mult(lax.rem(n, 8) * 32, 32), 32)
            value = own_at(q_at, place).astype(F32)
            for d in (1, 2, 3):
                value = value + land[d, q_at, place, :].astype(F32)
            total[q_at, place, :] = value.astype(BF)
            return carried

        lax.fori_loop(0, 32, body, 0)

    for d in (1, 3, 2):
        net.arrived(to_x + d, a_land.at[d])
    fold_lines(lambda n, place: both[n, x, 0, place, :], a_land, a_sum)
    last_y = []
    for d in (1, 3, 2):
        yy = lax.rem(y + d, 4)
        last_y.append(net.put(a_sum.at[yy], a_last.at[d], device(yy, x, c, z)))
    for d in (1, 3, 2):
        net.arrived(to_y + d, b_land.at[d])
    fold_lines(lambda n, place: both[y, n, 1, place, :], b_land, b_sum)
    last_x = []
    for d in (1, 3, 2):
        xx = lax.rem(x + d, 4)
        last_x.append(net.put(b_sum.at[xx], b_last.at[d], device(y, xx, c, z)))
    pump(we_job)
    pump(out_job)
    o_swap.wait_recv()
    o_out[0] = o[0]
    o_out[1] = o[1]
    o_out[2] = o_in[0]
    o_out[3] = o_in[1]
    dq_swap.wait_recv()
    dq_out[0] = dq_own[0]
    dq_out[1] = dq_in[...]
    for copies, total, last, at, half in (
        (last_y, a_sum, a_last, y, 0),
        (last_x, b_sum, b_last, x, 1),
    ):
        for copy in copies:
            copy.wait_recv()
        value = total[at].astype(F32)
        for d in (1, 2, 3):
            value = value + last[d].astype(F32)
        dkv_out[half] = value.astype(BF)
    for job in (hg_job, out_job, we_job):
        for _ in job:
            pass
    for d in (1, 2, 3):
        net.left(to_x + d, a_land.at[d])
        net.left(to_y + d, b_land.at[d])
    net.finish()


def backward(bounds, q, o, do, lse, kv, dwe, hg, out_parts):
    return pl.pallas_call(
        backward_kernel,
        name="backward",
        out_shape=(
            jax.ShapeDtypeStruct((2, HALF, 2 * HD), BF),
            jax.ShapeDtypeStruct((2, HALF, QW), BF),
            jax.ShapeDtypeStruct((4, ROWS, QW), BF),
            jax.ShapeDtypeStruct((8, 16, WE), BF),
            jax.ShapeDtypeStruct((4, ROWS, D), BF),
            jax.ShapeDtypeStruct((ROWS, D), F32),
        ),
        in_specs=[SM] + [VM] * 4 + [ANY] * 4,
        out_specs=(VM, VM, VM, ANY, ANY, VM),
        scratch_shapes=[
            pltpu.VMEM((4, 4, 2, 2, HALF, 2 * HD), BF),
            pltpu.VMEM((2, ROWS, QW), BF),
            pltpu.VMEM((2, HALF, QW), BF),
            pltpu.VMEM((HALF, QW), BF),
            pltpu.VMEM((2, QPG, HD, HALF), BF),
            pltpu.VMEM((2, QPG, HD, HALF), BF),
            pltpu.VMEM((2, QPG, 1, HALF), F32),
            pltpu.VMEM((2, QPG, 1, HALF), F32),
            pltpu.VMEM((2, QPG, HD, HALF), F32),
            pltpu.VMEM((2, 2, 2, HALF, 2 * HD), BF),
            pltpu.VMEM((4, 4, 2, HALF, 2 * HD), BF),
            pltpu.VMEM((4, 4, 2, HALF, 2 * HD), BF),
            pltpu.VMEM((4, 4, HALF, 2 * HD), BF),
            pltpu.VMEM((4, 4, HALF, 2 * HD), BF),
            pltpu.VMEM((4, HALF, 2 * HD), BF),
            pltpu.VMEM((4, HALF, 2 * HD), BF),
            pltpu.VMEM((4, HALF, 2 * HD), BF),
            pltpu.VMEM((4, HALF, 2 * HD), BF),
        ]
        + scatter_scratch(96, WE, 1024)
        + [pltpu.VMEM((96, WE), BF), pltpu.VMEM((8, 16, WE), BF)]
        + group_scratch(D)
        + sems(72, 16),
        compiler_params=pltpu.CompilerParams(
            collective_id=7, has_side_effects=True, vmem_limit_bytes=VMEM_LIMIT
        ),
    )(bounds, q, o, do, lse, kv, dwe, hg, out_parts)


def close_kernel(normed_part, dwq, normed_out, dwq_out, *scratch):
    n_own, n_land, w_own, w_land, w_both = scratch[:5]
    w_s = scratch[5:13]
    w_rows, w_pieces = scratch[13:15]
    ss, rs, ls = scratch[15:]
    pos = position()
    y, x, c, z = pos
    greet(z_peers(pos) + xy_peers(pos) + [sibling(pos)])
    net = Net(ss, rs, ls)

    def normed():
        kept = net.keep(normed_part.at[z], n_own)
        copies = [
            net.put(normed_part.at[lax.rem(z + d, 4)], n_land.at[d - 1], device(y, x, c, z + d))
            for d in (1, 3, 2)
        ]
        yield
        yield
        kept.wait()
        for copy in copies:
            copy.wait_recv()
        add_four(normed_out, [n_own] + [n_land.at[d] for d in range(3)], ROWS, 32)

    def weights():
        yield from fold_cores(net, dwq, pos, w_own, w_land, w_both)
        yield from scatter_xy(net, w_both, pos, GROUP_W, *w_s, w_rows)
        w_pieces[...] = spread_rows(w_rows[...], 4)
        kept = net.keep(w_pieces.at[z], dwq_out.at[z])
        pieces = [
            net.put(w_pieces.at[lax.rem(z + d, 4)], dwq_out.at[z], device(y, x, c, z + d))
            for d in (1, 3, 2)
        ]
        yield
        kept.wait()
        for copy in pieces:
            copy.wait_recv()

    run_jobs([weights(), normed()])
    net.finish()


def close_exchange(normed_part, dwq):
    return pl.pallas_call(
        close_kernel,
        name="close_exchange",
        out_shape=(
            jax.ShapeDtypeStruct((ROWS, D), F32),
            jax.ShapeDtypeStruct((4, 16, GQ), BF),
        ),
        in_specs=[ANY] * 2,
        out_specs=(VM, ANY),
        scratch_shapes=[
            pltpu.VMEM((ROWS, D), BF),
            pltpu.VMEM((3, ROWS, D), BF),
            pltpu.VMEM((4, 4, 48, GQ), BF),
            pltpu.VMEM((4, 4, 48, GQ), BF),
            pltpu.VMEM((4, 4, 48, GQ), BF),
        ]
        + scatter_scratch(48, GQ, GROUP_W)
        + [pltpu.VMEM((48, GQ), BF), pltpu.VMEM((4, 16, GQ), BF)]
        + sems(32, 8),
        compiler_params=pltpu.CompilerParams(
            collective_id=8, has_side_effects=True, vmem_limit_bytes=VMEM_LIMIT
        ),
    )(normed_part, dwq)


def dot(left, right):
    return jnp.dot(left, right, preferred_element_type=F32)


def dot_rows(left, right):
    return lax.dot_general(left, right, (((0,), (0,)), ((), ())), preferred_element_type=F32)


def dot_cols(left, right):
    return lax.dot_general(left, right, (((1,), (1,)), ((), ())), preferred_element_type=F32)


def inverse_rms(values):
    return lax.rsqrt(jnp.mean(values * values, axis=-1, keepdims=True) + epsilon)


def route_table(logits, expert_ids):
    used = jnp.any(
        expert_ids[:, :, None] == jnp.arange(EXPERTS, dtype=jnp.int32)[None, None, :], axis=1
    )
    top = jnp.max(jnp.where(used, logits, LOW), axis=-1, keepdims=True)
    raised = jnp.where(used, jnp.exp(logits - top), 0.0)
    return raised / jnp.sum(raised, axis=-1, keepdims=True)


def pad_rows(value):
    return jnp.pad(value, ((0, 0), (0, 4), (0, 0)))


def per_device(
    tokens,
    seq_bounds,
    expert_ids,
    attn_gain,
    qkv_weight,
    out_weight,
    mlp_gain,
    router_weight,
    expert_gate_up,
    expert_down,
    shared_gate_up,
    shared_down,
    out_cotangent,
):
    small = jnp.concatenate(
        [
            router_weight,
            mlp_gain[:, None],
            attn_gain[:, None],
            jnp.zeros((12, SMALL - EXPERTS - 2), F32),
        ],
        axis=1,
    ).astype(BF)
    wq_pieces = pad_rows(
        jnp.concatenate(
            [
                jnp.transpose(qkv_weight.astype(BF).reshape(12, HK, GROUP_W), (1, 0, 2)),
                jnp.broadcast_to(small[None], (4, 12, SMALL)),
            ],
            axis=-1,
        )
    )
    wo_piece = jnp.pad(jnp.transpose(out_weight.astype(BF), (1, 0)), ((0, 4), (0, 0)))
    shared_cut = jnp.transpose(shared_gate_up.astype(BF).reshape(12, 2, 8, FSL), (1, 2, 0, 3))
    down_cut = jnp.transpose(shared_down.astype(BF).reshape(8, FSL, 12), (0, 2, 1))
    gate_up_low = expert_gate_up.astype(BF)
    we_pieces = pad_rows(
        jnp.concatenate(
            [
                gate_up_low[:, :, :FE],
                shared_cut[0],
                gate_up_low[:, :, FE:],
                shared_cut[1],
                jnp.transpose(expert_down.astype(BF), (0, 2, 1)),
                down_cut,
            ],
            axis=-1,
        )
    )
    used = jnp.any(
        expert_ids[:, :, None] == jnp.arange(SMALL, dtype=jnp.int32)[None, None, :], axis=1
    ).astype(F32)
    fwd = forward(seq_bounds, tokens, wq_pieces, wo_piece, we_pieces, out_cotangent, used)
    w_qkv = fwd["wq"].reshape(D, WQ)[:, :GROUP_W]
    gain_attn = fwd["gains"][EXPERTS + 1]
    rows_group = fwd["tok"].reshape(BLK, D).astype(F32)
    scaled_group = rows_group * inverse_rms(rows_group)
    normed = (scaled_group * gain_attn).astype(BF)
    hidden, hidden_grad = fwd["hidden"], fwd["hidden_grad"]
    dkv_own, dq_all, attn_all, dwe_pieces, hidden_group, out_sum = backward(
        seq_bounds,
        *(fwd[k] for k in ("q", "o", "do", "lse", "kv", "dwe", "hidden_low", "out_parts")),
    )
    output = (hidden + out_sum).astype(BF)
    joined_grad = jnp.concatenate(
        [dq_all.reshape(BLK, QW), dkv_own.reshape(BLK, 2 * HD)], axis=-1
    )
    normed_part = dot_cols(joined_grad, w_qkv)
    attn_gain_part = jnp.sum(normed_part * scaled_group, axis=0)
    mixed_group = attn_all.reshape(BLK, QW)
    small_grad = fwd["small"] + jnp.where(
        jnp.arange(SMALL)[None, :] == EXPERTS + 1, attn_gain_part[:, None], 0.0
    ).astype(BF)
    dwq = jnp.concatenate(
        [
            dot_rows(normed, joined_grad).astype(BF),
            dot_rows(hidden_group.reshape(BLK, D), mixed_group).astype(BF),
            small_grad,
        ],
        axis=-1,
    )
    normed_grad, dwq_pieces = close_exchange(
        normed_part.astype(BF).reshape(4, ROWS, D), dwq.reshape(4, 4, 2, 48, GQ)
    )
    token_rows = tokens.astype(F32)
    token_scale = inverse_rms(token_rows)
    token_unit = token_rows * token_scale
    dn_tokens = normed_grad * gain_attn
    tokens_grad = hidden_grad + token_scale * (
        dn_tokens - token_unit * jnp.mean(dn_tokens * token_unit, axis=-1, keepdims=True)
    )
    dwq_own = dwq_pieces[:, :12].astype(F32)
    qkv_out = jnp.transpose(dwq_own[:, :, :GROUP_W], (1, 0, 2)).reshape(12, QKV)
    wo_out = jnp.transpose(dwq_own[:, :, GROUP_W : GROUP_W + QW], (0, 2, 1)).reshape(D, 12)
    small_out = jnp.sum(dwq_own[:, :, GROUP_W + QW :], axis=0)
    dwe_own = dwe_pieces[:, :12].astype(F32)
    gate_up_out = jnp.concatenate([dwe_own[:, :, :FE], dwe_own[:, :, UP : UP + FE]], axis=-1)
    down_out = jnp.transpose(dwe_own[:, :, 2 * UP : 2 * UP + FE], (0, 2, 1))
    shared_out = jnp.transpose(
        jnp.stack([dwe_own[:, :, FE:UP], dwe_own[:, :, UP + FE : 2 * UP]]), (2, 0, 1, 3)
    ).reshape(12, 2 * FS)
    shared_down_out = jnp.transpose(dwe_own[:, :, 2 * UP + FE :], (0, 2, 1)).reshape(FS, 12)
    return (
        output,
        tokens_grad,
        small_out[:, EXPERTS + 1],
        qkv_out,
        wo_out,
        small_out[:, EXPERTS],
        small_out[:, :EXPERTS],
        gate_up_out,
        down_out,
        shared_out,
        shared_down_out,
    )


def solution(mesh):
    both = ("blk", "head")
    in_specs = (
        P(both, None),
        P(),
        P(both, None),
        P(both),
        P(both, None),
        P(None, both),
        P(both),
        P(both, None),
        P(None, both, None),
        P(None, None, both),
        P(both, None),
        P(None, both),
        P(both, None),
    )
    out_specs = (
        P(both, None),
        P(both, None),
        P(both),
        P(both, None),
        P(None, both),
        P(both),
        P(both, None),
        P(None, both, None),
        P(None, None, both),
        P(both, None),
        P(None, both),
    )
    return jax.shard_map(
        per_device, mesh=mesh, in_specs=in_specs, out_specs=out_specs, check_vma=False
    )
```

```python
import functools

import jax
import jax.numpy as jnp
from jax import lax
from jax.experimental import pallas as pl
from jax.experimental.pallas import tpu as pltpu
from jax.sharding import PartitionSpec as P

D = 1536
HQ = 12
HK = 4
HD = 128
FE = 512
FS = 1024
EXPERTS = 8
QPG = 3
GROUP_W = 640
QKV = 2560
ROWS = 128
BLK = 512
HALF = 256
QW = 384
SMALL = 128
WQ = GROUP_W + SMALL
GQ = GROUP_W + QW + SMALL
FSL = FS // 8
UP = FE + FSL
WE = 3 * UP
NBLK = 32
MESH = pl.DeviceIdType.MESH
BF = jnp.bfloat16
F32 = jnp.float32
epsilon = 1e-05
LOW = -1e30
LOG2E = 1.4426950408889634
SCALE = HD**-0.5
VMEM_LIMIT = 60 * 1024 * 1024

ANY = pl.BlockSpec(memory_space=pl.ANY)
VM = pl.BlockSpec(memory_space=pltpu.VMEM)


def position():
    b = lax.axis_index("blk")
    z = lax.axis_index("head")
    return b // 8, lax.rem(b // 2, 4), lax.rem(b, 2), z


def device(y, x, c, z):
    return ((lax.rem(y, 4) * 4 + lax.rem(x, 4)) * 2 + lax.rem(c, 2), lax.rem(z, 4))


def mirror(pos):
    y, x, c, z = pos
    return 3 - y, 3 - x, 1 - c, z


def greet(targets):
    barrier = pltpu.get_barrier_semaphore()
    for target in targets:
        pl.semaphore_signal(barrier, inc=1, device_id=target, device_id_type=MESH)
    pl.semaphore_wait(barrier, len(targets))


def z_peers(pos):
    y, x, c, z = pos
    return [device(y, x, c, z + d) for d in (1, 2, 3)]


def xy_peers(pos):
    y, x, c, z = pos
    return [device(y, x + d, c, z) for d in (1, 2, 3)] + [
        device(y + d, x, c, z) for d in (1, 2, 3)
    ]


def sibling(pos):
    y, x, c, z = pos
    return device(y, x, c + 1, z)


def other_column(pos):
    y, x, c, z = pos
    return [device(y, x, c + 1, z + d) for d in (0, 1, 2, 3)]


class Net:
    def __init__(self, send_sems, recv_sems, local_sems):
        self.send_sems, self.recv_sems, self.local_sems = send_sems, recv_sems, local_sems
        self.count = 0
        self.locals = 0
        self.started = []

    def put(self, src, dst, target):
        k = self.count
        self.count += 1
        copy = pltpu.make_async_remote_copy(
            src_ref=src,
            dst_ref=dst,
            send_sem=self.send_sems.at[k],
            recv_sem=self.recv_sems.at[k],
            device_id=target,
            device_id_type=MESH,
        )
        copy.start()
        self.started.append(copy)
        return copy

    def reserve(self, count):
        k = self.count
        self.count += count
        return k

    def put_at(self, k, src, dst, target):
        copy = self.copy_at(k, src, dst, target)
        copy.start()

    def copy_at(self, k, src, dst, target):
        return pltpu.make_async_remote_copy(
            src_ref=src,
            dst_ref=dst,
            send_sem=self.send_sems.at[k],
            recv_sem=self.recv_sems.at[k],
            device_id=target,
            device_id_type=MESH,
        )

    def arrived(self, k, ref):
        pltpu.make_async_copy(ref, ref, self.recv_sems.at[k]).wait()

    def left(self, k, ref):
        pltpu.make_async_copy(ref, ref, self.send_sems.at[k]).wait()

    def keep(self, src, dst):
        k = self.locals
        self.locals += 1
        copy = pltpu.make_async_copy(src, dst, self.local_sems.at[k])
        copy.start()
        return copy

    def finish(self):
        for copy in self.started:
            copy.wait_send()


def sems(remote, local):
    return [
        pltpu.SemaphoreType.DMA((remote,)),
        pltpu.SemaphoreType.DMA((remote,)),
        pltpu.SemaphoreType.DMA((local,)),
    ]


def run_jobs(jobs):
    live = list(jobs)
    while live:
        still = []
        for job in live:
            try:
                next(job)
                still.append(job)
            except StopIteration:
                pass
        live = still


def all_of(start, length):
    return pl.ds(start, length)


def gather_xy(net, land, own, cut, pos, with_core):
    y, x, c, z = pos
    width = own.shape[-1]
    first, second = pl.ds(0, cut), pl.ds(cut, width - cut)

    def place(yy, xx, columns):
        if with_core:
            return land.at[yy, xx, c, :, columns]
        return land.at[yy, xx, :, columns]

    whole = slice(None)
    mine = land.at[y, x, c] if with_core else land.at[y, x]
    kept = net.keep(own, mine)
    along_x = [
        net.put(own.at[:, first], place(y, x, first), device(y, x + d, c, z)) for d in (1, 3, 2)
    ]
    along_y = [
        net.put(own.at[:, second], place(y, x, second), device(y + d, x, c, z)) for d in (1, 3, 2)
    ]
    yield
    kept.wait()
    for copy in along_x:
        copy.wait_recv()
    row = place(y, whole, first)
    then_y = [net.put(row, row, device(y + d, x, c, z)) for d in (1, 3)]
    passed = []
    if with_core:
        passed.append(net.put(row, row, sibling(pos)))
    for copy in along_y:
        copy.wait_recv()
    column = place(whole, x, second)
    then_x = [net.put(column, column, device(y, x + d, c, z)) for d in (1, 3)]
    if with_core:
        passed.append(net.put(column, column, sibling(pos)))
    yield
    relays = []
    for d, half in ((1, pl.ds(0, 2)), (3, pl.ds(2, 2))):
        yy, xx = lax.rem(y + 4 - d, 4), lax.rem(x + 4 - d, 4)
        then_y[d // 2].wait_recv()
        part = place(yy, half, first)
        relays.append(net.put(part, part, device(y + d, x, c, z)))
        then_x[d // 2].wait_recv()
        part = place(half, xx, second)
        relays.append(net.put(part, part, device(y, x + d, c, z)))
        if with_core:
            for got in (place(yy, whole, first), place(whole, xx, second)):
                passed.append(net.put(got, got, sibling(pos)))
    yield
    for copy in relays:
        copy.wait_recv()
    if with_core:
        yy, xx = lax.rem(y + 2, 4), lax.rem(x + 2, 4)
        for got in (place(yy, whole, first), place(whole, xx, second)):
            passed.append(net.put(got, got, sibling(pos)))
    yield
    for copy in passed:
        copy.wait_recv()


def pick_rows(groups):
    rows = lax.broadcasted_iota(jnp.int32, (12 * groups, 16 * groups), 0)
    cols = lax.broadcasted_iota(jnp.int32, (12 * groups, 16 * groups), 1)
    piece = cols // 16
    within = cols - piece * 16
    return jnp.where((rows == piece * 12 + within) & (within < 12), 1.0, 0.0).astype(BF)


def squeeze_rows(pieces, groups):
    flat = pieces.reshape(groups * 16, pieces.shape[-1])
    return jnp.dot(pick_rows(groups), flat, preferred_element_type=F32).astype(BF)


def spread_rows(rows, groups):
    wide = lax.dot_general(
        pick_rows(groups), rows, (((0,), (0,)), ((), ())), preferred_element_type=F32
    )
    return wide.astype(BF).reshape(groups, 16, rows.shape[-1])


def mult(value, of):
    return pl.multiple_of(value, of)


def transposed(value):
    return jnp.transpose(value.astype(F32), (1, 0)).astype(BF)


SM = pl.BlockSpec(memory_space=pltpu.SMEM)


def home_block(pos, z):
    y, x, c, _ = pos
    b = (y * 4 + x) * 2 + c
    return jnp.where(z < 2, b, NBLK - 1 - b)


RW = D + SMALL
FLOOR = -1e29
ROW_ROW = (((1,), (1,)), ((), ()))
COL_COL = (((0,), (0,)), ((), ()))
EXP_SCALE = SCALE * LOG2E


def exchange_heads(to_tokens, pos, src_at, dst_at, ss, rs):
    y, x, c, z = pos
    b = (y * 4 + x) * 2 + c

    def ends(k):
        target = (home_block(pos, k if to_tokens else z), k)
        return src_at(k), dst_at(z), target, (target[0] == b) & (k == z)

    def remote(k):
        part, slot, target, _ = ends(k)
        return pltpu.make_async_remote_copy(
            src_ref=part,
            dst_ref=slot,
            send_sem=ss.at[k],
            recv_sem=rs.at[z],
            device_id=target,
            device_id_type=MESH,
        )

    def start(k):
        part, slot, _, stays = ends(k)

        @pl.when(stays)
        def _():
            pltpu.make_async_copy(part, slot, rs.at[z]).start()

        @pl.when(jnp.logical_not(stays))
        def _():
            remote(k).start()

    def wait():
        for k in range(4):
            pltpu.make_async_copy(dst_at(k), dst_at(k), rs.at[k]).wait()
        for k in range(4):

            @pl.when(jnp.logical_not(ends(k)[3]))
            def _():
                remote(k).wait_send()

    return start, wait


def turn(n):
    return jnp.where(n == 2, 3, jnp.where(n == 3, 2, n))


def forward_kernel(
    bounds, tok, wq, wo, we, gy, used,
    wo_out, wq_out, kv_out, q_out, o_out, lse_out, tok_out,
    hidden_out, hidden_grad_out, hidden_low_out, gains_out, small_out, do_out, out_parts, dwe_out,
    wq_z, wq_slab, wq_land, wo_z, wo_slab, wo_land, we_z, we_slab, we_land, tok_all, kv_land, q_in,
    qt, m_ref, l_ref, acc, mixed, own_rows, rows_all, gy_all, inner_all, pre_all, parts, out_stage,
    core_land, both, z_land, dwe_stage, mixed_grad, do_in, ss, rs, ls, hs, hr, gs, gr, hs2, hr2,
):
    pos = position()
    y, x, c, z = pos
    b = (y * 4 + x) * 2 + c
    my, mx, mc, _ = mirror(pos)
    greet(
        z_peers(pos)
        + xy_peers(pos)
        + [device(my, mx, mc, d) for d in range(4)]
        + other_column(pos)
    )
    net = Net(ss, rs, ls)

    wq_pieces = [
        net.put(wq.at[lax.rem(z + d, 4)], wq_z.at[z], device(y, x, c, z + d)) for d in (1, 3, 2)
    ]
    wq_kept = net.keep(wq.at[z], wq_z.at[z])

    def out_weights():
        pieces = [net.put(wo, wo_z.at[z], device(y, x, c, z + d)) for d in (1, 3, 2)]
        kept = net.keep(wo, wo_z.at[z])
        yield
        kept.wait()
        for copy in pieces:
            copy.wait_recv()
        wo_slab[...] = squeeze_rows(wo_z[...], 4)
        yield from gather_xy(net, wo_land, wo_slab, D // 2, pos, True)

    def expert_weights():
        me = c * 4 + z
        pieces = []
        for dc in (0, 1):
            for d in (0, 1, 3, 2):
                if (dc, d) == (0, 0):
                    continue
                cc, zz = lax.rem(c + dc, 2), lax.rem(z + d, 4)
                pieces.append(net.put(we.at[cc * 4 + zz], we_z.at[me], device(y, x, cc, zz)))
        kept = net.keep(we.at[me], we_z.at[me])
        yield
        kept.wait()
        for copy in pieces:
            copy.wait_recv()
        we_slab[...] = squeeze_rows(we_z[...], 8)
        yield from gather_xy(net, we_land, we_slab, 1024, pos, False)

    def cotangent():
        mine = gy_all.at[z, c]
        kept = net.keep(gy, mine)
        copies = [(d, net.put(gy, mine, device(y, x, c, z + d))) for d in (1, 3, 2)]
        passed = [net.put(gy, mine, sibling(pos))]
        yield
        for d, copy in copies:
            copy.wait_recv()
            got = gy_all.at[lax.rem(z + 4 - d, 4), c]
            passed.append(net.put(got, got, sibling(pos)))
        yield
        kept.wait()
        for copy in passed:
            copy.wait_recv()

    def pump(job):
        try:
            next(job)
        except StopIteration:
            pass

    wo_job, we_job, gy_job = out_weights(), expert_weights(), cotangent()
    pump(wo_job)
    tok_copies = [net.put(tok, tok_all.at[z], device(y, x, c, z + d)) for d in (1, 3, 2)]
    tok_kept = net.keep(tok, tok_all.at[z])
    pump(we_job)
    pump(gy_job)

    wq_kept.wait()
    for copy in wq_pieces:
        copy.wait_recv()
    wq_slab[...] = squeeze_rows(wq_z[...], 4)
    wq_job = gather_xy(net, wq_land, wq_slab, QW, pos, True)
    pump(wq_job)
    pump(wo_job)
    pump(wq_job)
    pump(wo_job)
    pump(wq_job)
    pump(wq_job)
    pump(wq_job)
    wq_saved = net.keep(wq_land, wq_out)

    for i in range(4):
        part = wq_land[i, :, :, :, GROUP_W:].reshape(QW, SMALL)
        one_hot = (
            lax.broadcasted_iota(jnp.int32, (16, SMALL), 0)
            == lax.broadcasted_iota(jnp.int32, (16, SMALL), 1)
        ).astype(BF)
        gains_out[:, i * QW : (i + 1) * QW] = lax.dot_general(
            one_hot, part, (((1,), (1,)), ((), ())), preferred_element_type=F32
        )
    tok_kept.wait()
    for copy in tok_copies:
        copy.wait_recv()
    tok_saved = net.keep(tok_all, tok_out)
    gain_attn = gains_out[EXPERTS + 1 : EXPERTS + 2, :]

    def project(i, carried):
        rows = tok_all[i].astype(F32)
        unit = rows * lax.rsqrt(jnp.mean(rows * rows, axis=-1, keepdims=True) + epsilon)
        low = (unit * gain_attn).astype(BF)
        weights = wq_land[...].reshape(D, WQ)[:, :GROUP_W]
        joined = jnp.dot(low, weights, preferred_element_type=F32).astype(BF)
        half, place = i // 2, pl.ds(mult(lax.rem(i, 2) * ROWS, ROWS), ROWS)
        q_out[half, place, :] = joined[:, :QW]
        kv_land[y, x, c, half, place, :] = joined[:, QW:]
        return carried

    lax.fori_loop(0, 4, project, 0)

    swapped = net.put(q_out.at[1], q_in, device(my, mx, mc, z))
    whole = slice(None)
    along_x, along_y = [], []
    even, odd = kv_land.at[y, x, c, 0], kv_land.at[y, x, c, 1]
    for d in (1, 3, 2):
        along_x.append(net.put(even, even, device(y, x + d, c, z)))
        along_y.append(net.put(odd, odd, device(y + d, x, c, z)))
    m_ref[...] = jnp.full_like(m_ref, FLOOR)
    l_ref[...] = jnp.zeros_like(l_ref)
    acc[...] = jnp.zeros_like(acc)
    lo, hi = 2 * b, 2 * (NBLK - b) - 1
    starts = []
    for chunk in (lo, hi):
        at = chunk * HALF + lax.broadcasted_iota(jnp.int32, (1, HALF), 1)
        first = jnp.where(at >= bounds[1], bounds[1], jnp.where(at >= bounds[0], bounds[0], 0))
        starts.append((at, first))
    for copy in along_x:
        copy.wait_recv()
    row = kv_land.at[y, whole, c, 0]
    from_y, crossed_y, crossed_x = net.reserve(4), net.reserve(4), net.reserve(4)
    for d in (1, 3):
        net.put_at(from_y + d, row, row, device(y + d, x, c, z))
    net.put_at(crossed_y, row, row, sibling(pos))
    for copy in along_y:
        copy.wait_recv()
    column = kv_land.at[whole, x, c, 1]
    from_x = net.reserve(4)
    for d in (1, 3):
        net.put_at(from_x + d, column, column, device(y, x + d, c, z))
    relay_y, relay_x = net.reserve(4), net.reserve(4)
    net.put_at(crossed_x, column, column, sibling(pos))
    pump(wo_job)
    pump(wo_job)
    swapped.wait_recv()
    for h in range(QPG):
        qt[0, h] = transposed(q_out[0, :, h * HD : (h + 1) * HD])
        qt[1, h] = transposed(q_in[:, h * HD : (h + 1) * HD])
    q_out[2] = q_in[...]

    def update(ids, yy, xx, cc, half, masked):
        k_rows = kv_land[yy, xx, cc, half, :, :HD]
        v_rows = kv_land[yy, xx, cc, half, :, HD:]
        work = [(i, h) for i in ids for h in range(QPG)]
        scores = [jnp.dot(k_rows, qt[i, h], preferred_element_type=F32) for i, h in work]
        if masked:
            chunk = ((yy * 4 + xx) * 2 + cc) * 2 + half
            key_at = chunk * HALF + lax.broadcasted_iota(jnp.int32, (HALF, HALF), 0)
            allowed = {i: (key_at >= starts[i][1]) & (key_at <= starts[i][0]) for i in ids}
            scores = [jnp.where(allowed[i], s, LOW) for (i, _), s in zip(work, scores)]
        m_old = [m_ref[i, h] for i, h in work]
        l_old = [l_ref[i, h] for i, h in work]
        a_old = [acc[i, h] for i, h in work]
        m_new = [jnp.maximum(m, jnp.max(s, axis=0, keepdims=True)) for m, s in zip(m_old, scores)]
        p = [jnp.exp2((s - m) * EXP_SCALE) for s, m in zip(scores, m_new)]
        alpha = [jnp.exp2((m - n) * EXP_SCALE) for m, n in zip(m_old, m_new)]
        pv = [
            lax.dot_general(
                v_rows, w.astype(BF), (((0,), (0,)), ((), ())), preferred_element_type=F32
            )
            for w in p
        ]
        for n, (i, h) in enumerate(work):
            m_ref[i, h] = m_new[n]
            l_ref[i, h] = l_old[n] * alpha[n] + jnp.sum(p[n], axis=0, keepdims=True)
            acc[i, h] = a_old[n] * alpha[n] + pv[n]

    late = 2 * NBLK - 2

    def chunk_step(yy, xx, cc, half):
        chunk = ((yy * 4 + xx) * 2 + cc) * 2 + half
        in_lo, in_hi = chunk <= lo, chunk <= hi
        masked = (chunk <= 1) | (chunk == lo) | (chunk == hi)
        early = chunk < late
        plain = early & jnp.logical_not(masked)

        @pl.when(plain & in_lo & in_hi)
        def _():
            update((0, 1), yy, xx, cc, half, False)

        @pl.when(plain & in_lo & jnp.logical_not(in_hi))
        def _():
            update((0,), yy, xx, cc, half, False)

        @pl.when(plain & in_hi & jnp.logical_not(in_lo))
        def _():
            update((1,), yy, xx, cc, half, False)

        @pl.when(early & masked)
        def _():
            update((0, 1), yy, xx, cc, half, True)

    def stage(n, carried):
        d = turn(n)
        yy, xx = lax.rem(y + 4 - d, 4), lax.rem(x + 4 - d, 4)
        row, column = kv_land.at[yy, whole, c, 0], kv_land.at[whole, xx, c, 1]

        @pl.when(n == 1)
        def _():
            for e in (1, 3):
                near_y, near_x = lax.rem(y + 4 - e, 4), lax.rem(x + 4 - e, 4)
                part = pl.ds(e - 1, 2)
                net.arrived(from_y + e, row)
                line = kv_land.at[near_y, part, c, 0]
                net.put_at(relay_y + e, line, line, device(y + e, x, c, z))
                net.arrived(from_x + e, column)
                line = kv_land.at[part, near_x, c, 1]
                net.put_at(relay_x + e, line, line, device(y, x + e, c, z))
            for e in (1, 3):
                near_y, near_x = lax.rem(y + 4 - e, 4), lax.rem(x + 4 - e, 4)
                line = kv_land.at[near_y, whole, c, 0]
                net.put_at(crossed_y + e, line, line, sibling(pos))
                line = kv_land.at[whole, near_x, c, 1]
                net.put_at(crossed_x + e, line, line, sibling(pos))

        @pl.when(n == 3)
        def _():
            for e in (1, 3):
                part = pl.ds(e - 1, 2)
                net.arrived(relay_y + e, kv_land.at[yy, part, c, 0])
                net.arrived(relay_x + e, kv_land.at[part, xx, c, 1])
            net.put_at(crossed_y + 2, row, row, sibling(pos))
            net.put_at(crossed_x + 2, column, column, sibling(pos))

        net.arrived(crossed_y + d, kv_land.at[yy, whole, 1 - c, 0])
        net.arrived(crossed_x + d, kv_land.at[whole, xx, 1 - c, 1])

        def step(t, carried):
            half = t // 8
            chunk_step(
                jnp.where(half == 0, yy, (t - 8) // 2),
                jnp.where(half == 0, t // 2, xx),
                lax.rem(t, 2),
                half,
            )
            return carried

        lax.fori_loop(0, 16, step, 0)
        return carried

    lax.fori_loop(0, 2, stage, 0)
    pump(we_job)
    lax.fori_loop(2, 3, stage, 0)
    pump(we_job)
    lax.fori_loop(3, 4, stage, 0)
    for n in range(4):
        for k in (crossed_y, crossed_x):
            net.left(k + n, row)
    for n in (1, 3):
        net.left(from_y + n, row)
        net.left(from_x + n, column)
        net.left(relay_y + n, kv_land.at[y, pl.ds(0, 2), c, 0])
        net.left(relay_x + n, kv_land.at[pl.ds(0, 2), x, c, 1])
    kv_saved = net.keep(kv_land, kv_out)

    for i, chunk in enumerate((lo, hi)):

        @pl.when(chunk >= late)
        def _():
            third = starts[i][0] >= bounds[1]
            for h in range(QPG):
                m_ref[i, h] = jnp.where(third, FLOOR, m_ref[i, h])
                l_ref[i, h] = jnp.where(third, 0.0, l_ref[i, h])
                acc[i, h] = jnp.where(third, 0.0, acc[i, h])
            lax.fori_loop(0, 2, lambda half, _: update((i,), 3, 3, 1, half, True), None)

    start, wait_mixed = exchange_heads(
        True, pos, lambda k: o_out.at[k], lambda g: mixed.at[:, pl.ds(mult(g * QW, QW), QW)], hs, hr
    )
    for i in range(2):
        for h in range(QPG):
            total = l_ref[i, h]
            lse_out[i, h] = m_ref[i, h] * EXP_SCALE + jnp.log(total) * LOG2E
            value = jnp.transpose(acc[i, h] / total, (1, 0)).astype(BF)
            o_out[2 * i, :, h * HD : (h + 1) * HD] = value[:ROWS]
            o_out[2 * i + 1, :, h * HD : (h + 1) * HD] = value[ROWS:]
        start(2 * i)
        start(2 * i + 1)

    pump(wo_job)
    pump(wo_job)
    wo_saved = net.keep(wo_land, wo_out)
    wait_mixed()
    pump(we_job)

    def add_hidden(i, carried):
        columns = pl.ds(mult(i * QW, QW), QW)
        hidden_out[:, columns] = tok[:, columns].astype(F32) + lax.dot_general(
            mixed[...], wo_land[i].reshape(QW, D), ROW_ROW, preferred_element_type=F32
        )
        return carried

    lax.fori_loop(0, 4, add_hidden, 0)
    hidden = hidden_out[...]
    unit = hidden * lax.rsqrt(jnp.mean(hidden * hidden, axis=-1, keepdims=True) + epsilon)
    low = (unit * gains_out[EXPERTS : EXPERTS + 1, :]).astype(BF)
    own_rows[:, :D] = low
    small_weights = wq_land[:, :, :, :, GROUP_W:].reshape(D, SMALL)
    logits = jnp.dot(low, small_weights, preferred_element_type=F32)
    is_used = used[...] > 0.0
    top = jnp.max(jnp.where(is_used, logits, LOW), axis=-1, keepdims=True)
    raised = jnp.where(is_used, jnp.exp(logits - top), 0.0)
    route = raised / jnp.sum(raised, axis=-1, keepdims=True)
    coarse = route.astype(BF).astype(F32)
    own_rows[:, D:] = (coarse + pltpu.roll(route - coarse, EXPERTS, 1)).astype(BF)

    mine = rows_all.at[z, c]
    rows_kept = net.keep(own_rows, mine)
    from_z, crossed_z = net.reserve(4), net.reserve(4)
    relay_z = net.reserve(4)
    for d in (1, 3):
        net.put_at(from_z + d, own_rows, mine, device(y, x, c, z + d))
    net.put_at(crossed_z, own_rows, mine, sibling(pos))
    for job in (gy_job, we_job, wo_job, wq_job):
        for _ in job:
            pass
    rows_kept.wait()
    to_core, to_z = net.reserve(4), net.reserve(4)
    me = c * 4 + z
    gate_columns, up_columns, down_columns = (slice(i * UP, (i + 1) * UP) for i in range(3))

    def weights(columns):
        return we_land[:, :, :, columns].reshape(D, UP)

    def finish_block(n):
        d, slot = turn(n), lax.rem(n, 2)
        zz = lax.rem(z + 4 - d, 4)
        net.arrived(to_core + n, core_land.at[n])
        both[n] = (parts[slot, c].astype(F32) + core_land[n].astype(F32)).astype(BF)
        net.left(to_core + n, parts.at[slot, 1 - c])

        @pl.when(n > 0)
        def _():
            net.put_at(to_z + d, both.at[n], z_land.at[d], device(y, x, c, zz))

    def expert_block(n, carried):
        d, slot = turn(n), lax.rem(n, 2)
        zz = lax.rem(z + 4 - d, 4)
        got = rows_all.at[zz, c]

        @pl.when(n == 1)
        def _():
            for e in (1, 3):
                near = rows_all.at[lax.rem(z + 4 - e, 4), c]
                net.arrived(from_z + e, near)
                part = near.at[pl.ds((e - 1) * 32, 64)]
                net.put_at(relay_z + e, part, part, device(y, x, c, z + e))
                net.put_at(crossed_z + e, near, near, sibling(pos))

        @pl.when(n == 3)
        def _():
            for e in (1, 3):
                net.arrived(relay_z + e, got.at[pl.ds((e - 1) * 32, 64)])
            net.put_at(crossed_z + 2, got, got, sibling(pos))

        net.arrived(crossed_z + d, rows_all.at[zz, 1 - c])

        @pl.when(n > 1)
        def _():
            pltpu.make_async_copy(out_stage.at[slot], out_stage.at[slot], gs.at[slot]).wait()

        rows = rows_all[zz].reshape(2 * ROWS, RW)
        x_rows, lanes = rows[:, :D], rows[:, D:].astype(F32)
        lane = lax.broadcasted_iota(jnp.int32, lanes.shape, 1)
        route = jnp.sum(
            jnp.where((lane == me) | (lane == me + EXPERTS), lanes, 0.0), axis=-1, keepdims=True
        )
        gy_rows = gy_all[zz].reshape(2 * ROWS, D)
        gate = jnp.dot(x_rows, weights(gate_columns), preferred_element_type=F32)
        up = jnp.dot(x_rows, weights(up_columns), preferred_element_type=F32)
        raw = jnp.dot(gy_rows, weights(down_columns), preferred_element_type=F32)
        unit_lane = lax.broadcasted_iota(jnp.int32, gate.shape, 1)
        share = jnp.where(unit_lane < FE, route, 1.0)
        sig = 1.0 / (1.0 + jnp.exp(-gate))
        silu = gate * sig
        inner = silu * up
        scaled = (inner * share).astype(BF)
        inner_all[zz] = scaled
        route_grad = jnp.sum(inner[:, :FE] * raw[:, :FE], axis=-1, keepdims=True)
        inner_grad = raw * share
        pre_grad = jnp.concatenate(
            [inner_grad * up * (sig + silu * (1.0 - sig)), inner_grad * silu], axis=-1
        ).astype(BF)
        pre_all[zz] = pre_grad
        out_stage[slot] = (
            lax.dot_general(scaled, weights(down_columns), ROW_ROW, preferred_element_type=F32)
            .astype(BF)
            .reshape(2, ROWS, D)
        )
        pltpu.make_async_copy(out_stage.at[slot], out_parts.at[zz], gs.at[slot]).start()
        rows_grad = lax.dot_general(
            pre_grad[:, :UP], weights(gate_columns), ROW_ROW, preferred_element_type=F32
        ) + lax.dot_general(
            pre_grad[:, UP:], weights(up_columns), ROW_ROW, preferred_element_type=F32
        )
        parts[slot, :, :, :D] = rows_grad.astype(BF).reshape(2, ROWS, D)
        high = route_grad.astype(BF).astype(F32)
        parts[slot, :, :, D:] = (
            jnp.where(lane == me, high, 0.0) + jnp.where(lane == me + EXPERTS, route_grad - high, 0.0)
        ).astype(BF).reshape(2, ROWS, SMALL)
        net.put_at(to_core + n, parts.at[slot, 1 - c], core_land.at[n], sibling(pos))

        @pl.when(n > 0)
        def _():
            finish_block(n - 1)

        return carried

    lax.fori_loop(0, 4, expert_block, 0)
    finish_block(3)
    for slot in range(2):
        pltpu.make_async_copy(out_stage.at[slot], out_stage.at[slot], gs.at[slot]).wait()

    def weight_grads(t, carried):
        slot = lax.rem(t, 2)

        @pl.when(t > 1)
        def _():
            pltpu.make_async_copy(dwe_stage.at[slot], dwe_stage.at[slot], gr.at[slot]).wait()

        columns = pl.ds(mult(t * QW, QW), QW)
        for i in range(3):
            value = jnp.zeros((QW, UP), F32)
            for k in range(4):
                left = (rows_all if i < 2 else gy_all)[k, :, :, columns].reshape(2 * ROWS, QW)
                right = pre_all[k, :, i * UP : (i + 1) * UP] if i < 2 else inner_all[k]
                value = value + lax.dot_general(left, right, COL_COL, preferred_element_type=F32)
            dwe_stage[slot, :, :, i * UP : (i + 1) * UP] = value.astype(BF).reshape(4, 96, UP)
        pltpu.make_async_copy(dwe_stage.at[slot], dwe_out.at[t], gr.at[slot]).start()
        return carried

    lax.fori_loop(0, 4, weight_grads, 0)

    for d in (1, 2, 3):
        net.arrived(to_z + d, z_land.at[d])

    def total(columns):
        value = both[0, :, columns].astype(F32)
        for d in (1, 2, 3):
            value = value + z_land[d, :, columns].astype(F32)
        return value

    lane = lax.broadcasted_iota(jnp.int32, (ROWS, SMALL), 1)
    route_grads = total(slice(D, RW))
    route_grads = route_grads + pltpu.roll(route_grads, SMALL - EXPERTS, 1)
    logits_grad = (
        route * (route_grads - jnp.sum(route * route_grads, axis=-1, keepdims=True))
    ).astype(BF)
    normed_grad = total(slice(0, D)) + lax.dot_general(
        logits_grad, small_weights, ROW_ROW, preferred_element_type=F32
    )
    hidden = hidden_out[...]
    scale = lax.rsqrt(jnp.mean(hidden * hidden, axis=-1, keepdims=True) + epsilon)
    unit = hidden * scale
    dn = normed_grad * gains_out[EXPERTS : EXPERTS + 1, :]
    hidden_grad = gy_all[z, c].astype(F32) + scale * (
        dn - unit * jnp.mean(dn * unit, axis=-1, keepdims=True)
    )
    hidden_grad_out[...] = hidden_grad
    hidden_low = hidden_grad.astype(BF)
    hidden_low_out[...] = hidden_low
    total_grad = jnp.zeros((ROWS, D), F32)
    for i in range(4):
        total_grad = total_grad + jnp.dot(
            hidden_low[:, i * QW : (i + 1) * QW],
            wo_land[i].reshape(QW, D),
            preferred_element_type=F32,
        )
    start, wait_heads = exchange_heads(
        False, pos, lambda g: mixed_grad.at[g], lambda k: do_in.at[k], hs2, hr2
    )
    for g in range(4):
        mixed_grad[g] = total_grad[:, g * QW : (g + 1) * QW].astype(BF)
        start(g)
    gain_column = jnp.where(lane == EXPERTS, 1.0, 0.0).astype(BF)
    small_out[...] = (
        lax.dot_general(own_rows[:, :D], logits_grad, COL_COL, preferred_element_type=F32)
        + lax.dot_general(
            (normed_grad * unit).astype(BF), gain_column, COL_COL, preferred_element_type=F32
        )
    ).astype(BF)
    for n in range(4):
        net.left(crossed_z + n, own_rows)
        if n:
            net.left(to_z + n, both.at[n])
    for n in (1, 3):
        net.left(from_z + n, own_rows)
        net.left(relay_z + n, own_rows.at[pl.ds(0, 64)])
    for slot in range(2):
        pltpu.make_async_copy(dwe_stage.at[slot], dwe_stage.at[slot], gr.at[slot]).wait()
    wait_heads()
    do_out[...] = do_in[...]
    for copy in (wq_saved, tok_saved, kv_saved, wo_saved):
        copy.wait()
    net.finish()


def forward(bounds, tok, wq, wo, we, gy, used):
    outs = {
        "wo": ((4, 4, 2, 48, D), BF, ANY),
        "wq": ((4, 4, 2, 48, WQ), BF, ANY),
        "kv": ((4, 4, 2, 2, HALF, 2 * HD), BF, ANY),
        "q": ((3, HALF, QW), BF, VM),
        "o": ((4, ROWS, QW), BF, VM),
        "lse": ((2, QPG, 1, HALF), F32, VM),
        "tok": ((4, ROWS, D), BF, ANY),
        "hidden": ((ROWS, D), F32, VM),
        "hidden_grad": ((ROWS, D), F32, VM),
        "hidden_low": ((ROWS, D), BF, VM),
        "gains": ((16, D), F32, VM),
        "small": ((D, SMALL), BF, VM),
        "do": ((4, ROWS, QW), BF, VM),
        "out_parts": ((4, 2, ROWS, D), BF, ANY),
        "dwe": ((4, 4, 96, WE), BF, ANY),
    }
    values = pl.pallas_call(
        forward_kernel,
        name="forward",
        out_shape=tuple(jax.ShapeDtypeStruct(s, t) for s, t, _ in outs.values()),
        in_specs=[SM, VM, ANY, ANY, ANY, ANY, VM],
        out_specs=tuple(m for _, _, m in outs.values()),
        scratch_shapes=[
            pltpu.VMEM((4, 16, WQ), BF),
            pltpu.VMEM((48, WQ), BF),
            pltpu.VMEM((4, 4, 2, 48, WQ), BF),
            pltpu.VMEM((4, 16, D), BF),
            pltpu.VMEM((48, D), BF),
            pltpu.VMEM((4, 4, 2, 48, D), BF),
            pltpu.VMEM((8, 16, WE), BF),
            pltpu.VMEM((96, WE), BF),
            pltpu.VMEM((4, 4, 96, WE), BF),
            pltpu.VMEM((4, ROWS, D), BF),
            pltpu.VMEM((4, 4, 2, 2, HALF, 2 * HD), BF),
            pltpu.VMEM((HALF, QW), BF),
            pltpu.VMEM((2, QPG, HD, HALF), BF),
            pltpu.VMEM((2, QPG, 1, HALF), F32),
            pltpu.VMEM((2, QPG, 1, HALF), F32),
            pltpu.VMEM((2, QPG, HD, HALF), F32),
            pltpu.VMEM((ROWS, D), BF),
            pltpu.VMEM((ROWS, RW), BF),
            pltpu.VMEM((4, 2, ROWS, RW), BF),
            pltpu.VMEM((4, 2, ROWS, D), BF),
            pltpu.VMEM((4, 2 * ROWS, UP), BF),
            pltpu.VMEM((4, 2 * ROWS, 2 * UP), BF),
            pltpu.VMEM((2, 2, ROWS, RW), BF),
            pltpu.VMEM((2, 2, ROWS, D), BF),
            pltpu.VMEM((4, ROWS, RW), BF),
            pltpu.VMEM((4, ROWS, RW), BF),
            pltpu.VMEM((4, ROWS, RW), BF),
            pltpu.VMEM((2, 4, 96, WE), BF),
            pltpu.VMEM((4, ROWS, QW), BF),
            pltpu.VMEM((4, ROWS, QW), BF),
        ]
        + sems(144, 32)
        + [pltpu.SemaphoreType.DMA((4,))] * 6,
        compiler_params=pltpu.CompilerParams(
            collective_id=1, has_side_effects=True, vmem_limit_bytes=VMEM_LIMIT
        ),
    )(bounds, tok, wq, wo, we, gy, used)
    return dict(zip(outs, values))


def add_into(dst, left, right, rows):
    step = 32

    def body(i, carried):
        place = pl.ds(mult(i * step, step), step)
        dst[place, :] = (left[place, :].astype(F32) + right[place, :].astype(F32)).astype(
            dst.dtype
        )
        return carried

    lax.fori_loop(0, rows // step, body, 0)


def add_four(dst, parts, rows, step):
    def body(i, carried):
        place = pl.ds(mult(i * step, step), step)
        total = parts[0][place, :].astype(F32)
        for part in parts[1:]:
            total = total + part[place, :].astype(F32)
        dst[place, :] = total.astype(dst.dtype)
        return carried

    lax.fori_loop(0, rows // step, body, 0)


def sum_group(net, parts, pos, core_land, own, both, z_land, out):
    y, x, c, z = pos
    order = (0, 1, 3, 2)
    crossing, kept = [], []
    for d in order:
        zz = lax.rem(z + d, 4)
        crossing.append(net.put(parts.at[zz, 1 - c], core_land.at[zz], sibling(pos)))
        kept.append(net.keep(parts.at[zz, c], own.at[zz]))
    yield
    arriving = []
    for n, d in enumerate(order):
        zz = lax.rem(z + d, 4)
        crossing[n].wait_recv()
        kept[n].wait()
        add_into(both.at[zz], own.at[zz], core_land.at[zz], ROWS)
        if d:
            arriving.append(net.put(both.at[zz], z_land.at[d - 1], device(y, x, c, zz)))
    yield
    for copy in arriving:
        copy.wait_recv()
    add_four(out, [both.at[z]] + [z_land.at[d] for d in range(3)], ROWS, 32)


def group_scratch(width):
    return [
        pltpu.VMEM((4, ROWS, width), BF),
        pltpu.VMEM((4, ROWS, width), BF),
        pltpu.VMEM((4, ROWS, width), BF),
        pltpu.VMEM((3, ROWS, width), BF),
    ]


def fold_parts(own, land, total, rows):
    step = 16

    def body(i, carried):
        q = i // (rows // step)
        place = pl.ds(mult(lax.rem(i, rows // step) * step, step), step)
        value = own[q, place, :].astype(F32)
        for d in range(3):
            value = value + land[d, q, place, :].astype(F32)
        total[q, place, :] = value.astype(BF)
        return carried

    lax.fori_loop(0, 4 * (rows // step), body, 0)


def scatter_first(net, src, pos, cut, a_own, a_land, b_own, b_land, a_sum, b_sum):
    y, x, c, z = pos
    rows, width = src.shape[2], src.shape[3]
    first, second = pl.ds(0, cut), pl.ds(cut, width - cut)
    whole = slice(None)
    keep_a = net.keep(src.at[whole, x, whole, first], a_own)
    keep_b = net.keep(src.at[y, whole, whole, second], b_own)
    to_x, to_y = [], []
    for d in (1, 3, 2):
        xx, yy = lax.rem(x + d, 4), lax.rem(y + d, 4)
        to_x.append(
            net.put(src.at[whole, xx, whole, first], a_land.at[d - 1], device(y, xx, c, z))
        )
        to_y.append(
            net.put(src.at[yy, whole, whole, second], b_land.at[d - 1], device(yy, x, c, z))
        )
    yield
    keep_a.wait()
    for copy in to_x:
        copy.wait_recv()
    fold_parts(a_own, a_land, a_sum, rows)
    keep_b.wait()
    for copy in to_y:
        copy.wait_recv()
    fold_parts(b_own, b_land, b_sum, rows)


def scatter_second(net, pos, cut, a_sum, a_last, b_sum, b_last, out):
    y, x, c, z = pos
    rows, width = out.shape
    last_y, last_x = [], []
    for d in (1, 3, 2):
        yy, xx = lax.rem(y + d, 4), lax.rem(x + d, 4)
        last_y.append(net.put(a_sum.at[yy], a_last.at[d - 1], device(yy, x, c, z)))
        last_x.append(net.put(b_sum.at[xx], b_last.at[d - 1], device(y, xx, c, z)))
    yield
    for copy in last_y:
        copy.wait_recv()
    for copy in last_x:
        copy.wait_recv()
    step = 16
    first, second = slice(0, cut), slice(cut, width)

    def final(i, carried):
        place = pl.ds(mult(i * step, step), step)
        for at, own, last, columns in ((y, a_sum, a_last, first), (x, b_sum, b_last, second)):
            value = own[at, place, :].astype(F32)
            for d in range(3):
                value = value + last[d, place, :].astype(F32)
            out[place, columns] = value.astype(BF)
        return carried

    lax.fori_loop(0, rows // step, final, 0)


def first_scratch(rows, width, cut):
    shapes = []
    for w in (cut, width - cut):
        shapes += [pltpu.VMEM((4, rows, w), BF), pltpu.VMEM((3, 4, rows, w), BF)]
    return shapes


def second_scratch(rows, width, cut):
    return [pltpu.VMEM((3, rows, cut), BF), pltpu.VMEM((3, rows, width - cut), BF)]


def backward_kernel(
    bounds, q, o, do, lse, kv_in, dwe, hg, out_parts,
    dkv_out, dq_out, o_out, we_a, we_b, hg_all, out_sum,
    kv, o_in, dq_own, dq_in, qt, dot_t, delta, late_lse, dqt, part, core_land, both, a_land, b_land,
    a_sum, b_sum, a_last, b_last, *scratch,
):
    we_s = scratch[:4]
    group_s = scratch[4:8]
    ss, rs, ls = scratch[8:]
    pos = position()
    y, x, c, z = pos
    b = (y * 4 + x) * 2 + c
    net = Net(ss, rs, ls)
    kv_kept = net.keep(kv_in, kv)
    greet(z_peers(pos) + xy_peers(pos) + [device(*mirror(pos))] + other_column(pos))
    o_swap = net.put(o.at[pl.ds(2, 2)], o_in, device(*mirror(pos)))
    whole = slice(None)

    def experts():
        yield from scatter_first(net, dwe, pos, 1024, *we_s, we_a, we_b)

    def rows_of_group():
        mine = hg_all.at[z]
        kept = net.keep(hg, mine)
        copies = [net.put(hg, mine, device(y, x, c, z + d)) for d in (1, 3, 2)]
        yield
        kept.wait()
        for copy in copies:
            copy.wait_recv()

    def pump(job):
        try:
            next(job)
        except StopIteration:
            pass

    we_job = experts()
    out_job = sum_group(net, out_parts, pos, *group_s, out_sum)
    hg_job = rows_of_group()
    pump(out_job)
    pump(we_job)
    pump(hg_job)

    lo, hi = 2 * b, 2 * (NBLK - b) - 1
    late = 2 * NBLK - 2
    starts = []
    for i, chunk in enumerate((lo, hi)):
        at = chunk * HALF + lax.broadcasted_iota(jnp.int32, (1, HALF), 1)
        first = jnp.where(at >= bounds[1], bounds[1], jnp.where(at >= bounds[0], bounds[0], 0))
        starts.append((at, first))
        third = at >= bounds[1]
        for h in range(QPG):
            columns = slice(h * HD, (h + 1) * HD)
            qt[i, h] = transposed(q[2 * i, :, columns])
            do_t = jnp.transpose(
                do[2 * i : 2 * i + 2, :, columns].reshape(HALF, HD).astype(F32), (1, 0)
            )
            o_t = jnp.transpose(
                o[2 * i : 2 * i + 2, :, columns].reshape(HALF, HD).astype(F32), (1, 0)
            )
            dot_t[i, h] = do_t.astype(BF)
            delta[i, h] = jnp.sum(do_t * o_t, axis=0, keepdims=True)
            late_lse[i, h] = jnp.where(third, -LOW, lse[i, h])
    dqt[...] = jnp.zeros_like(dqt)
    kv_kept.wait()
    pump(out_job)

    def pairs(ids, yy, xx, cc, half, slot, masked):
        k_rows = kv[yy, xx, cc, half, :, :HD]
        v_rows = kv[yy, xx, cc, half, :, HD:]
        work = [(i, h) for i in ids for h in range(QPG)]
        scores = [jnp.dot(k_rows, qt[i, h], preferred_element_type=F32) for i, h in work]
        dp = [jnp.dot(v_rows, dot_t[i, h], preferred_element_type=F32) for i, h in work]
        if masked:
            chunk = ((yy * 4 + xx) * 2 + cc) * 2 + half
            key_at = chunk * HALF + lax.broadcasted_iota(jnp.int32, (HALF, HALF), 0)
            allowed = {i: (key_at >= starts[i][1]) & (key_at <= starts[i][0]) for i in ids}
            p = [
                jnp.where(allowed[i], jnp.exp2(s * EXP_SCALE - lse[i, h]), 0.0)
                for (i, h), s in zip(work, scores)
            ]
        else:
            p = [
                jnp.exp2(s * EXP_SCALE - late_lse[i, h]) for (i, h), s in zip(work, scores)
            ]
        ds = [(w * (g - delta[i, h])).astype(BF) for (i, h), w, g in zip(work, p, dp)]
        dk = jnp.zeros((HALF, HD), F32)
        dv = jnp.zeros((HALF, HD), F32)
        dq = []
        for n, (i, h) in enumerate(work):
            columns = slice(h * HD, (h + 1) * HD)
            do_rows = do[2 * i : 2 * i + 2, :, columns].reshape(HALF, HD)
            dv = dv + jnp.dot(p[n].astype(BF), do_rows, preferred_element_type=F32)
            dk = dk + jnp.dot(ds[n], q[2 * i, :, columns], preferred_element_type=F32)
            dq.append(lax.dot_general(k_rows, ds[n], COL_COL, preferred_element_type=F32))
        for n, (i, h) in enumerate(work):
            dqt[i, h] += dq[n]
        part[slot, cc, half, :, :HD] = (dk * SCALE).astype(BF)
        part[slot, cc, half, :, HD:] = dv.astype(BF)

    def chunk_step(yy, xx, cc, half, slot):
        chunk = ((yy * 4 + xx) * 2 + cc) * 2 + half
        in_lo, in_hi = chunk <= lo, chunk <= hi
        special = (chunk <= 1) | (chunk == lo) | (chunk == hi) | (chunk >= late)
        masked = special & (in_lo | in_hi)
        plain = jnp.logical_not(special)

        @pl.when(plain & in_lo & in_hi)
        def _():
            pairs((0, 1), yy, xx, cc, half, slot, False)

        @pl.when(plain & in_lo & jnp.logical_not(in_hi))
        def _():
            pairs((0,), yy, xx, cc, half, slot, False)

        @pl.when(plain & in_hi & jnp.logical_not(in_lo))
        def _():
            pairs((1,), yy, xx, cc, half, slot, False)

        @pl.when(masked)
        def _():
            pairs((0, 1), yy, xx, cc, half, slot, True)

        @pl.when(jnp.logical_not(in_lo | in_hi))
        def _():
            part[slot, cc, half] = jnp.zeros((HALF, 2 * HD), BF)

    def chip(t):
        dy = jnp.where(
            t < 4,
            t,
            jnp.where(
                t < 7,
                1,
                jnp.where(
                    t < 10,
                    jnp.where(t == 7, 0, t - 6),
                    jnp.where(
                        t < 12, 3, jnp.where(t < 14, 2 * (t - 12), 2 * (15 - t))
                    ),
                ),
            ),
        )
        dx = jnp.where(
            t < 4,
            1,
            jnp.where(
                t < 7,
                jnp.where(t == 4, 0, t - 3),
                jnp.where(
                    t < 10,
                    3,
                    jnp.where(t < 12, 2 * (t - 10), jnp.where(t < 14, 2, 0)),
                ),
            ),
        )
        return lax.rem(y + dy, 4), lax.rem(x + dx, 4)

    to_core, to_x, to_y = net.reserve(16), net.reserve(4), net.reserve(4)

    def fold_chip(t):
        yy, xx = chip(t)
        slot = lax.rem(t, 2)
        net.arrived(to_core + t, core_land.at[yy, xx])
        both[yy, xx] = (part[slot, c].astype(F32) + core_land[yy, xx].astype(F32)).astype(BF)
        net.left(to_core + t, part.at[slot, 1 - c])

    def send_lines(d):
        xx, yy = lax.rem(x + d, 4), lax.rem(y + d, 4)
        net.put_at(to_x + d, both.at[whole, xx, 0], a_land.at[d], device(y, xx, c, z))
        net.put_at(to_y + d, both.at[yy, whole, 1], b_land.at[d], device(yy, x, c, z))

    def chip_step(t, carried):
        yy, xx = chip(t)
        slot = lax.rem(t, 2)

        def step(n, carried):
            chunk_step(yy, xx, n // 2, lax.rem(n, 2), slot)
            return carried

        lax.fori_loop(0, 4, step, 0)
        net.put_at(to_core + t, part.at[slot, 1 - c], core_land.at[yy, xx], sibling(pos))

        @pl.when(t > 0)
        def _():
            fold_chip(t - 1)

        for at, d in ((7, 1), (12, 3), (15, 2)):

            @pl.when(t == at)
            def _():
                send_lines(d)

        return carried

    lax.fori_loop(0, 16, chip_step, 0)
    for i in range(2):
        for h in range(QPG):
            dq_own[i, :, h * HD : (h + 1) * HD] = jnp.transpose(dqt[i, h] * SCALE, (1, 0)).astype(
                BF
            )
    dq_swap = net.put(dq_own.at[1], dq_in, device(*mirror(pos)))
    lax.fori_loop(15, 16, lambda t, _: fold_chip(t), None)

    def fold_lines(own_at, land, total):
        def body(n, carried):
            q_at, place = n // 8, pl.ds(mult(lax.rem(n, 8) * 32, 32), 32)
            value = own_at(q_at, place).astype(F32)
            for d in (1, 2, 3):
                value = value + land[d, q_at, place, :].astype(F32)
            total[q_at, place, :] = value.astype(BF)
            return carried

        lax.fori_loop(0, 32, body, 0)

    for d in (1, 3, 2):
        net.arrived(to_x + d, a_land.at[d])
    fold_lines(lambda n, place: both[n, x, 0, place, :], a_land, a_sum)
    last_y = []
    for d in (1, 3, 2):
        yy = lax.rem(y + d, 4)
        last_y.append(net.put(a_sum.at[yy], a_last.at[d], device(yy, x, c, z)))
    for d in (1, 3, 2):
        net.arrived(to_y + d, b_land.at[d])
    fold_lines(lambda n, place: both[y, n, 1, place, :], b_land, b_sum)
    last_x = []
    for d in (1, 3, 2):
        xx = lax.rem(x + d, 4)
        last_x.append(net.put(b_sum.at[xx], b_last.at[d], device(y, xx, c, z)))
    pump(we_job)
    pump(out_job)
    o_swap.wait_recv()
    o_out[0] = o[0]
    o_out[1] = o[1]
    o_out[2] = o_in[0]
    o_out[3] = o_in[1]
    dq_swap.wait_recv()
    dq_out[0] = dq_own[0]
    dq_out[1] = dq_in[...]
    for copies, total, last, at, half in (
        (last_y, a_sum, a_last, y, 0),
        (last_x, b_sum, b_last, x, 1),
    ):
        for copy in copies:
            copy.wait_recv()
        value = total[at].astype(F32)
        for d in (1, 2, 3):
            value = value + last[d].astype(F32)
        dkv_out[half] = value.astype(BF)
    for job in (hg_job, out_job, we_job):
        for _ in job:
            pass
    for d in (1, 2, 3):
        net.left(to_x + d, a_land.at[d])
        net.left(to_y + d, b_land.at[d])
    net.finish()


def backward(bounds, q, o, do, lse, kv, dwe, hg, out_parts):
    return pl.pallas_call(
        backward_kernel,
        name="backward",
        out_shape=(
            jax.ShapeDtypeStruct((2, HALF, 2 * HD), BF),
            jax.ShapeDtypeStruct((2, HALF, QW), BF),
            jax.ShapeDtypeStruct((4, ROWS, QW), BF),
            jax.ShapeDtypeStruct((4, 96, 1024), BF),
            jax.ShapeDtypeStruct((4, 96, WE - 1024), BF),
            jax.ShapeDtypeStruct((4, ROWS, D), BF),
            jax.ShapeDtypeStruct((ROWS, D), F32),
        ),
        in_specs=[SM] + [VM] * 4 + [ANY] * 4,
        out_specs=(VM, VM, VM, VM, VM, ANY, VM),
        scratch_shapes=[
            pltpu.VMEM((4, 4, 2, 2, HALF, 2 * HD), BF),
            pltpu.VMEM((2, ROWS, QW), BF),
            pltpu.VMEM((2, HALF, QW), BF),
            pltpu.VMEM((HALF, QW), BF),
            pltpu.VMEM((2, QPG, HD, HALF), BF),
            pltpu.VMEM((2, QPG, HD, HALF), BF),
            pltpu.VMEM((2, QPG, 1, HALF), F32),
            pltpu.VMEM((2, QPG, 1, HALF), F32),
            pltpu.VMEM((2, QPG, HD, HALF), F32),
            pltpu.VMEM((2, 2, 2, HALF, 2 * HD), BF),
            pltpu.VMEM((4, 4, 2, HALF, 2 * HD), BF),
            pltpu.VMEM((4, 4, 2, HALF, 2 * HD), BF),
            pltpu.VMEM((4, 4, HALF, 2 * HD), BF),
            pltpu.VMEM((4, 4, HALF, 2 * HD), BF),
            pltpu.VMEM((4, HALF, 2 * HD), BF),
            pltpu.VMEM((4, HALF, 2 * HD), BF),
            pltpu.VMEM((4, HALF, 2 * HD), BF),
            pltpu.VMEM((4, HALF, 2 * HD), BF),
        ]
        + first_scratch(96, WE, 1024)
        + group_scratch(D)
        + sems(72, 16),
        compiler_params=pltpu.CompilerParams(
            collective_id=7, has_side_effects=True, vmem_limit_bytes=VMEM_LIMIT
        ),
    )(bounds, q, o, do, lse, kv, dwe, hg, out_parts)


def close_kernel(
    dq, dkv, o, hg, tok, wq, gains, small, hidden_grad, we_a, we_b,
    tokens_grad, dwq_out, dwe_out,
    joined, row_sum, n_part, n_land, dwq, w_land, w_both, *scratch,
):
    w_first, w_second, we_last = scratch[:4], scratch[4:6], scratch[6:8]
    w_a, w_b, w_rows, w_pieces, we_rows, we_pieces = scratch[8:14]
    ss, rs, ls = scratch[14:]
    pos = position()
    y, x, c, z = pos
    greet(z_peers(pos) + xy_peers(pos) + other_column(pos))
    net = Net(ss, rs, ls)
    experts_job = scatter_second(net, pos, 1024, we_a, we_last[0], we_b, we_last[1], we_rows)
    next(experts_job)
    joined[:, :, :QW] = dq[...].reshape(4, ROWS, QW)
    joined[:, :, QW:] = dkv[...].reshape(4, ROWS, 2 * HD)
    gain_attn = gains[EXPERTS + 1 : EXPERTS + 2, :]
    row_sum[...] = jnp.zeros_like(row_sum)
    to_z, to_core = net.reserve(4), net.reserve(4)

    def normed_block(n, carried):
        d = turn(n)
        zz = lax.rem(z + d, 4)
        weights = wq[...].reshape(D, WQ)[:, :GROUP_W]
        grad = lax.dot_general(joined[zz], weights, ROW_ROW, preferred_element_type=F32)
        rows = tok[zz].astype(F32)
        unit = rows * lax.rsqrt(jnp.mean(rows * rows, axis=-1, keepdims=True) + epsilon)
        row_sum[...] += jnp.sum(grad * unit, axis=0, keepdims=True)
        n_part[zz] = grad.astype(BF)

        @pl.when(n > 0)
        def _():
            net.put_at(to_z + d, n_part.at[zz], n_land.at[d], device(y, x, c, zz))

        return carried

    lax.fori_loop(0, 4, normed_block, 0)
    high = row_sum[...].astype(BF)
    low = (row_sum[...] - high.astype(F32)).astype(BF)
    at = lax.broadcasted_iota(jnp.int32, (16, D), 0)
    two_rows = jnp.where(
        at == 0, high.astype(F32), jnp.where(at == 1, low.astype(F32), 0.0)
    ).astype(BF)
    pick = (
        (lax.broadcasted_iota(jnp.int32, (16, SMALL), 0) < 2)
        & (lax.broadcasted_iota(jnp.int32, (16, SMALL), 1) == EXPERTS + 1)
    )
    pick = jnp.where(pick, 1.0, 0.0).astype(BF)
    column = lax.dot_general(two_rows, pick, COL_COL, preferred_element_type=F32)
    dwq[:, :, :, :, GROUP_W + QW :] = (
        (small[...].astype(F32) + column).astype(BF).reshape(4, 4, 2, 48, SMALL)
    )

    def weight_grads(t, carried):
        columns = pl.ds(mult(t * QW, QW), QW)
        gain = gains[EXPERTS + 1 : EXPERTS + 2, columns]
        qkv_grad = jnp.zeros((QW, GROUP_W), F32)
        wo_grad = jnp.zeros((QW, QW), F32)
        for k in range(4):
            rows = tok[k].astype(F32)
            scale = lax.rsqrt(jnp.mean(rows * rows, axis=-1, keepdims=True) + epsilon)
            normed = (tok[k, :, columns].astype(F32) * scale * gain).astype(BF)
            qkv_grad = qkv_grad + lax.dot_general(
                normed, joined[k], COL_COL, preferred_element_type=F32
            )
            wo_grad = wo_grad + lax.dot_general(
                hg[k, :, columns], o[k], COL_COL, preferred_element_type=F32
            )
        dwq[t, :, :, :, :GROUP_W] = qkv_grad.astype(BF).reshape(4, 2, 48, GROUP_W)
        dwq[t, :, :, :, GROUP_W : GROUP_W + QW] = wo_grad.astype(BF).reshape(4, 2, 48, QW)
        net.put_at(to_core + t, dwq.at[t, :, 1 - c], w_land.at[t], sibling(pos))
        return carried

    lax.fori_loop(0, 4, weight_grads, 0)

    def fold(t, carried):
        net.arrived(to_core + t, w_land.at[t])

        def body(i, inner):
            xx, place = i // 3, pl.ds(mult(lax.rem(i, 3) * 16, 16), 16)
            w_both[t, xx, place, :] = (
                dwq[t, xx, c, place, :].astype(F32) + w_land[t, xx, place, :].astype(F32)
            ).astype(BF)
            return inner

        lax.fori_loop(0, 12, body, 0)
        net.left(to_core + t, w_land.at[t])
        return carried

    lax.fori_loop(0, 4, fold, 0)
    weights_job = scatter_first(net, w_both, pos, GROUP_W, *w_first, w_a, w_b)
    next(weights_job)
    for _ in experts_job:
        pass
    we_pieces[...] = spread_rows(we_rows[...], 8)
    me = c * 4 + z
    expert_pieces = []
    for dc in (0, 1):
        for d in (0, 1, 3, 2):
            if (dc, d) == (0, 0):
                continue
            cc, zz = lax.rem(c + dc, 2), lax.rem(z + d, 4)
            expert_pieces.append(
                net.put(we_pieces.at[cc * 4 + zz], dwe_out.at[me], device(y, x, cc, zz))
            )
    expert_kept = net.keep(we_pieces.at[me], dwe_out.at[me])
    for d in (1, 2, 3):
        net.arrived(to_z + d, n_land.at[d])
    normed_grad = n_part[z].astype(F32)
    for d in (1, 2, 3):
        normed_grad = normed_grad + n_land[d].astype(F32)
    rows = tok[z].astype(F32)
    scale = lax.rsqrt(jnp.mean(rows * rows, axis=-1, keepdims=True) + epsilon)
    unit = rows * scale
    dn = normed_grad * gain_attn
    tokens_grad[...] = hidden_grad[...] + scale * (
        dn - unit * jnp.mean(dn * unit, axis=-1, keepdims=True)
    )
    for _ in weights_job:
        pass
    for _ in scatter_second(net, pos, GROUP_W, w_a, w_second[0], w_b, w_second[1], w_rows):
        pass
    w_pieces[...] = spread_rows(w_rows[...], 4)
    kept = net.keep(w_pieces.at[z], dwq_out.at[z])
    pieces = [
        net.put(w_pieces.at[lax.rem(z + d, 4)], dwq_out.at[z], device(y, x, c, z + d))
        for d in (1, 3, 2)
    ]
    expert_kept.wait()
    for copy in expert_pieces:
        copy.wait_recv()
    kept.wait()
    for copy in pieces:
        copy.wait_recv()
    for d in (1, 2, 3):
        net.left(to_z + d, n_land.at[d])
    net.finish()


def closing(dq, dkv, o, hg, tok, wq, gains, small, hidden_grad, we_a, we_b):
    return pl.pallas_call(
        close_kernel,
        name="closing",
        out_shape=(
            jax.ShapeDtypeStruct((ROWS, D), F32),
            jax.ShapeDtypeStruct((4, 16, GQ), BF),
            jax.ShapeDtypeStruct((8, 16, WE), BF),
        ),
        in_specs=[VM] * 11,
        out_specs=(VM, ANY, ANY),
        scratch_shapes=[
            pltpu.VMEM((4, ROWS, GROUP_W), BF),
            pltpu.VMEM((1, D), F32),
            pltpu.VMEM((4, ROWS, D), BF),
            pltpu.VMEM((4, ROWS, D), BF),
            pltpu.VMEM((4, 4, 2, 48, GQ), BF),
            pltpu.VMEM((4, 4, 48, GQ), BF),
            pltpu.VMEM((4, 4, 48, GQ), BF),
        ]
        + first_scratch(48, GQ, GROUP_W)
        + second_scratch(48, GQ, GROUP_W)
        + second_scratch(96, WE, 1024)
        + [
            pltpu.VMEM((4, 48, GROUP_W), BF),
            pltpu.VMEM((4, 48, GQ - GROUP_W), BF),
            pltpu.VMEM((48, GQ), BF),
            pltpu.VMEM((4, 16, GQ), BF),
            pltpu.VMEM((96, WE), BF),
            pltpu.VMEM((8, 16, WE), BF),
        ]
        + sems(48, 8),
        compiler_params=pltpu.CompilerParams(
            collective_id=8, has_side_effects=True, vmem_limit_bytes=VMEM_LIMIT
        ),
    )(dq, dkv, o, hg, tok, wq, gains, small, hidden_grad, we_a, we_b)


def dot(left, right):
    return jnp.dot(left, right, preferred_element_type=F32)


def dot_rows(left, right):
    return lax.dot_general(left, right, (((0,), (0,)), ((), ())), preferred_element_type=F32)


def dot_cols(left, right):
    return lax.dot_general(left, right, (((1,), (1,)), ((), ())), preferred_element_type=F32)


def inverse_rms(values):
    return lax.rsqrt(jnp.mean(values * values, axis=-1, keepdims=True) + epsilon)


def route_table(logits, expert_ids):
    used = jnp.any(
        expert_ids[:, :, None] == jnp.arange(EXPERTS, dtype=jnp.int32)[None, None, :], axis=1
    )
    top = jnp.max(jnp.where(used, logits, LOW), axis=-1, keepdims=True)
    raised = jnp.where(used, jnp.exp(logits - top), 0.0)
    return raised / jnp.sum(raised, axis=-1, keepdims=True)


def pad_rows(value):
    return jnp.pad(value, ((0, 0), (0, 4), (0, 0)))


def per_device(
    tokens,
    seq_bounds,
    expert_ids,
    attn_gain,
    qkv_weight,
    out_weight,
    mlp_gain,
    router_weight,
    expert_gate_up,
    expert_down,
    shared_gate_up,
    shared_down,
    out_cotangent,
):
    small = jnp.concatenate(
        [
            router_weight,
            mlp_gain[:, None],
            attn_gain[:, None],
            jnp.zeros((12, SMALL - EXPERTS - 2), F32),
        ],
        axis=1,
    ).astype(BF)
    wq_pieces = pad_rows(
        jnp.concatenate(
            [
                jnp.transpose(qkv_weight.astype(BF).reshape(12, HK, GROUP_W), (1, 0, 2)),
                jnp.broadcast_to(small[None], (4, 12, SMALL)),
            ],
            axis=-1,
        )
    )
    wo_piece = jnp.pad(jnp.transpose(out_weight.astype(BF), (1, 0)), ((0, 4), (0, 0)))
    shared_cut = jnp.transpose(shared_gate_up.astype(BF).reshape(12, 2, 8, FSL), (1, 2, 0, 3))
    down_cut = jnp.transpose(shared_down.astype(BF).reshape(8, FSL, 12), (0, 2, 1))
    gate_up_low = expert_gate_up.astype(BF)
    we_pieces = pad_rows(
        jnp.concatenate(
            [
                gate_up_low[:, :, :FE],
                shared_cut[0],
                gate_up_low[:, :, FE:],
                shared_cut[1],
                jnp.transpose(expert_down.astype(BF), (0, 2, 1)),
                down_cut,
            ],
            axis=-1,
        )
    )
    used = jnp.any(
        expert_ids[:, :, None] == jnp.arange(SMALL, dtype=jnp.int32)[None, None, :], axis=1
    ).astype(F32)
    fwd = forward(seq_bounds, tokens, wq_pieces, wo_piece, we_pieces, out_cotangent, used)
    dkv_own, dq_all, attn_all, we_a, we_b, hidden_group, out_sum = backward(
        seq_bounds,
        *(fwd[k] for k in ("q", "o", "do", "lse", "kv", "dwe", "hidden_low", "out_parts")),
    )
    output = (fwd["hidden"] + out_sum).astype(BF)
    tokens_grad, dwq_pieces, dwe_pieces = closing(
        dq_all,
        dkv_own,
        attn_all,
        hidden_group,
        *(fwd[k] for k in ("tok", "wq", "gains", "small", "hidden_grad")),
        we_a,
        we_b,
    )
    dwq_own = dwq_pieces[:, :12].astype(F32)
    qkv_out = jnp.transpose(dwq_own[:, :, :GROUP_W], (1, 0, 2)).reshape(12, QKV)
    wo_out = jnp.transpose(dwq_own[:, :, GROUP_W : GROUP_W + QW], (0, 2, 1)).reshape(D, 12)
    small_out = jnp.sum(dwq_own[:, :, GROUP_W + QW :], axis=0)
    dwe_own = dwe_pieces[:, :12].astype(F32)
    gate_up_out = jnp.concatenate([dwe_own[:, :, :FE], dwe_own[:, :, UP : UP + FE]], axis=-1)
    down_out = jnp.transpose(dwe_own[:, :, 2 * UP : 2 * UP + FE], (0, 2, 1))
    shared_out = jnp.transpose(
        jnp.stack([dwe_own[:, :, FE:UP], dwe_own[:, :, UP + FE : 2 * UP]]), (2, 0, 1, 3)
    ).reshape(12, 2 * FS)
    shared_down_out = jnp.transpose(dwe_own[:, :, 2 * UP + FE :], (0, 2, 1)).reshape(FS, 12)
    return (
        output,
        tokens_grad,
        small_out[:, EXPERTS + 1],
        qkv_out,
        wo_out,
        small_out[:, EXPERTS],
        small_out[:, :EXPERTS],
        gate_up_out,
        down_out,
        shared_out,
        shared_down_out,
    )


def solution(mesh):
    both = ("blk", "head")
    in_specs = (
        P(both, None),
        P(),
        P(both, None),
        P(both),
        P(both, None),
        P(None, both),
        P(both),
        P(both, None),
        P(None, both, None),
        P(None, None, both),
        P(both, None),
        P(None, both),
        P(both, None),
    )
    out_specs = (
        P(both, None),
        P(both, None),
        P(both),
        P(both, None),
        P(None, both),
        P(both),
        P(both, None),
        P(None, both, None),
        P(None, None, both),
        P(both, None),
        P(None, both),
    )
    return jax.shard_map(
        per_device, mesh=mesh, in_specs=in_specs, out_specs=out_specs, check_vma=False
    )
```

```python
import functools

import jax
import jax.numpy as jnp
from jax import lax
from jax.experimental import pallas as pl
from jax.experimental.pallas import tpu as pltpu
from jax.sharding import PartitionSpec as P

D = 1536
HQ = 12
HK = 4
HD = 128
FE = 512
FS = 1024
EXPERTS = 8
QPG = 3
GROUP_W = 640
QKV = 2560
ROWS = 128
BLK = 512
HALF = 256
QW = 384
SMALL = 128
WQ = GROUP_W + SMALL
GQ = GROUP_W + QW + SMALL
PAIR = QPG * HALF
LANES = {(0, 1): slice(0, 2 * PAIR), (0,): slice(0, PAIR), (1,): slice(PAIR, 2 * PAIR)}
FSL = FS // 8
UP = FE + FSL
WE = 3 * UP
NBLK = 32
MESH = pl.DeviceIdType.MESH
BF = jnp.bfloat16
F32 = jnp.float32
epsilon = 1e-05
LOW = -1e30
LOG2E = 1.4426950408889634
SCALE = HD**-0.5
VMEM_LIMIT = 60 * 1024 * 1024

ANY = pl.BlockSpec(memory_space=pl.ANY)
VM = pl.BlockSpec(memory_space=pltpu.VMEM)


def position():
    b = lax.axis_index("blk")
    z = lax.axis_index("head")
    return b // 8, lax.rem(b // 2, 4), lax.rem(b, 2), z


def device(y, x, c, z):
    return ((lax.rem(y, 4) * 4 + lax.rem(x, 4)) * 2 + lax.rem(c, 2), lax.rem(z, 4))


def mirror(pos):
    y, x, c, z = pos
    return 3 - y, 3 - x, 1 - c, z


def greet(targets):
    barrier = pltpu.get_barrier_semaphore()
    for target in targets:
        pl.semaphore_signal(barrier, inc=1, device_id=target, device_id_type=MESH)
    pl.semaphore_wait(barrier, len(targets))


def z_peers(pos):
    y, x, c, z = pos
    return [device(y, x, c, z + d) for d in (1, 2, 3)]


def xy_peers(pos):
    y, x, c, z = pos
    return [device(y, x + d, c, z) for d in (1, 2, 3)] + [
        device(y + d, x, c, z) for d in (1, 2, 3)
    ]


def sibling(pos):
    y, x, c, z = pos
    return device(y, x, c + 1, z)


def other_column(pos):
    y, x, c, z = pos
    return [device(y, x, c + 1, z + d) for d in (0, 1, 2, 3)]


class Net:
    def __init__(self, send_sems, recv_sems, local_sems):
        self.send_sems, self.recv_sems, self.local_sems = send_sems, recv_sems, local_sems
        self.count = 0
        self.locals = 0
        self.started = []

    def put(self, src, dst, target):
        k = self.count
        self.count += 1
        copy = pltpu.make_async_remote_copy(
            src_ref=src,
            dst_ref=dst,
            send_sem=self.send_sems.at[k],
            recv_sem=self.recv_sems.at[k],
            device_id=target,
            device_id_type=MESH,
        )
        copy.start()
        self.started.append(copy)
        return copy

    def reserve(self, count):
        k = self.count
        self.count += count
        return k

    def put_at(self, k, src, dst, target):
        copy = self.copy_at(k, src, dst, target)
        copy.start()

    def copy_at(self, k, src, dst, target):
        return pltpu.make_async_remote_copy(
            src_ref=src,
            dst_ref=dst,
            send_sem=self.send_sems.at[k],
            recv_sem=self.recv_sems.at[k],
            device_id=target,
            device_id_type=MESH,
        )

    def arrived(self, k, ref):
        pltpu.make_async_copy(ref, ref, self.recv_sems.at[k]).wait()

    def left(self, k, ref):
        pltpu.make_async_copy(ref, ref, self.send_sems.at[k]).wait()

    def keep(self, src, dst):
        k = self.locals
        self.locals += 1
        copy = pltpu.make_async_copy(src, dst, self.local_sems.at[k])
        copy.start()
        return copy

    def finish(self):
        for copy in self.started:
            copy.wait_send()


def sems(remote, local):
    return [
        pltpu.SemaphoreType.DMA((remote,)),
        pltpu.SemaphoreType.DMA((remote,)),
        pltpu.SemaphoreType.DMA((local,)),
    ]


def run_jobs(jobs):
    live = list(jobs)
    while live:
        still = []
        for job in live:
            try:
                next(job)
                still.append(job)
            except StopIteration:
                pass
        live = still


def all_of(start, length):
    return pl.ds(start, length)


def gather_xy(net, land, own, cut, pos, with_core):
    y, x, c, z = pos
    width = own.shape[-1]
    first, second = pl.ds(0, cut), pl.ds(cut, width - cut)

    def place(yy, xx, columns):
        if with_core:
            return land.at[yy, xx, c, :, columns]
        return land.at[yy, xx, :, columns]

    whole = slice(None)
    mine = land.at[y, x, c] if with_core else land.at[y, x]
    kept = net.keep(own, mine)
    along_x = [
        net.put(own.at[:, first], place(y, x, first), device(y, x + d, c, z)) for d in (1, 3, 2)
    ]
    along_y = [
        net.put(own.at[:, second], place(y, x, second), device(y + d, x, c, z)) for d in (1, 3, 2)
    ]
    yield
    kept.wait()
    for copy in along_x:
        copy.wait_recv()
    row = place(y, whole, first)
    then_y = [net.put(row, row, device(y + d, x, c, z)) for d in (1, 3)]
    passed = []
    if with_core:
        passed.append(net.put(row, row, sibling(pos)))
    for copy in along_y:
        copy.wait_recv()
    column = place(whole, x, second)
    then_x = [net.put(column, column, device(y, x + d, c, z)) for d in (1, 3)]
    if with_core:
        passed.append(net.put(column, column, sibling(pos)))
    yield
    relays = []
    for d, half in ((1, pl.ds(0, 2)), (3, pl.ds(2, 2))):
        yy, xx = lax.rem(y + 4 - d, 4), lax.rem(x + 4 - d, 4)
        then_y[d // 2].wait_recv()
        part = place(yy, half, first)
        relays.append(net.put(part, part, device(y + d, x, c, z)))
        then_x[d // 2].wait_recv()
        part = place(half, xx, second)
        relays.append(net.put(part, part, device(y, x + d, c, z)))
        if with_core:
            for got in (place(yy, whole, first), place(whole, xx, second)):
                passed.append(net.put(got, got, sibling(pos)))
    yield
    for copy in relays:
        copy.wait_recv()
    if with_core:
        yy, xx = lax.rem(y + 2, 4), lax.rem(x + 2, 4)
        for got in (place(yy, whole, first), place(whole, xx, second)):
            passed.append(net.put(got, got, sibling(pos)))
    yield
    for copy in passed:
        copy.wait_recv()


def pick_rows(groups):
    rows = lax.broadcasted_iota(jnp.int32, (12 * groups, 16 * groups), 0)
    cols = lax.broadcasted_iota(jnp.int32, (12 * groups, 16 * groups), 1)
    piece = cols // 16
    within = cols - piece * 16
    return jnp.where((rows == piece * 12 + within) & (within < 12), 1.0, 0.0).astype(BF)


def squeeze_rows(pieces, groups):
    flat = pieces.reshape(groups * 16, pieces.shape[-1])
    return jnp.dot(pick_rows(groups), flat, preferred_element_type=F32).astype(BF)


def spread_rows(rows, groups):
    wide = lax.dot_general(
        pick_rows(groups), rows, (((0,), (0,)), ((), ())), preferred_element_type=F32
    )
    return wide.astype(BF).reshape(groups, 16, rows.shape[-1])


def mult(value, of):
    return pl.multiple_of(value, of)


def transposed(value):
    return jnp.transpose(value.astype(F32), (1, 0)).astype(BF)


SM = pl.BlockSpec(memory_space=pltpu.SMEM)


def home_block(pos, z):
    y, x, c, _ = pos
    b = (y * 4 + x) * 2 + c
    return jnp.where(z < 2, b, NBLK - 1 - b)


RW = D + SMALL
FLOOR = -1e29
ROW_ROW = (((1,), (1,)), ((), ()))
COL_COL = (((0,), (0,)), ((), ()))
EXP_SCALE = SCALE * LOG2E


def exchange_heads(to_tokens, pos, src_at, dst_at, ss, rs):
    y, x, c, z = pos
    b = (y * 4 + x) * 2 + c

    def ends(k):
        target = (home_block(pos, k if to_tokens else z), k)
        return src_at(k), dst_at(z), target, (target[0] == b) & (k == z)

    def remote(k):
        part, slot, target, _ = ends(k)
        return pltpu.make_async_remote_copy(
            src_ref=part,
            dst_ref=slot,
            send_sem=ss.at[k],
            recv_sem=rs.at[z],
            device_id=target,
            device_id_type=MESH,
        )

    def start(k):
        part, slot, _, stays = ends(k)

        @pl.when(stays)
        def _():
            pltpu.make_async_copy(part, slot, rs.at[z]).start()

        @pl.when(jnp.logical_not(stays))
        def _():
            remote(k).start()

    def wait():
        for k in range(4):
            pltpu.make_async_copy(dst_at(k), dst_at(k), rs.at[k]).wait()
        for k in range(4):

            @pl.when(jnp.logical_not(ends(k)[3]))
            def _():
                remote(k).wait_send()

    return start, wait


def query_places(bounds, lo, hi):
    lane = lax.broadcasted_iota(jnp.int32, (1, 2 * PAIR), 1)
    at = jnp.where(lane < PAIR, lo, hi) * HALF + lax.rem(lane, HALF)
    first = jnp.where(at >= bounds[1], bounds[1], jnp.where(at >= bounds[0], bounds[0], 0))
    return at, first


def turn(n):
    return jnp.where(n == 2, 3, jnp.where(n == 3, 2, n))


def forward_kernel(
    bounds, tok, wq, wo, we, gy, used,
    wo_out, wq_out, kv_out, q_out, o_out, lse_out, tok_out,
    hidden_out, hidden_grad_out, hidden_low_out, gains_out, small_out, do_out, out_parts, dwe_out,
    wq_z, wq_slab, wq_land, wo_z, wo_slab, wo_land, we_z, we_slab, we_land, tok_all, kv_land, q_in,
    qt, m_ref, l_ref, acc, mixed, own_rows, rows_all, gy_all, inner_all, pre_all, parts, out_stage,
    core_land, both, z_land, dwe_stage, mixed_grad, do_in, ss, rs, ls, hs, hr, gs, gr, hs2, hr2,
):
    pos = position()
    y, x, c, z = pos
    b = (y * 4 + x) * 2 + c
    my, mx, mc, _ = mirror(pos)
    greet(
        z_peers(pos)
        + xy_peers(pos)
        + [device(my, mx, mc, d) for d in range(4)]
        + other_column(pos)
    )
    net = Net(ss, rs, ls)

    wq_pieces = [
        net.put(wq.at[lax.rem(z + d, 4)], wq_z.at[z], device(y, x, c, z + d)) for d in (1, 3, 2)
    ]
    wq_kept = net.keep(wq.at[z], wq_z.at[z])

    def out_weights():
        pieces = [net.put(wo, wo_z.at[z], device(y, x, c, z + d)) for d in (1, 3, 2)]
        kept = net.keep(wo, wo_z.at[z])
        yield
        kept.wait()
        for copy in pieces:
            copy.wait_recv()
        wo_slab[...] = squeeze_rows(wo_z[...], 4)
        yield from gather_xy(net, wo_land, wo_slab, D // 2, pos, True)

    def expert_weights():
        me = c * 4 + z
        pieces = []
        for dc in (0, 1):
            for d in (0, 1, 3, 2):
                if (dc, d) == (0, 0):
                    continue
                cc, zz = lax.rem(c + dc, 2), lax.rem(z + d, 4)
                pieces.append(net.put(we.at[cc * 4 + zz], we_z.at[me], device(y, x, cc, zz)))
        kept = net.keep(we.at[me], we_z.at[me])
        yield
        kept.wait()
        for copy in pieces:
            copy.wait_recv()
        we_slab[...] = squeeze_rows(we_z[...], 8)
        yield from gather_xy(net, we_land, we_slab, 1024, pos, False)

    def cotangent():
        mine = gy_all.at[z, c]
        kept = net.keep(gy, mine)
        copies = [(d, net.put(gy, mine, device(y, x, c, z + d))) for d in (1, 3, 2)]
        passed = [net.put(gy, mine, sibling(pos))]
        yield
        for d, copy in copies:
            copy.wait_recv()
            got = gy_all.at[lax.rem(z + 4 - d, 4), c]
            passed.append(net.put(got, got, sibling(pos)))
        yield
        kept.wait()
        for copy in passed:
            copy.wait_recv()

    def pump(job):
        try:
            next(job)
        except StopIteration:
            pass

    wo_job, we_job, gy_job = out_weights(), expert_weights(), cotangent()
    pump(wo_job)
    tok_copies = [net.put(tok, tok_all.at[z], device(y, x, c, z + d)) for d in (1, 3, 2)]
    tok_kept = net.keep(tok, tok_all.at[z])
    pump(we_job)
    pump(gy_job)

    wq_kept.wait()
    for copy in wq_pieces:
        copy.wait_recv()
    wq_slab[...] = squeeze_rows(wq_z[...], 4)
    wq_job = gather_xy(net, wq_land, wq_slab, QW, pos, True)
    pump(wq_job)
    pump(wo_job)
    pump(wq_job)
    pump(wo_job)
    pump(wq_job)
    pump(wq_job)
    pump(wq_job)
    wq_saved = net.keep(wq_land, wq_out)

    for i in range(4):
        part = wq_land[i, :, :, :, GROUP_W:].reshape(QW, SMALL)
        one_hot = (
            lax.broadcasted_iota(jnp.int32, (16, SMALL), 0)
            == lax.broadcasted_iota(jnp.int32, (16, SMALL), 1)
        ).astype(BF)
        gains_out[:, i * QW : (i + 1) * QW] = lax.dot_general(
            one_hot, part, (((1,), (1,)), ((), ())), preferred_element_type=F32
        )
    tok_kept.wait()
    for copy in tok_copies:
        copy.wait_recv()
    tok_saved = net.keep(tok_all, tok_out)
    gain_attn = gains_out[EXPERTS + 1 : EXPERTS + 2, :]

    def normalise(i, carried):
        rows = tok_all[i].astype(F32)
        unit = rows * lax.rsqrt(jnp.mean(rows * rows, axis=-1, keepdims=True) + epsilon)
        out_stage[i // 2, lax.rem(i, 2)] = (unit * gain_attn).astype(BF)
        return carried

    lax.fori_loop(0, 4, normalise, 0)
    joined = jnp.dot(
        out_stage[...].reshape(BLK, D),
        wq_land[...].reshape(D, WQ)[:, :GROUP_W],
        preferred_element_type=F32,
    ).astype(BF)
    for half in range(2):
        rows = joined[half * HALF : (half + 1) * HALF]
        q_out[half] = rows[:, :QW]
        kv_land[y, x, c, half] = rows[:, QW:]

    swapped = net.put(q_out.at[1], q_in, device(my, mx, mc, z))
    whole = slice(None)
    along_x, along_y = [], []
    even, odd = kv_land.at[y, x, c, 0], kv_land.at[y, x, c, 1]
    for d in (1, 3, 2):
        along_x.append(net.put(even, even, device(y, x + d, c, z)))
        along_y.append(net.put(odd, odd, device(y + d, x, c, z)))
    m_ref[...] = jnp.full_like(m_ref, FLOOR)
    l_ref[...] = jnp.zeros_like(l_ref)
    acc[...] = jnp.zeros_like(acc)
    lo, hi = 2 * b, 2 * (NBLK - b) - 1
    at, first = query_places(bounds, lo, hi)
    for copy in along_x:
        copy.wait_recv()
    row = kv_land.at[y, whole, c, 0]
    from_y, crossed_y, crossed_x = net.reserve(4), net.reserve(4), net.reserve(4)
    for d in (1, 3):
        net.put_at(from_y + d, row, row, device(y + d, x, c, z))
    net.put_at(crossed_y, row, row, sibling(pos))
    for copy in along_y:
        copy.wait_recv()
    column = kv_land.at[whole, x, c, 1]
    from_x = net.reserve(4)
    for d in (1, 3):
        net.put_at(from_x + d, column, column, device(y, x + d, c, z))
    relay_y, relay_x = net.reserve(4), net.reserve(4)
    net.put_at(crossed_x, column, column, sibling(pos))
    pump(wo_job)
    pump(wo_job)
    swapped.wait_recv()
    for h in range(QPG):
        for i, rows in enumerate((q_out.at[0], q_in)):
            lanes = slice(i * PAIR + h * HALF, i * PAIR + (h + 1) * HALF)
            qt[:, lanes] = transposed(rows[:, h * HD : (h + 1) * HD])
    q_out[2] = q_in[...]

    def update(ids, yy, xx, cc, half, masked):
        k_rows = kv_land[yy, xx, cc, half, :, :HD]
        v_rows = kv_land[yy, xx, cc, half, :, HD:]
        lanes = LANES[ids]
        scores = jnp.dot(k_rows, qt[:, lanes], preferred_element_type=F32)
        if masked:
            chunk = ((yy * 4 + xx) * 2 + cc) * 2 + half
            key_at = chunk * HALF + lax.broadcasted_iota(jnp.int32, scores.shape, 0)
            allowed = (key_at >= first[:, lanes]) & (key_at <= at[:, lanes])
            scores = jnp.where(allowed, scores, LOW)
        m_old = m_ref[:, lanes]
        m_new = jnp.maximum(m_old, jnp.max(scores, axis=0, keepdims=True))
        p = jnp.exp2((scores - m_new) * EXP_SCALE)
        alpha = jnp.exp2((m_old - m_new) * EXP_SCALE)
        m_ref[:, lanes] = m_new
        l_ref[:, lanes] = l_ref[:, lanes] * alpha + jnp.sum(p, axis=0, keepdims=True)
        acc[:, lanes] = acc[:, lanes] * alpha + lax.dot_general(
            v_rows, p.astype(BF), COL_COL, preferred_element_type=F32
        )

    late = 2 * NBLK - 2

    def chunk_step(yy, xx, cc, half):
        chunk = ((yy * 4 + xx) * 2 + cc) * 2 + half
        in_lo, in_hi = chunk <= lo, chunk <= hi
        masked = (chunk <= 1) | (chunk == lo) | (chunk == hi)
        early = chunk < late
        plain = early & jnp.logical_not(masked)

        @pl.when(plain & in_lo & in_hi)
        def _():
            update((0, 1), yy, xx, cc, half, False)

        @pl.when(plain & in_lo & jnp.logical_not(in_hi))
        def _():
            update((0,), yy, xx, cc, half, False)

        @pl.when(plain & in_hi & jnp.logical_not(in_lo))
        def _():
            update((1,), yy, xx, cc, half, False)

        @pl.when(early & masked)
        def _():
            update((0, 1), yy, xx, cc, half, True)

    def stage(n, carried):
        d = turn(n)
        yy, xx = lax.rem(y + 4 - d, 4), lax.rem(x + 4 - d, 4)
        net.arrived(crossed_y + d, kv_land.at[yy, whole, 1 - c, 0])
        net.arrived(crossed_x + d, kv_land.at[whole, xx, 1 - c, 1])

        def step(t, carried):
            half = t // 8
            chunk_step(
                jnp.where(half == 0, yy, (t - 8) // 2),
                jnp.where(half == 0, t // 2, xx),
                lax.rem(t, 2),
                half,
            )
            return carried

        lax.fori_loop(0, 16, step, 0)
        return carried

    lax.fori_loop(0, 1, stage, 0)
    for e in (1, 3):
        near_y, near_x = lax.rem(y + 4 - e, 4), lax.rem(x + 4 - e, 4)
        part = pl.ds(e - 1, 2)
        net.arrived(from_y + e, row)
        line = kv_land.at[near_y, part, c, 0]
        net.put_at(relay_y + e, line, line, device(y + e, x, c, z))
        net.arrived(from_x + e, column)
        line = kv_land.at[part, near_x, c, 1]
        net.put_at(relay_x + e, line, line, device(y, x + e, c, z))
    for e in (1, 3):
        near_y, near_x = lax.rem(y + 4 - e, 4), lax.rem(x + 4 - e, 4)
        line = kv_land.at[near_y, whole, c, 0]
        net.put_at(crossed_y + e, line, line, sibling(pos))
        line = kv_land.at[whole, near_x, c, 1]
        net.put_at(crossed_x + e, line, line, sibling(pos))
    pump(we_job)
    lax.fori_loop(1, 2, stage, 0)
    pump(we_job)
    far_y, far_x = lax.rem(y + 2, 4), lax.rem(x + 2, 4)
    for e in (1, 3):
        part = pl.ds(e - 1, 2)
        net.arrived(relay_y + e, kv_land.at[far_y, part, c, 0])
        net.arrived(relay_x + e, kv_land.at[part, far_x, c, 1])
    line = kv_land.at[far_y, whole, c, 0]
    net.put_at(crossed_y + 2, line, line, sibling(pos))
    line = kv_land.at[whole, far_x, c, 1]
    net.put_at(crossed_x + 2, line, line, sibling(pos))
    lax.fori_loop(2, 4, stage, 0)
    for n in range(4):
        for k in (crossed_y, crossed_x):
            net.left(k + n, row)
    for n in (1, 3):
        net.left(from_y + n, row)
        net.left(from_x + n, column)
        net.left(relay_y + n, kv_land.at[y, pl.ds(0, 2), c, 0])
        net.left(relay_x + n, kv_land.at[pl.ds(0, 2), x, c, 1])
    kv_saved = net.keep(kv_land, kv_out)

    for i, chunk in enumerate((lo, hi)):

        @pl.when(chunk >= late)
        def _():
            lanes = LANES[(i,)]
            third = at[:, lanes] >= bounds[1]
            m_ref[:, lanes] = jnp.where(third, FLOOR, m_ref[:, lanes])
            l_ref[:, lanes] = jnp.where(third, 0.0, l_ref[:, lanes])
            acc[:, lanes] = jnp.where(third, 0.0, acc[:, lanes])
            lax.fori_loop(0, 2, lambda half, _: update((i,), 3, 3, 1, half, True), None)

    start, wait_mixed = exchange_heads(
        True, pos, lambda k: o_out.at[k], lambda g: mixed.at[:, pl.ds(mult(g * QW, QW), QW)], hs, hr
    )
    for i in range(2):
        for h in range(QPG):
            lanes = slice(i * PAIR + h * HALF, i * PAIR + (h + 1) * HALF)
            total = l_ref[:, lanes]
            lse_out[:, lanes] = m_ref[:, lanes] * EXP_SCALE + jnp.log(total) * LOG2E
            value = jnp.transpose(acc[:, lanes] / total, (1, 0)).astype(BF)
            o_out[2 * i, :, h * HD : (h + 1) * HD] = value[:ROWS]
            o_out[2 * i + 1, :, h * HD : (h + 1) * HD] = value[ROWS:]
        start(2 * i)
        start(2 * i + 1)

    pump(wo_job)
    pump(wo_job)
    wo_saved = net.keep(wo_land, wo_out)
    wait_mixed()
    pump(we_job)

    def add_hidden(i, carried):
        columns = pl.ds(mult(i * QW, QW), QW)
        hidden_out[:, columns] = tok[:, columns].astype(F32) + lax.dot_general(
            mixed[...], wo_land[i].reshape(QW, D), ROW_ROW, preferred_element_type=F32
        )
        return carried

    lax.fori_loop(0, 4, add_hidden, 0)
    hidden = hidden_out[...]
    unit = hidden * lax.rsqrt(jnp.mean(hidden * hidden, axis=-1, keepdims=True) + epsilon)
    low = (unit * gains_out[EXPERTS : EXPERTS + 1, :]).astype(BF)
    own_rows[:, :D] = low
    small_weights = wq_land[:, :, :, :, GROUP_W:].reshape(D, SMALL)
    logits = jnp.dot(low, small_weights, preferred_element_type=F32)
    is_used = used[...] > 0.0
    top = jnp.max(jnp.where(is_used, logits, LOW), axis=-1, keepdims=True)
    raised = jnp.where(is_used, jnp.exp(logits - top), 0.0)
    route = raised / jnp.sum(raised, axis=-1, keepdims=True)
    coarse = route.astype(BF).astype(F32)
    own_rows[:, D:] = (coarse + pltpu.roll(route - coarse, EXPERTS, 1)).astype(BF)

    mine = rows_all.at[z, c]
    rows_kept = net.keep(own_rows, mine)
    from_z, crossed_z = net.reserve(4), net.reserve(4)
    relay_z = net.reserve(4)
    for d in (1, 3):
        net.put_at(from_z + d, own_rows, mine, device(y, x, c, z + d))
    net.put_at(crossed_z, own_rows, mine, sibling(pos))
    for job in (gy_job, we_job, wo_job, wq_job):
        for _ in job:
            pass
    rows_kept.wait()
    to_core, to_z = net.reserve(4), net.reserve(4)
    me = c * 4 + z
    gate_columns, up_columns, down_columns = (slice(i * UP, (i + 1) * UP) for i in range(3))

    def weights(columns):
        return we_land[:, :, :, columns].reshape(D, UP)

    def finish_block(n):
        d, slot = turn(n), lax.rem(n, 2)
        zz = lax.rem(z + 4 - d, 4)
        net.arrived(to_core + n, core_land.at[n])
        both[n] = (parts[slot, c].astype(F32) + core_land[n].astype(F32)).astype(BF)
        net.left(to_core + n, parts.at[slot, 1 - c])

        @pl.when(n > 0)
        def _():
            net.put_at(to_z + d, both.at[n], z_land.at[d], device(y, x, c, zz))

    def expert_block(n, carried):
        d, slot = turn(n), lax.rem(n, 2)
        zz = lax.rem(z + 4 - d, 4)
        got = rows_all.at[zz, c]

        @pl.when(n == 1)
        def _():
            for e in (1, 3):
                near = rows_all.at[lax.rem(z + 4 - e, 4), c]
                net.arrived(from_z + e, near)
                part = near.at[pl.ds((e - 1) * 32, 64)]
                net.put_at(relay_z + e, part, part, device(y, x, c, z + e))
                net.put_at(crossed_z + e, near, near, sibling(pos))

        @pl.when(n == 3)
        def _():
            for e in (1, 3):
                net.arrived(relay_z + e, got.at[pl.ds((e - 1) * 32, 64)])
            net.put_at(crossed_z + 2, got, got, sibling(pos))

        net.arrived(crossed_z + d, rows_all.at[zz, 1 - c])

        @pl.when(n > 1)
        def _():
            pltpu.make_async_copy(out_stage.at[slot], out_stage.at[slot], gs.at[slot]).wait()

        rows = rows_all[zz].reshape(2 * ROWS, RW)
        x_rows, lanes = rows[:, :D], rows[:, D:].astype(F32)
        lane = lax.broadcasted_iota(jnp.int32, lanes.shape, 1)
        route = jnp.sum(
            jnp.where((lane == me) | (lane == me + EXPERTS), lanes, 0.0), axis=-1, keepdims=True
        )
        gy_rows = gy_all[zz].reshape(2 * ROWS, D)
        gate = jnp.dot(x_rows, weights(gate_columns), preferred_element_type=F32)
        up = jnp.dot(x_rows, weights(up_columns), preferred_element_type=F32)
        raw = jnp.dot(gy_rows, weights(down_columns), preferred_element_type=F32)
        unit_lane = lax.broadcasted_iota(jnp.int32, gate.shape, 1)
        share = jnp.where(unit_lane < FE, route, 1.0)
        sig = 1.0 / (1.0 + jnp.exp(-gate))
        silu = gate * sig
        inner = silu * up
        scaled = (inner * share).astype(BF)
        inner_all[zz] = scaled
        route_grad = jnp.sum(inner[:, :FE] * raw[:, :FE], axis=-1, keepdims=True)
        inner_grad = raw * share
        pre_grad = jnp.concatenate(
            [inner_grad * up * (sig + silu * (1.0 - sig)), inner_grad * silu], axis=-1
        ).astype(BF)
        pre_all[zz] = pre_grad
        out_stage[slot] = (
            lax.dot_general(scaled, weights(down_columns), ROW_ROW, preferred_element_type=F32)
            .astype(BF)
            .reshape(2, ROWS, D)
        )
        pltpu.make_async_copy(out_stage.at[slot], out_parts.at[zz], gs.at[slot]).start()
        rows_grad = lax.dot_general(
            pre_grad[:, :UP], weights(gate_columns), ROW_ROW, preferred_element_type=F32
        ) + lax.dot_general(
            pre_grad[:, UP:], weights(up_columns), ROW_ROW, preferred_element_type=F32
        )
        parts[slot, :, :, :D] = rows_grad.astype(BF).reshape(2, ROWS, D)
        high = route_grad.astype(BF).astype(F32)
        parts[slot, :, :, D:] = (
            jnp.where(lane == me, high, 0.0) + jnp.where(lane == me + EXPERTS, route_grad - high, 0.0)
        ).astype(BF).reshape(2, ROWS, SMALL)
        net.put_at(to_core + n, parts.at[slot, 1 - c], core_land.at[n], sibling(pos))

        @pl.when(n > 0)
        def _():
            finish_block(n - 1)

        return carried

    lax.fori_loop(0, 4, expert_block, 0)
    finish_block(3)
    for slot in range(2):
        pltpu.make_async_copy(out_stage.at[slot], out_stage.at[slot], gs.at[slot]).wait()

    def weight_grads(t, carried):
        slot = lax.rem(t, 2)

        @pl.when(t > 1)
        def _():
            pltpu.make_async_copy(dwe_stage.at[slot], dwe_stage.at[slot], gr.at[slot]).wait()

        columns = pl.ds(mult(t * QW, QW), QW)
        for i in range(3):
            value = jnp.zeros((QW, UP), F32)
            for k in range(4):
                left = (rows_all if i < 2 else gy_all)[k, :, :, columns].reshape(2 * ROWS, QW)
                right = pre_all[k, :, i * UP : (i + 1) * UP] if i < 2 else inner_all[k]
                value = value + lax.dot_general(left, right, COL_COL, preferred_element_type=F32)
            dwe_stage[slot, :, :, i * UP : (i + 1) * UP] = value.astype(BF).reshape(4, 96, UP)
        pltpu.make_async_copy(dwe_stage.at[slot], dwe_out.at[t], gr.at[slot]).start()
        return carried

    lax.fori_loop(0, 4, weight_grads, 0)

    for d in (1, 2, 3):
        net.arrived(to_z + d, z_land.at[d])

    def total(columns):
        value = both[0, :, columns].astype(F32)
        for d in (1, 2, 3):
            value = value + z_land[d, :, columns].astype(F32)
        return value

    lane = lax.broadcasted_iota(jnp.int32, (ROWS, SMALL), 1)
    route_grads = total(slice(D, RW))
    route_grads = route_grads + pltpu.roll(route_grads, SMALL - EXPERTS, 1)
    logits_grad = (
        route * (route_grads - jnp.sum(route * route_grads, axis=-1, keepdims=True))
    ).astype(BF)
    normed_grad = total(slice(0, D)) + lax.dot_general(
        logits_grad, small_weights, ROW_ROW, preferred_element_type=F32
    )
    hidden = hidden_out[...]
    scale = lax.rsqrt(jnp.mean(hidden * hidden, axis=-1, keepdims=True) + epsilon)
    unit = hidden * scale
    dn = normed_grad * gains_out[EXPERTS : EXPERTS + 1, :]
    hidden_grad = gy_all[z, c].astype(F32) + scale * (
        dn - unit * jnp.mean(dn * unit, axis=-1, keepdims=True)
    )
    hidden_grad_out[...] = hidden_grad
    hidden_low = hidden_grad.astype(BF)
    hidden_low_out[...] = hidden_low
    total_grad = jnp.zeros((ROWS, D), F32)
    for i in range(4):
        total_grad = total_grad + jnp.dot(
            hidden_low[:, i * QW : (i + 1) * QW],
            wo_land[i].reshape(QW, D),
            preferred_element_type=F32,
        )
    start, wait_heads = exchange_heads(
        False, pos, lambda g: mixed_grad.at[g], lambda k: do_in.at[k], hs2, hr2
    )
    for g in range(4):
        mixed_grad[g] = total_grad[:, g * QW : (g + 1) * QW].astype(BF)
        start(g)
    gain_column = jnp.where(lane == EXPERTS, 1.0, 0.0).astype(BF)
    small_out[...] = (
        lax.dot_general(own_rows[:, :D], logits_grad, COL_COL, preferred_element_type=F32)
        + lax.dot_general(
            (normed_grad * unit).astype(BF), gain_column, COL_COL, preferred_element_type=F32
        )
    ).astype(BF)
    for n in range(4):
        net.left(crossed_z + n, own_rows)
        if n:
            net.left(to_z + n, both.at[n])
    for n in (1, 3):
        net.left(from_z + n, own_rows)
        net.left(relay_z + n, own_rows.at[pl.ds(0, 64)])
    for slot in range(2):
        pltpu.make_async_copy(dwe_stage.at[slot], dwe_stage.at[slot], gr.at[slot]).wait()
    wait_heads()
    do_out[...] = do_in[...]
    for copy in (wq_saved, tok_saved, kv_saved, wo_saved):
        copy.wait()
    net.finish()


def forward(bounds, tok, wq, wo, we, gy, used):
    outs = {
        "wo": ((4, 4, 2, 48, D), BF, ANY),
        "wq": ((4, 4, 2, 48, WQ), BF, ANY),
        "kv": ((4, 4, 2, 2, HALF, 2 * HD), BF, ANY),
        "q": ((3, HALF, QW), BF, VM),
        "o": ((4, ROWS, QW), BF, VM),
        "lse": ((1, 2 * PAIR), F32, VM),
        "tok": ((4, ROWS, D), BF, ANY),
        "hidden": ((ROWS, D), F32, VM),
        "hidden_grad": ((ROWS, D), F32, VM),
        "hidden_low": ((ROWS, D), BF, VM),
        "gains": ((16, D), F32, VM),
        "small": ((D, SMALL), BF, VM),
        "do": ((4, ROWS, QW), BF, VM),
        "out_parts": ((4, 2, ROWS, D), BF, ANY),
        "dwe": ((4, 4, 96, WE), BF, ANY),
    }
    values = pl.pallas_call(
        forward_kernel,
        name="forward",
        out_shape=tuple(jax.ShapeDtypeStruct(s, t) for s, t, _ in outs.values()),
        in_specs=[SM, VM, ANY, ANY, ANY, ANY, VM],
        out_specs=tuple(m for _, _, m in outs.values()),
        scratch_shapes=[
            pltpu.VMEM((4, 16, WQ), BF),
            pltpu.VMEM((48, WQ), BF),
            pltpu.VMEM((4, 4, 2, 48, WQ), BF),
            pltpu.VMEM((4, 16, D), BF),
            pltpu.VMEM((48, D), BF),
            pltpu.VMEM((4, 4, 2, 48, D), BF),
            pltpu.VMEM((8, 16, WE), BF),
            pltpu.VMEM((96, WE), BF),
            pltpu.VMEM((4, 4, 96, WE), BF),
            pltpu.VMEM((4, ROWS, D), BF),
            pltpu.VMEM((4, 4, 2, 2, HALF, 2 * HD), BF),
            pltpu.VMEM((HALF, QW), BF),
            pltpu.VMEM((HD, 2 * PAIR), BF),
            pltpu.VMEM((1, 2 * PAIR), F32),
            pltpu.VMEM((1, 2 * PAIR), F32),
            pltpu.VMEM((HD, 2 * PAIR), F32),
            pltpu.VMEM((ROWS, D), BF),
            pltpu.VMEM((ROWS, RW), BF),
            pltpu.VMEM((4, 2, ROWS, RW), BF),
            pltpu.VMEM((4, 2, ROWS, D), BF),
            pltpu.VMEM((4, 2 * ROWS, UP), BF),
            pltpu.VMEM((4, 2 * ROWS, 2 * UP), BF),
            pltpu.VMEM((2, 2, ROWS, RW), BF),
            pltpu.VMEM((2, 2, ROWS, D), BF),
            pltpu.VMEM((4, ROWS, RW), BF),
            pltpu.VMEM((4, ROWS, RW), BF),
            pltpu.VMEM((4, ROWS, RW), BF),
            pltpu.VMEM((2, 4, 96, WE), BF),
            pltpu.VMEM((4, ROWS, QW), BF),
            pltpu.VMEM((4, ROWS, QW), BF),
        ]
        + sems(144, 32)
        + [pltpu.SemaphoreType.DMA((4,))] * 6,
        compiler_params=pltpu.CompilerParams(
            collective_id=1, has_side_effects=True, vmem_limit_bytes=VMEM_LIMIT
        ),
    )(bounds, tok, wq, wo, we, gy, used)
    return dict(zip(outs, values))


def add_into(dst, left, right, rows):
    step = 32

    def body(i, carried):
        place = pl.ds(mult(i * step, step), step)
        dst[place, :] = (left[place, :].astype(F32) + right[place, :].astype(F32)).astype(
            dst.dtype
        )
        return carried

    lax.fori_loop(0, rows // step, body, 0)


def add_four(dst, parts, rows, step):
    def body(i, carried):
        place = pl.ds(mult(i * step, step), step)
        total = parts[0][place, :].astype(F32)
        for part in parts[1:]:
            total = total + part[place, :].astype(F32)
        dst[place, :] = total.astype(dst.dtype)
        return carried

    lax.fori_loop(0, rows // step, body, 0)


def sum_group(net, parts, pos, core_land, own, both, z_land, out):
    y, x, c, z = pos
    order = (0, 1, 3, 2)
    crossing, kept = [], []
    for d in order:
        zz = lax.rem(z + d, 4)
        crossing.append(net.put(parts.at[zz, 1 - c], core_land.at[zz], sibling(pos)))
        kept.append(net.keep(parts.at[zz, c], own.at[zz]))
    yield
    arriving = []
    for n, d in enumerate(order):
        zz = lax.rem(z + d, 4)
        crossing[n].wait_recv()
        kept[n].wait()
        add_into(both.at[zz], own.at[zz], core_land.at[zz], ROWS)
        if d:
            arriving.append(net.put(both.at[zz], z_land.at[d - 1], device(y, x, c, zz)))
    yield
    for copy in arriving:
        copy.wait_recv()
    add_four(out, [both.at[z]] + [z_land.at[d] for d in range(3)], ROWS, 32)


def group_scratch(width):
    return [
        pltpu.VMEM((4, ROWS, width), BF),
        pltpu.VMEM((4, ROWS, width), BF),
        pltpu.VMEM((4, ROWS, width), BF),
        pltpu.VMEM((3, ROWS, width), BF),
    ]


def fold_parts(own, land, total, rows):
    step = 16

    def body(i, carried):
        q = i // (rows // step)
        place = pl.ds(mult(lax.rem(i, rows // step) * step, step), step)
        value = own[q, place, :].astype(F32)
        for d in range(3):
            value = value + land[d, q, place, :].astype(F32)
        total[q, place, :] = value.astype(BF)
        return carried

    lax.fori_loop(0, 4 * (rows // step), body, 0)


def scatter_first(net, src, pos, cut, a_own, a_land, b_own, b_land, a_sum, b_sum):
    y, x, c, z = pos
    rows, width = src.shape[2], src.shape[3]
    first, second = pl.ds(0, cut), pl.ds(cut, width - cut)
    whole = slice(None)
    keep_a = net.keep(src.at[whole, x, whole, first], a_own)
    keep_b = net.keep(src.at[y, whole, whole, second], b_own)
    to_x, to_y = [], []
    for d in (1, 3, 2):
        xx, yy = lax.rem(x + d, 4), lax.rem(y + d, 4)
        to_x.append(
            net.put(src.at[whole, xx, whole, first], a_land.at[d - 1], device(y, xx, c, z))
        )
        to_y.append(
            net.put(src.at[yy, whole, whole, second], b_land.at[d - 1], device(yy, x, c, z))
        )
    yield
    keep_a.wait()
    for copy in to_x:
        copy.wait_recv()
    fold_parts(a_own, a_land, a_sum, rows)
    keep_b.wait()
    for copy in to_y:
        copy.wait_recv()
    fold_parts(b_own, b_land, b_sum, rows)


def scatter_second(net, pos, cut, a_sum, a_last, b_sum, b_last, out):
    y, x, c, z = pos
    rows, width = out.shape
    last_y, last_x = [], []
    for d in (1, 3, 2):
        yy, xx = lax.rem(y + d, 4), lax.rem(x + d, 4)
        last_y.append(net.put(a_sum.at[yy], a_last.at[d - 1], device(yy, x, c, z)))
        last_x.append(net.put(b_sum.at[xx], b_last.at[d - 1], device(y, xx, c, z)))
    yield
    for copy in last_y:
        copy.wait_recv()
    for copy in last_x:
        copy.wait_recv()
    step = 16
    first, second = slice(0, cut), slice(cut, width)

    def final(i, carried):
        place = pl.ds(mult(i * step, step), step)
        for at, own, last, columns in ((y, a_sum, a_last, first), (x, b_sum, b_last, second)):
            value = own[at, place, :].astype(F32)
            for d in range(3):
                value = value + last[d, place, :].astype(F32)
            out[place, columns] = value.astype(BF)
        return carried

    lax.fori_loop(0, rows // step, final, 0)


def first_scratch(rows, width, cut):
    shapes = []
    for w in (cut, width - cut):
        shapes += [pltpu.VMEM((4, rows, w), BF), pltpu.VMEM((3, 4, rows, w), BF)]
    return shapes


def second_scratch(rows, width, cut):
    return [pltpu.VMEM((3, rows, cut), BF), pltpu.VMEM((3, rows, width - cut), BF)]


def backward_kernel(
    bounds, q, o, do, lse, kv_in, dwe, hg, out_parts,
    dkv_out, dq_out, o_out, we_a, we_b, hg_all, out_sum,
    kv, o_in, dq_own, dq_in, q_rows, do_rows, qt, dot_t, delta, late_lse, dqt, part, core_land, both, a_land, b_land,
    a_sum, b_sum, a_last, b_last, *scratch,
):
    we_s = scratch[:4]
    group_s = scratch[4:8]
    ss, rs, ls = scratch[8:]
    pos = position()
    y, x, c, z = pos
    b = (y * 4 + x) * 2 + c
    net = Net(ss, rs, ls)
    kv_kept = net.keep(kv_in, kv)
    greet(z_peers(pos) + xy_peers(pos) + [device(*mirror(pos))] + other_column(pos))
    o_swap = net.put(o.at[pl.ds(2, 2)], o_in, device(*mirror(pos)))
    whole = slice(None)

    def experts():
        yield from scatter_first(net, dwe, pos, 1024, *we_s, we_a, we_b)

    def rows_of_group():
        mine = hg_all.at[z]
        kept = net.keep(hg, mine)
        copies = [net.put(hg, mine, device(y, x, c, z + d)) for d in (1, 3, 2)]
        yield
        kept.wait()
        for copy in copies:
            copy.wait_recv()

    def pump(job):
        try:
            next(job)
        except StopIteration:
            pass

    we_job = experts()
    out_job = sum_group(net, out_parts, pos, *group_s, out_sum)
    hg_job = rows_of_group()
    pump(out_job)
    pump(we_job)
    pump(hg_job)

    lo, hi = 2 * b, 2 * (NBLK - b) - 1
    late = 2 * NBLK - 2
    at, first = query_places(bounds, lo, hi)
    for i in range(2):
        for h in range(QPG):
            columns = slice(h * HD, (h + 1) * HD)
            lanes = slice(i * PAIR + h * HALF, i * PAIR + (h + 1) * HALF)
            q_rows[lanes, :] = q[2 * i, :, columns]
            qt[:, lanes] = transposed(q[2 * i, :, columns])
            rows = do[2 * i : 2 * i + 2, :, columns].reshape(HALF, HD)
            do_rows[lanes, :] = rows
            do_t = jnp.transpose(rows.astype(F32), (1, 0))
            o_t = jnp.transpose(
                o[2 * i : 2 * i + 2, :, columns].reshape(HALF, HD).astype(F32), (1, 0)
            )
            dot_t[:, lanes] = do_t.astype(BF)
            delta[:, lanes] = jnp.sum(do_t * o_t, axis=0, keepdims=True)
    late_lse[...] = jnp.where(at >= bounds[1], -LOW, lse[...])
    dqt[...] = jnp.zeros_like(dqt)
    kv_kept.wait()
    pump(out_job)

    def pairs(ids, yy, xx, cc, half, slot, masked):
        k_rows = kv[yy, xx, cc, half, :, :HD]
        v_rows = kv[yy, xx, cc, half, :, HD:]
        lanes = LANES[ids]
        scores = jnp.dot(k_rows, qt[:, lanes], preferred_element_type=F32)
        dp = jnp.dot(v_rows, dot_t[:, lanes], preferred_element_type=F32)
        if masked:
            chunk = ((yy * 4 + xx) * 2 + cc) * 2 + half
            key_at = chunk * HALF + lax.broadcasted_iota(jnp.int32, scores.shape, 0)
            allowed = (key_at >= first[:, lanes]) & (key_at <= at[:, lanes])
            p = jnp.where(allowed, jnp.exp2(scores * EXP_SCALE - lse[:, lanes]), 0.0)
        else:
            p = jnp.exp2(scores * EXP_SCALE - late_lse[:, lanes])
        ds = (p * (dp - delta[:, lanes])).astype(BF)
        dv = jnp.dot(p.astype(BF), do_rows[lanes, :], preferred_element_type=F32)
        dk = jnp.dot(ds, q_rows[lanes, :], preferred_element_type=F32)
        dqt[:, lanes] += lax.dot_general(k_rows, ds, COL_COL, preferred_element_type=F32)
        part[slot, cc, half, :, :HD] = (dk * SCALE).astype(BF)
        part[slot, cc, half, :, HD:] = dv.astype(BF)

    def chunk_step(yy, xx, cc, half, slot):
        chunk = ((yy * 4 + xx) * 2 + cc) * 2 + half
        in_lo, in_hi = chunk <= lo, chunk <= hi
        special = (chunk <= 1) | (chunk == lo) | (chunk == hi) | (chunk >= late)
        masked = special & (in_lo | in_hi)
        plain = jnp.logical_not(special)

        @pl.when(plain & in_lo & in_hi)
        def _():
            pairs((0, 1), yy, xx, cc, half, slot, False)

        @pl.when(plain & in_lo & jnp.logical_not(in_hi))
        def _():
            pairs((0,), yy, xx, cc, half, slot, False)

        @pl.when(plain & in_hi & jnp.logical_not(in_lo))
        def _():
            pairs((1,), yy, xx, cc, half, slot, False)

        @pl.when(masked)
        def _():
            pairs((0, 1), yy, xx, cc, half, slot, True)

        @pl.when(jnp.logical_not(in_lo | in_hi))
        def _():
            part[slot, cc, half] = jnp.zeros((HALF, 2 * HD), BF)

    def chip(t):
        dy = jnp.where(
            t < 4,
            t,
            jnp.where(
                t < 7,
                1,
                jnp.where(
                    t < 10,
                    jnp.where(t == 7, 0, t - 6),
                    jnp.where(
                        t < 12, 3, jnp.where(t < 14, 2 * (t - 12), 2 * (15 - t))
                    ),
                ),
            ),
        )
        dx = jnp.where(
            t < 4,
            1,
            jnp.where(
                t < 7,
                jnp.where(t == 4, 0, t - 3),
                jnp.where(
                    t < 10,
                    3,
                    jnp.where(t < 12, 2 * (t - 10), jnp.where(t < 14, 2, 0)),
                ),
            ),
        )
        return lax.rem(y + dy, 4), lax.rem(x + dx, 4)

    to_core, to_x, to_y = net.reserve(16), net.reserve(4), net.reserve(4)

    def fold_chip(t):
        yy, xx = chip(t)
        slot = lax.rem(t, 2)
        net.arrived(to_core + t, core_land.at[yy, xx])
        both[yy, xx] = (part[slot, c].astype(F32) + core_land[yy, xx].astype(F32)).astype(BF)
        net.left(to_core + t, part.at[slot, 1 - c])

    def send_lines(d):
        xx, yy = lax.rem(x + d, 4), lax.rem(y + d, 4)
        net.put_at(to_x + d, both.at[whole, xx, 0], a_land.at[d], device(y, xx, c, z))
        net.put_at(to_y + d, both.at[yy, whole, 1], b_land.at[d], device(yy, x, c, z))

    far_x, far_y = net.reserve(4), net.reserve(4)

    def send_far(odd):
        xx, yy = lax.rem(x + 2, 4), lax.rem(y + 2, 4)
        for e in (odd, odd + 2):
            ye, xe = lax.rem(y + e, 4), lax.rem(x + e, 4)
            net.put_at(far_x + e, both.at[ye, xx, 0], a_land.at[2, ye], device(y, xx, c, z))
            net.put_at(far_y + e, both.at[yy, xe, 1], b_land.at[2, xe], device(yy, x, c, z))

    def chip_step(t, carried):
        yy, xx = chip(t)
        slot = lax.rem(t, 2)

        def step(n, carried):
            chunk_step(yy, xx, n // 2, lax.rem(n, 2), slot)
            return carried

        lax.fori_loop(0, 4, step, 0)
        net.put_at(to_core + t, part.at[slot, 1 - c], core_land.at[yy, xx], sibling(pos))

        @pl.when(t > 0)
        def _():
            fold_chip(t - 1)

        for at_chip, send in (
            (7, lambda: send_lines(1)),
            (12, lambda: (send_lines(3), send_far(1))),
            (15, lambda: send_far(0)),
        ):

            @pl.when(t == at_chip)
            def _():
                send()

        return carried

    lax.fori_loop(0, 16, chip_step, 0)
    for i in range(2):
        for h in range(QPG):
            lanes = slice(i * PAIR + h * HALF, i * PAIR + (h + 1) * HALF)
            dq_own[i, :, h * HD : (h + 1) * HD] = jnp.transpose(
                dqt[:, lanes] * SCALE, (1, 0)
            ).astype(BF)
    dq_swap = net.put(dq_own.at[1], dq_in, device(*mirror(pos)))
    lax.fori_loop(15, 16, lambda t, _: fold_chip(t), None)

    def fold_lines(own_at, land, total):
        def body(n, carried):
            q_at, place = n // 8, pl.ds(mult(lax.rem(n, 8) * 32, 32), 32)
            value = own_at(q_at, place).astype(F32)
            for d in (1, 2, 3):
                value = value + land[d, q_at, place, :].astype(F32)
            total[q_at, place, :] = value.astype(BF)
            return carried

        lax.fori_loop(0, 32, body, 0)

    for d in (1, 3):
        net.arrived(to_x + d, a_land.at[d])
    for e in range(4):
        net.arrived(far_x + e, a_land.at[2, e])
    fold_lines(lambda n, place: both[n, x, 0, place, :], a_land, a_sum)
    last_y = []
    for d in (1, 3, 2):
        yy = lax.rem(y + d, 4)
        last_y.append(net.put(a_sum.at[yy], a_last.at[d], device(yy, x, c, z)))
    for d in (1, 3):
        net.arrived(to_y + d, b_land.at[d])
    for e in range(4):
        net.arrived(far_y + e, b_land.at[2, e])
    fold_lines(lambda n, place: both[y, n, 1, place, :], b_land, b_sum)
    last_x = []
    for d in (1, 3, 2):
        xx = lax.rem(x + d, 4)
        last_x.append(net.put(b_sum.at[xx], b_last.at[d], device(y, xx, c, z)))
    pump(we_job)
    pump(out_job)
    o_swap.wait_recv()
    o_out[0] = o[0]
    o_out[1] = o[1]
    o_out[2] = o_in[0]
    o_out[3] = o_in[1]
    dq_swap.wait_recv()
    dq_out[0] = dq_own[0]
    dq_out[1] = dq_in[...]
    for copies, total, last, at, half in (
        (last_y, a_sum, a_last, y, 0),
        (last_x, b_sum, b_last, x, 1),
    ):
        for copy in copies:
            copy.wait_recv()
        value = total[at].astype(F32)
        for d in (1, 2, 3):
            value = value + last[d].astype(F32)
        dkv_out[half] = value.astype(BF)
    for job in (hg_job, out_job, we_job):
        for _ in job:
            pass
    for d in (1, 3):
        net.left(to_x + d, a_land.at[d])
        net.left(to_y + d, b_land.at[d])
    for e in range(4):
        net.left(far_x + e, a_land.at[2, e])
        net.left(far_y + e, b_land.at[2, e])
    net.finish()


def backward(bounds, q, o, do, lse, kv, dwe, hg, out_parts):
    return pl.pallas_call(
        backward_kernel,
        name="backward",
        out_shape=(
            jax.ShapeDtypeStruct((2, HALF, 2 * HD), BF),
            jax.ShapeDtypeStruct((2, HALF, QW), BF),
            jax.ShapeDtypeStruct((4, ROWS, QW), BF),
            jax.ShapeDtypeStruct((4, 96, 1024), BF),
            jax.ShapeDtypeStruct((4, 96, WE - 1024), BF),
            jax.ShapeDtypeStruct((4, ROWS, D), BF),
            jax.ShapeDtypeStruct((ROWS, D), F32),
        ),
        in_specs=[SM] + [VM] * 4 + [ANY] * 4,
        out_specs=(VM, VM, VM, VM, VM, ANY, VM),
        scratch_shapes=[
            pltpu.VMEM((4, 4, 2, 2, HALF, 2 * HD), BF),
            pltpu.VMEM((2, ROWS, QW), BF),
            pltpu.VMEM((2, HALF, QW), BF),
            pltpu.VMEM((HALF, QW), BF),
            pltpu.VMEM((2 * PAIR, HD), BF),
            pltpu.VMEM((2 * PAIR, HD), BF),
            pltpu.VMEM((HD, 2 * PAIR), BF),
            pltpu.VMEM((HD, 2 * PAIR), BF),
            pltpu.VMEM((1, 2 * PAIR), F32),
            pltpu.VMEM((1, 2 * PAIR), F32),
            pltpu.VMEM((HD, 2 * PAIR), F32),
            pltpu.VMEM((2, 2, 2, HALF, 2 * HD), BF),
            pltpu.VMEM((4, 4, 2, HALF, 2 * HD), BF),
            pltpu.VMEM((4, 4, 2, HALF, 2 * HD), BF),
            pltpu.VMEM((4, 4, HALF, 2 * HD), BF),
            pltpu.VMEM((4, 4, HALF, 2 * HD), BF),
            pltpu.VMEM((4, HALF, 2 * HD), BF),
            pltpu.VMEM((4, HALF, 2 * HD), BF),
            pltpu.VMEM((4, HALF, 2 * HD), BF),
            pltpu.VMEM((4, HALF, 2 * HD), BF),
        ]
        + first_scratch(96, WE, 1024)
        + group_scratch(D)
        + sems(72, 16),
        compiler_params=pltpu.CompilerParams(
            collective_id=7, has_side_effects=True, vmem_limit_bytes=VMEM_LIMIT
        ),
    )(bounds, q, o, do, lse, kv, dwe, hg, out_parts)


def close_kernel(
    dq, dkv, o, hg_in, tok_in, wq_in, gains, small, we_a_in, we_b_in,
    norm_grad, dwq_out, dwe_out, hg, tok, wq, we_a, we_b,
    joined, unit_all, n_part, n_land, dwq, w_land, w_both, *scratch,
):
    w_first, w_second, we_last = scratch[:4], scratch[4:6], scratch[6:8]
    w_a, w_b, w_rows, w_pieces, we_rows, we_pieces = scratch[8:14]
    ss, rs, ls = scratch[14:]
    pos = position()
    y, x, c, z = pos
    net = Net(ss, rs, ls)
    loads = [
        net.keep(src, dst)
        for src, dst in (
            (tok_in, tok), (hg_in, hg), (wq_in, wq), (we_a_in, we_a), (we_b_in, we_b)
        )
    ]
    greet(z_peers(pos) + xy_peers(pos) + other_column(pos))
    for copy in loads:
        copy.wait()
    experts_job = scatter_second(net, pos, 1024, we_a, we_last[0], we_b, we_last[1], we_rows)
    next(experts_job)
    joined[:, :, :QW] = dq[...].reshape(4, ROWS, QW)
    joined[:, :, QW:] = dkv[...].reshape(4, ROWS, 2 * HD)
    gain_attn = gains[EXPERTS + 1 : EXPERTS + 2, :]
    to_z, to_core = net.reserve(4), net.reserve(4)

    def normalise(k, carried):
        rows = tok[k].astype(F32)
        scale = lax.rsqrt(jnp.mean(rows * rows, axis=-1, keepdims=True) + epsilon)
        unit_all[k] = (rows * scale).astype(BF)
        return carried

    lax.fori_loop(0, 4, normalise, 0)

    def fold(t):
        net.arrived(to_core + t, w_land.at[t])

        def body(i, inner):
            xx, place = i // 3, pl.ds(mult(lax.rem(i, 3) * 16, 16), 16)
            w_both[t, xx, place, :] = (
                dwq[t, xx, c, place, :].astype(F32) + w_land[t, xx, place, :].astype(F32)
            ).astype(BF)
            return inner

        lax.fori_loop(0, 12, body, 0)
        net.left(to_core + t, w_land.at[t])

    def weight_grads(t, carried):
        columns = pl.ds(mult(t * QW, QW), QW)
        unit_grad = jnp.zeros((QW, GROUP_W), F32)
        wo_grad = jnp.zeros((QW, QW), F32)
        for k in range(4):
            unit_grad = unit_grad + lax.dot_general(
                unit_all[k, :, columns], joined[k], COL_COL, preferred_element_type=F32
            )
            wo_grad = wo_grad + lax.dot_general(
                hg[k, :, columns], o[k], COL_COL, preferred_element_type=F32
            )
        weights = wq[t].reshape(QW, WQ).astype(F32)
        lane = lax.broadcasted_iota(jnp.int32, (QW, SMALL), 1)
        here = lane == EXPERTS + 1
        small_weights = weights[:, GROUP_W:]
        gain = jnp.sum(jnp.where(here, small_weights, 0.0), axis=-1, keepdims=True)
        gain_grad = jnp.sum(unit_grad * weights[:, :GROUP_W], axis=-1, keepdims=True)
        small_grad = small[pl.ds(mult(t * QW, QW), QW), :].astype(F32)
        small_grad = jnp.where(here, gain_grad, small_grad)
        dwq[t, :, :, :, :GROUP_W] = (unit_grad * gain).astype(BF).reshape(4, 2, 48, GROUP_W)
        dwq[t, :, :, :, GROUP_W : GROUP_W + QW] = wo_grad.astype(BF).reshape(4, 2, 48, QW)
        dwq[t, :, :, :, GROUP_W + QW :] = small_grad.astype(BF).reshape(4, 2, 48, SMALL)
        net.put_at(to_core + t, dwq.at[t, :, 1 - c], w_land.at[t], sibling(pos))

        @pl.when(t > 0)
        def _():
            fold(t - 1)

        return carried

    lax.fori_loop(0, 4, weight_grads, 0)
    fold(3)
    weights_job = scatter_first(net, w_both, pos, GROUP_W, *w_first, w_a, w_b)
    next(weights_job)

    normed_grads = lax.dot_general(
        joined[...].reshape(BLK, GROUP_W),
        wq[...].reshape(D, WQ)[:, :GROUP_W],
        ROW_ROW,
        preferred_element_type=F32,
    )
    n_part[...] = normed_grads.astype(BF).reshape(4, ROWS, D)
    for d in (1, 3, 2):
        zz = lax.rem(z + d, 4)
        net.put_at(to_z + d, n_part.at[zz], n_land.at[d], device(y, x, c, zz))
    for _ in experts_job:
        pass
    we_pieces[...] = spread_rows(we_rows[...], 8)
    me = c * 4 + z
    expert_pieces = []
    for dc in (0, 1):
        for d in (0, 1, 3, 2):
            if (dc, d) == (0, 0):
                continue
            cc, zz = lax.rem(c + dc, 2), lax.rem(z + d, 4)
            expert_pieces.append(
                net.put(we_pieces.at[cc * 4 + zz], dwe_out.at[me], device(y, x, cc, zz))
            )
    expert_kept = net.keep(we_pieces.at[me], dwe_out.at[me])
    for _ in weights_job:
        pass
    weights_job = scatter_second(net, pos, GROUP_W, w_a, w_second[0], w_b, w_second[1], w_rows)
    next(weights_job)
    for d in (1, 2, 3):
        net.arrived(to_z + d, n_land.at[d])
    normed_grad = n_part[z].astype(F32)
    for d in (1, 2, 3):
        normed_grad = normed_grad + n_land[d].astype(F32)
    rows = tok[z].astype(F32)
    scale = lax.rsqrt(jnp.mean(rows * rows, axis=-1, keepdims=True) + epsilon)
    unit = rows * scale
    dn = normed_grad * gain_attn
    norm_grad[...] = scale * (
        dn - unit * jnp.mean(dn * unit, axis=-1, keepdims=True)
    )
    for _ in weights_job:
        pass
    w_pieces[...] = spread_rows(w_rows[...], 4)
    kept = net.keep(w_pieces.at[z], dwq_out.at[z])
    pieces = [
        net.put(w_pieces.at[lax.rem(z + d, 4)], dwq_out.at[z], device(y, x, c, z + d))
        for d in (1, 3, 2)
    ]
    expert_kept.wait()
    for copy in expert_pieces:
        copy.wait_recv()
    kept.wait()
    for copy in pieces:
        copy.wait_recv()
    for d in (1, 2, 3):
        net.left(to_z + d, n_land.at[d])
    net.finish()


def closing(dq, dkv, o, hg, tok, wq, gains, small, we_a, we_b):
    return pl.pallas_call(
        close_kernel,
        name="closing",
        out_shape=(
            jax.ShapeDtypeStruct((ROWS, D), F32),
            jax.ShapeDtypeStruct((4, 16, GQ), BF),
            jax.ShapeDtypeStruct((8, 16, WE), BF),
        ),
        in_specs=[VM] * 3 + [ANY] * 3 + [VM] * 2 + [ANY] * 2,
        out_specs=(VM, ANY, ANY),
        scratch_shapes=[
            pltpu.VMEM((4, ROWS, D), BF),
            pltpu.VMEM((4, ROWS, D), BF),
            pltpu.VMEM((4, 4, 2, 48, WQ), BF),
            pltpu.VMEM((4, 96, 1024), BF),
            pltpu.VMEM((4, 96, WE - 1024), BF),
            pltpu.VMEM((4, ROWS, GROUP_W), BF),
            pltpu.VMEM((4, ROWS, D), BF),
            pltpu.VMEM((4, ROWS, D), BF),
            pltpu.VMEM((4, ROWS, D), BF),
            pltpu.VMEM((4, 4, 2, 48, GQ), BF),
            pltpu.VMEM((4, 4, 48, GQ), BF),
            pltpu.VMEM((4, 4, 48, GQ), BF),
        ]
        + first_scratch(48, GQ, GROUP_W)
        + second_scratch(48, GQ, GROUP_W)
        + second_scratch(96, WE, 1024)
        + [
            pltpu.VMEM((4, 48, GROUP_W), BF),
            pltpu.VMEM((4, 48, GQ - GROUP_W), BF),
            pltpu.VMEM((48, GQ), BF),
            pltpu.VMEM((4, 16, GQ), BF),
            pltpu.VMEM((96, WE), BF),
            pltpu.VMEM((8, 16, WE), BF),
        ]
        + sems(48, 12),
        compiler_params=pltpu.CompilerParams(
            collective_id=8, has_side_effects=True, vmem_limit_bytes=VMEM_LIMIT
        ),
    )(dq, dkv, o, hg, tok, wq, gains, small, we_a, we_b)


def row_pad():
    at = lax.broadcasted_iota(jnp.int32, (16, 12), 0)
    return jnp.where(at == lax.broadcasted_iota(jnp.int32, (16, 12), 1), 1.0, 0.0)


def lane_pick(rows, lane):
    return jnp.where(lax.broadcasted_iota(jnp.int32, (rows, SMALL), 1) == lane, 1.0, 0.0)


def pack_kernel(
    qkv, out_w, router, gain_mlp, gain_attn, gate_up, down, shared_up, shared_down, ids,
    wq, wo, we, used,
):
    pad = row_pad()
    low = pad.astype(BF)

    def padded(value):
        return jnp.dot(low, value.astype(BF), preferred_element_type=F32).astype(BF)

    same = lane_equal(EXPERTS)
    wide = lax.dot_general(router[...].astype(BF), same, COL_COL, preferred_element_type=F32)
    small = jnp.dot(low, wide.astype(BF), preferred_element_type=F32)
    for lane, gain in ((EXPERTS, gain_mlp), (EXPERTS + 1, gain_attn)):
        small = small + jnp.dot(
            (pad * gain[...]).astype(BF),
            lane_pick(12, lane).astype(BF),
            preferred_element_type=F32,
        )
    for g in range(HK):
        wq[g, :, :GROUP_W] = padded(qkv[:, g * GROUP_W : (g + 1) * GROUP_W])
        wq[g, :, GROUP_W:] = small.astype(BF)
    wo[...] = padded(out_w[...])
    for e in range(EXPERTS):
        share = slice(e * FSL, (e + 1) * FSL)
        we[e, :, :FE] = padded(gate_up[:, e, :FE])
        we[e, :, FE:UP] = padded(shared_up[:, share])
        we[e, :, UP : UP + FE] = padded(gate_up[:, e, FE:])
        we[e, :, UP + FE : 2 * UP] = padded(shared_up[:, FS + e * FSL : FS + (e + 1) * FSL])
        we[e, :, 2 * UP : 2 * UP + FE] = padded(down[:, e, :])
        we[e, :, 2 * UP + FE :] = padded(shared_down[:, share])
    expert = lax.broadcasted_iota(jnp.int32, (EXPERTS, ROWS), 0)
    named = expert == ids[0:1, :]
    for k in range(1, 6):
        named = named | (expert == ids[k : k + 1, :])
    used[...] = lax.dot_general(
        jnp.where(named, 1.0, 0.0).astype(BF), same, COL_COL, preferred_element_type=F32
    )


def lane_equal(rows):
    at = lax.broadcasted_iota(jnp.int32, (rows, SMALL), 0)
    return jnp.where(at == lax.broadcasted_iota(jnp.int32, (rows, SMALL), 1), 1.0, 0.0).astype(BF)


def packing(*shards):
    return pl.pallas_call(
        pack_kernel,
        name="pack_shards",
        out_shape=(
            jax.ShapeDtypeStruct((4, 16, WQ), BF),
            jax.ShapeDtypeStruct((16, D), BF),
            jax.ShapeDtypeStruct((8, 16, WE), BF),
            jax.ShapeDtypeStruct((ROWS, SMALL), F32),
        ),
        in_specs=[VM] * 10,
        out_specs=(VM,) * 4,
        compiler_params=pltpu.CompilerParams(vmem_limit_bytes=VMEM_LIMIT),
    )(*shards)


def unpack_kernel(
    dwq, dwe, hidden, out_sum, hidden_grad, norm_grad,
    output, tokens_grad, gain_attn, qkv, out_w, gain_mlp, router, gate_up, down, shared_up,
    shared_down,
):
    output[...] = (hidden[...] + out_sum[...]).astype(BF)
    tokens_grad[...] = hidden_grad[...] + norm_grad[...]
    total = jnp.zeros((16, 16), F32)
    pick = lane_equal(16)
    for g in range(HK):
        qkv[:, g * GROUP_W : (g + 1) * GROUP_W] = dwq[g, :, :GROUP_W].astype(F32)[:12]
        out_w[:, g * QW : (g + 1) * QW] = dwq[g, :, GROUP_W : GROUP_W + QW].astype(F32)[:12]
        total = total + lax.dot_general(
            pick, dwq[g, :, GROUP_W + QW :], ROW_ROW, preferred_element_type=F32
        )
    router[...] = total[:EXPERTS, :12]
    gain_mlp[...] = total[EXPERTS : EXPERTS + 1, :12]
    gain_attn[...] = total[EXPERTS + 1 : EXPERTS + 2, :12]
    for e in range(EXPERTS):
        share = slice(e * FSL, (e + 1) * FSL)
        gate_up[:, e, :FE] = dwe[e, :, :FE].astype(F32)[:12]
        gate_up[:, e, FE:] = dwe[e, :, UP : UP + FE].astype(F32)[:12]
        shared_up[:, share] = dwe[e, :, FE:UP].astype(F32)[:12]
        shared_up[:, FS + e * FSL : FS + (e + 1) * FSL] = (
            dwe[e, :, UP + FE : 2 * UP].astype(F32)[:12]
        )
        down[:, e, :] = dwe[e, :, 2 * UP : 2 * UP + FE].astype(F32)[:12]
        shared_down[:, share] = dwe[e, :, 2 * UP + FE :].astype(F32)[:12]


def unpacking(*values):
    return pl.pallas_call(
        unpack_kernel,
        name="unpack_shards",
        out_shape=(
            jax.ShapeDtypeStruct((ROWS, D), BF),
            jax.ShapeDtypeStruct((ROWS, D), F32),
            jax.ShapeDtypeStruct((1, 12), F32),
            jax.ShapeDtypeStruct((12, QKV), F32),
            jax.ShapeDtypeStruct((12, D), F32),
            jax.ShapeDtypeStruct((1, 12), F32),
            jax.ShapeDtypeStruct((EXPERTS, 12), F32),
            jax.ShapeDtypeStruct((12, EXPERTS, 2 * FE), F32),
            jax.ShapeDtypeStruct((12, EXPERTS, FE), F32),
            jax.ShapeDtypeStruct((12, 2 * FS), F32),
            jax.ShapeDtypeStruct((12, FS), F32),
        ),
        in_specs=[VM] * 6,
        out_specs=(VM,) * 11,
        compiler_params=pltpu.CompilerParams(vmem_limit_bytes=VMEM_LIMIT),
    )(*values)


def per_device(
    tokens,
    seq_bounds,
    expert_ids,
    attn_gain,
    qkv_weight,
    out_weight,
    mlp_gain,
    router_weight,
    expert_gate_up,
    expert_down,
    shared_gate_up,
    shared_down,
    out_cotangent,
):
    wq_pieces, wo_piece, we_pieces, used = packing(
        qkv_weight,
        out_weight.T,
        router_weight.T,
        mlp_gain[None],
        attn_gain[None],
        jnp.transpose(expert_gate_up, (1, 0, 2)),
        jnp.transpose(expert_down, (2, 0, 1)),
        shared_gate_up,
        shared_down.T,
        expert_ids.T,
    )
    fwd = forward(seq_bounds, tokens, wq_pieces, wo_piece, we_pieces, out_cotangent, used)
    dkv_own, dq_all, attn_all, we_a, we_b, hidden_group, out_sum = backward(
        seq_bounds,
        *(fwd[k] for k in ("q", "o", "do", "lse", "kv", "dwe", "hidden_low", "out_parts")),
    )
    norm_grad, dwq_pieces, dwe_pieces = closing(
        dq_all,
        dkv_own,
        attn_all,
        hidden_group,
        *(fwd[k] for k in ("tok", "wq", "gains", "small")),
        we_a,
        we_b,
    )
    (
        output, tokens_grad, attn_gain_out, qkv_out, wo_out, mlp_gain_out, router_out,
        gate_up_out, down_out, shared_out, shared_down_out,
    ) = unpacking(
        dwq_pieces, dwe_pieces, fwd["hidden"], out_sum, fwd["hidden_grad"], norm_grad
    )
    return (
        output,
        tokens_grad,
        attn_gain_out.reshape(12),
        qkv_out,
        wo_out.T,
        mlp_gain_out.reshape(12),
        router_out.T,
        jnp.transpose(gate_up_out, (1, 0, 2)),
        jnp.transpose(down_out, (1, 2, 0)),
        shared_out,
        shared_down_out.T,
    )


def solution(mesh):
    both = ("blk", "head")
    in_specs = (
        P(both, None),
        P(),
        P(both, None),
        P(both),
        P(both, None),
        P(None, both),
        P(both),
        P(both, None),
        P(None, both, None),
        P(None, None, both),
        P(both, None),
        P(None, both),
        P(both, None),
    )
    out_specs = (
        P(both, None),
        P(both, None),
        P(both),
        P(both, None),
        P(None, both),
        P(both),
        P(both, None),
        P(None, both, None),
        P(None, None, both),
        P(both, None),
        P(None, both),
    )
    return jax.shard_map(
        per_device, mesh=mesh, in_specs=in_specs, out_specs=out_specs, check_vma=False
    )
```

```python
import functools

import jax
import jax.numpy as jnp
from jax import lax
from jax.experimental import pallas as pl
from jax.experimental.pallas import tpu as pltpu
from jax.sharding import PartitionSpec as P

D = 1536
HQ = 12
HK = 4
HD = 128
FE = 512
FS = 1024
EXPERTS = 8
QPG = 3
GROUP_W = 640
QKV = 2560
ROWS = 128
BLK = 512
HALF = 256
QW = 384
SMALL = 128
WQ = GROUP_W + SMALL
GQ = GROUP_W + QW + SMALL
PAIR = QPG * HALF
LANES = {(0, 1): slice(0, 2 * PAIR), (0,): slice(0, PAIR), (1,): slice(PAIR, 2 * PAIR)}


def head_lanes(ids):
    lanes = LANES[ids]
    return [slice(k, k + HALF) for k in range(lanes.start, lanes.stop, HALF)]


def pair_places(chunk, keys, queries):
    row = lax.broadcasted_iota(jnp.int32, (keys, queries), 0)
    return chunk * HALF + row + jnp.where(row >= HALF, HALF, 0)


def pair_cases(chunk, lo, hi):
    other = chunk + 2
    full_lo, full_hi, out_lo, out_hi = other < lo, other < hi, chunk > lo, chunk > hi
    plain = (chunk > 1) & (other < 2 * NBLK - 2) & (full_lo | out_lo) & (full_hi | out_hi)
    none = out_lo & out_hi
    return (
        plain & full_lo & full_hi,
        plain & full_lo & out_hi,
        plain & out_lo & full_hi,
        jnp.logical_not(plain) & jnp.logical_not(none),
        none,
    )

FSL = FS // 8
UP = FE + FSL
WE = 3 * UP
NBLK = 32
MESH = pl.DeviceIdType.MESH
BF = jnp.bfloat16
F32 = jnp.float32
epsilon = 1e-05
LOW = -1e30
LOG2E = 1.4426950408889634
SCALE = HD**-0.5
VMEM_LIMIT = 60 * 1024 * 1024

ANY = pl.BlockSpec(memory_space=pl.ANY)
VM = pl.BlockSpec(memory_space=pltpu.VMEM)


def position():
    b = lax.axis_index("blk")
    z = lax.axis_index("head")
    return b // 8, lax.rem(b // 2, 4), lax.rem(b, 2), z


def device(y, x, c, z):
    return ((lax.rem(y, 4) * 4 + lax.rem(x, 4)) * 2 + lax.rem(c, 2), lax.rem(z, 4))


def mirror(pos):
    y, x, c, z = pos
    return 3 - y, 3 - x, 1 - c, z


def greet(targets):
    barrier = pltpu.get_barrier_semaphore()
    for target in targets:
        pl.semaphore_signal(barrier, inc=1, device_id=target, device_id_type=MESH)
    pl.semaphore_wait(barrier, len(targets))


def z_peers(pos):
    y, x, c, z = pos
    return [device(y, x, c, z + d) for d in (1, 2, 3)]


def xy_peers(pos):
    y, x, c, z = pos
    return [device(y, x + d, c, z) for d in (1, 2, 3)] + [
        device(y + d, x, c, z) for d in (1, 2, 3)
    ]


def sibling(pos):
    y, x, c, z = pos
    return device(y, x, c + 1, z)


def other_column(pos):
    y, x, c, z = pos
    return [device(y, x, c + 1, z + d) for d in (0, 1, 2, 3)]


class Net:
    def __init__(self, send_sems, recv_sems, local_sems):
        self.send_sems, self.recv_sems, self.local_sems = send_sems, recv_sems, local_sems
        self.count = 0
        self.locals = 0
        self.started = []

    def put(self, src, dst, target):
        k = self.count
        self.count += 1
        copy = pltpu.make_async_remote_copy(
            src_ref=src,
            dst_ref=dst,
            send_sem=self.send_sems.at[k],
            recv_sem=self.recv_sems.at[k],
            device_id=target,
            device_id_type=MESH,
        )
        copy.start()
        self.started.append(copy)
        return copy

    def reserve(self, count):
        k = self.count
        self.count += count
        return k

    def put_at(self, k, src, dst, target):
        copy = self.copy_at(k, src, dst, target)
        copy.start()

    def copy_at(self, k, src, dst, target):
        return pltpu.make_async_remote_copy(
            src_ref=src,
            dst_ref=dst,
            send_sem=self.send_sems.at[k],
            recv_sem=self.recv_sems.at[k],
            device_id=target,
            device_id_type=MESH,
        )

    def arrived(self, k, ref):
        pltpu.make_async_copy(ref, ref, self.recv_sems.at[k]).wait()

    def left(self, k, ref):
        pltpu.make_async_copy(ref, ref, self.send_sems.at[k]).wait()

    def keep(self, src, dst):
        k = self.locals
        self.locals += 1
        copy = pltpu.make_async_copy(src, dst, self.local_sems.at[k])
        copy.start()
        return copy

    def finish(self):
        for copy in self.started:
            copy.wait_send()


def sems(remote, local):
    return [
        pltpu.SemaphoreType.DMA((remote,)),
        pltpu.SemaphoreType.DMA((remote,)),
        pltpu.SemaphoreType.DMA((local,)),
    ]


def run_jobs(jobs):
    live = list(jobs)
    while live:
        still = []
        for job in live:
            try:
                next(job)
                still.append(job)
            except StopIteration:
                pass
        live = still


def all_of(start, length):
    return pl.ds(start, length)


def gather_xy(net, land, own, cut, pos, with_core):
    y, x, c, z = pos
    width = own.shape[-1]
    first, second = pl.ds(0, cut), pl.ds(cut, width - cut)

    def place(yy, xx, columns):
        if with_core:
            return land.at[yy, xx, c, :, columns]
        return land.at[yy, xx, :, columns]

    whole = slice(None)
    mine = land.at[y, x, c] if with_core else land.at[y, x]
    kept = net.keep(own, mine)
    along_x = [
        net.put(own.at[:, first], place(y, x, first), device(y, x + d, c, z)) for d in (1, 3, 2)
    ]
    along_y = [
        net.put(own.at[:, second], place(y, x, second), device(y + d, x, c, z)) for d in (1, 3, 2)
    ]
    yield
    kept.wait()
    for copy in along_x:
        copy.wait_recv()
    row = place(y, whole, first)
    then_y = [net.put(row, row, device(y + d, x, c, z)) for d in (1, 3)]
    passed = []
    if with_core:
        passed.append(net.put(row, row, sibling(pos)))
    for copy in along_y:
        copy.wait_recv()
    column = place(whole, x, second)
    then_x = [net.put(column, column, device(y, x + d, c, z)) for d in (1, 3)]
    if with_core:
        passed.append(net.put(column, column, sibling(pos)))
    yield
    relays = []
    for d, half in ((1, pl.ds(0, 2)), (3, pl.ds(2, 2))):
        yy, xx = lax.rem(y + 4 - d, 4), lax.rem(x + 4 - d, 4)
        then_y[d // 2].wait_recv()
        part = place(yy, half, first)
        relays.append(net.put(part, part, device(y + d, x, c, z)))
        then_x[d // 2].wait_recv()
        part = place(half, xx, second)
        relays.append(net.put(part, part, device(y, x + d, c, z)))
        if with_core:
            for got in (place(yy, whole, first), place(whole, xx, second)):
                passed.append(net.put(got, got, sibling(pos)))
    yield
    for copy in relays:
        copy.wait_recv()
    if with_core:
        yy, xx = lax.rem(y + 2, 4), lax.rem(x + 2, 4)
        for got in (place(yy, whole, first), place(whole, xx, second)):
            passed.append(net.put(got, got, sibling(pos)))
    yield
    for copy in passed:
        copy.wait_recv()


def pick_rows(groups):
    rows = lax.broadcasted_iota(jnp.int32, (12 * groups, 16 * groups), 0)
    cols = lax.broadcasted_iota(jnp.int32, (12 * groups, 16 * groups), 1)
    piece = cols // 16
    within = cols - piece * 16
    return jnp.where((rows == piece * 12 + within) & (within < 12), 1.0, 0.0).astype(BF)


def squeeze_rows(pieces, groups):
    flat = pieces.reshape(groups * 16, pieces.shape[-1])
    return jnp.dot(pick_rows(groups), flat, preferred_element_type=F32).astype(BF)


def spread_rows(rows, groups):
    wide = lax.dot_general(
        pick_rows(groups), rows, (((0,), (0,)), ((), ())), preferred_element_type=F32
    )
    return wide.astype(BF).reshape(groups, 16, rows.shape[-1])


def mult(value, of):
    return pl.multiple_of(value, of)


def transposed(value):
    return jnp.transpose(value.astype(F32), (1, 0)).astype(BF)


SM = pl.BlockSpec(memory_space=pltpu.SMEM)


def home_block(pos, z):
    y, x, c, _ = pos
    b = (y * 4 + x) * 2 + c
    return jnp.where(z < 2, b, NBLK - 1 - b)


RW = D + SMALL
FLOOR = -1e29
ROW_ROW = (((1,), (1,)), ((), ()))
COL_COL = (((0,), (0,)), ((), ()))
EXP_SCALE = SCALE * LOG2E


def exchange_heads(to_tokens, pos, src_at, dst_at, ss, rs):
    y, x, c, z = pos
    b = (y * 4 + x) * 2 + c

    def ends(k):
        target = (home_block(pos, k if to_tokens else z), k)
        return src_at(k), dst_at(z), target, (target[0] == b) & (k == z)

    def remote(k):
        part, slot, target, _ = ends(k)
        return pltpu.make_async_remote_copy(
            src_ref=part,
            dst_ref=slot,
            send_sem=ss.at[k],
            recv_sem=rs.at[z],
            device_id=target,
            device_id_type=MESH,
        )

    def start(k):
        part, slot, _, stays = ends(k)

        @pl.when(stays)
        def _():
            pltpu.make_async_copy(part, slot, rs.at[z]).start()

        @pl.when(jnp.logical_not(stays))
        def _():
            remote(k).start()

    def wait():
        for k in range(4):
            pltpu.make_async_copy(dst_at(k), dst_at(k), rs.at[k]).wait()
        for k in range(4):

            @pl.when(jnp.logical_not(ends(k)[3]))
            def _():
                remote(k).wait_send()

    return start, wait


def query_places(bounds, lo, hi):
    lane = lax.broadcasted_iota(jnp.int32, (1, 2 * PAIR), 1)
    at = jnp.where(lane < PAIR, lo, hi) * HALF + lax.rem(lane, HALF)
    first = jnp.where(at >= bounds[1], bounds[1], jnp.where(at >= bounds[0], bounds[0], 0))
    return at, first


def turn(n):
    return jnp.where(n == 2, 3, jnp.where(n == 3, 2, n))


def forward_kernel(
    bounds, tok, wq, wo, we, gy, used,
    wo_out, wq_out, kv_out, q_out, o_out, lse_out, tok_out,
    hidden_out, hidden_grad_out, hidden_low_out, gains_out, small_out, do_out, out_parts, dwe_out,
    wq_z, wq_slab, wq_land, wo_z, wo_slab, wo_land, we_z, we_slab, we_land, tok_all, kv_land, q_in,
    qt, m_ref, l_ref, acc, mixed, own_rows, rows_all, gy_all, inner_all, pre_all, parts, out_stage,
    core_land, both, z_land, dwe_stage, mixed_grad, do_in, ss, rs, ls, hs, hr, gs, gr, hs2, hr2,
):
    pos = position()
    y, x, c, z = pos
    b = (y * 4 + x) * 2 + c
    my, mx, mc, _ = mirror(pos)
    greet(
        z_peers(pos)
        + xy_peers(pos)
        + [device(my, mx, mc, d) for d in range(4)]
        + other_column(pos)
    )
    net = Net(ss, rs, ls)

    wq_pieces = [
        net.put(wq.at[lax.rem(z + d, 4)], wq_z.at[z], device(y, x, c, z + d)) for d in (1, 3, 2)
    ]
    wq_kept = net.keep(wq.at[z], wq_z.at[z])

    def out_weights():
        pieces = [net.put(wo, wo_z.at[z], device(y, x, c, z + d)) for d in (1, 3, 2)]
        kept = net.keep(wo, wo_z.at[z])
        yield
        kept.wait()
        for copy in pieces:
            copy.wait_recv()
        wo_slab[...] = squeeze_rows(wo_z[...], 4)
        yield from gather_xy(net, wo_land, wo_slab, D // 2, pos, True)

    def expert_weights():
        me = c * 4 + z
        pieces = []
        for dc in (0, 1):
            for d in (0, 1, 3, 2):
                if (dc, d) == (0, 0):
                    continue
                cc, zz = lax.rem(c + dc, 2), lax.rem(z + d, 4)
                pieces.append(net.put(we.at[cc * 4 + zz], we_z.at[me], device(y, x, cc, zz)))
        kept = net.keep(we.at[me], we_z.at[me])
        yield
        kept.wait()
        for copy in pieces:
            copy.wait_recv()
        we_slab[...] = squeeze_rows(we_z[...], 8)
        yield from gather_xy(net, we_land, we_slab, 1024, pos, False)

    def cotangent():
        mine = gy_all.at[z, c]
        kept = net.keep(gy, mine)
        copies = [(d, net.put(gy, mine, device(y, x, c, z + d))) for d in (1, 3, 2)]
        passed = [net.put(gy, mine, sibling(pos))]
        yield
        for d, copy in copies:
            copy.wait_recv()
            got = gy_all.at[lax.rem(z + 4 - d, 4), c]
            passed.append(net.put(got, got, sibling(pos)))
        yield
        kept.wait()
        for copy in passed:
            copy.wait_recv()

    def pump(job):
        try:
            next(job)
        except StopIteration:
            pass

    wo_job, we_job, gy_job = out_weights(), expert_weights(), cotangent()
    pump(wo_job)
    tok_copies = [net.put(tok, tok_all.at[z], device(y, x, c, z + d)) for d in (1, 3, 2)]
    tok_kept = net.keep(tok, tok_all.at[z])
    pump(we_job)
    pump(gy_job)

    wq_kept.wait()
    for copy in wq_pieces:
        copy.wait_recv()
    wq_slab[...] = squeeze_rows(wq_z[...], 4)
    wq_job = gather_xy(net, wq_land, wq_slab, QW, pos, True)
    pump(wq_job)
    pump(wo_job)
    pump(wq_job)
    pump(wo_job)
    pump(wq_job)
    pump(wq_job)
    pump(wq_job)
    wq_saved = net.keep(wq_land, wq_out)

    for i in range(4):
        part = wq_land[i, :, :, :, GROUP_W:].reshape(QW, SMALL)
        one_hot = (
            lax.broadcasted_iota(jnp.int32, (16, SMALL), 0)
            == lax.broadcasted_iota(jnp.int32, (16, SMALL), 1)
        ).astype(BF)
        gains_out[:, i * QW : (i + 1) * QW] = lax.dot_general(
            one_hot, part, (((1,), (1,)), ((), ())), preferred_element_type=F32
        )
    tok_kept.wait()
    for copy in tok_copies:
        copy.wait_recv()
    tok_saved = net.keep(tok_all, tok_out)
    gain_attn = gains_out[EXPERTS + 1 : EXPERTS + 2, :]

    def normalise(i, carried):
        rows = tok_all[i].astype(F32)
        unit = rows * lax.rsqrt(jnp.mean(rows * rows, axis=-1, keepdims=True) + epsilon)
        out_stage[i // 2, lax.rem(i, 2)] = (unit * gain_attn).astype(BF)
        return carried

    lax.fori_loop(0, 4, normalise, 0)
    joined = jnp.dot(
        out_stage[...].reshape(BLK, D),
        wq_land[...].reshape(D, WQ)[:, :GROUP_W],
        preferred_element_type=F32,
    ).astype(BF)
    for half in range(2):
        rows = joined[half * HALF : (half + 1) * HALF]
        q_out[half] = rows[:, :QW]
        kv_land[y, x, c, half] = rows[:, QW:]

    swapped = net.put(q_out.at[1], q_in, device(my, mx, mc, z))
    whole = slice(None)
    along_x, along_y = [], []
    even, odd = kv_land.at[y, x, c, 0], kv_land.at[y, x, c, 1]
    for d in (1, 3, 2):
        along_x.append(net.put(even, even, device(y, x + d, c, z)))
        along_y.append(net.put(odd, odd, device(y + d, x, c, z)))
    m_ref[...] = jnp.full_like(m_ref, FLOOR)
    l_ref[...] = jnp.zeros_like(l_ref)
    acc[...] = jnp.zeros_like(acc)
    lo, hi = 2 * b, 2 * (NBLK - b) - 1
    at, first = query_places(bounds, lo, hi)
    for copy in along_x:
        copy.wait_recv()
    row = kv_land.at[y, whole, c, 0]
    from_y, crossed_y, crossed_x = net.reserve(4), net.reserve(4), net.reserve(4)
    for d in (1, 3):
        net.put_at(from_y + d, row, row, device(y + d, x, c, z))
    net.put_at(crossed_y, row, row, sibling(pos))
    for copy in along_y:
        copy.wait_recv()
    column = kv_land.at[whole, x, c, 1]
    from_x = net.reserve(4)
    for d in (1, 3):
        net.put_at(from_x + d, column, column, device(y, x + d, c, z))
    relay_y, relay_x = net.reserve(4), net.reserve(4)
    net.put_at(crossed_x, column, column, sibling(pos))
    pump(wo_job)
    pump(wo_job)
    swapped.wait_recv()
    for h in range(QPG):
        for i, rows in enumerate((q_out.at[0], q_in)):
            lanes = slice(i * PAIR + h * HALF, i * PAIR + (h + 1) * HALF)
            qt[:, lanes] = transposed(rows[:, h * HD : (h + 1) * HD])
    q_out[2] = q_in[...]

    def update(ids, block, chunk, masked):
        k_rows, v_rows = block[:, :HD], block[:, HD:]
        groups = head_lanes(ids)
        scores = [jnp.dot(k_rows, qt[:, g], preferred_element_type=F32) for g in groups]
        if masked:
            key_at = pair_places(chunk, block.shape[0], HALF)
            scores = [
                jnp.where((key_at >= first[:, g]) & (key_at <= at[:, g]), s, LOW)
                for g, s in zip(groups, scores)
            ]
        m_old = [m_ref[:, g] for g in groups]
        m_new = [jnp.maximum(m, jnp.max(s, axis=0, keepdims=True)) for m, s in zip(m_old, scores)]
        p = [jnp.exp2((s - m) * EXP_SCALE) for s, m in zip(scores, m_new)]
        alpha = [jnp.exp2((m - n) * EXP_SCALE) for m, n in zip(m_old, m_new)]
        pv = [
            lax.dot_general(v_rows, w.astype(BF), COL_COL, preferred_element_type=F32) for w in p
        ]
        sums = [jnp.sum(w, axis=0, keepdims=True) for w in p]
        for n, g in enumerate(groups):
            m_ref[:, g] = m_new[n]
            l_ref[:, g] = l_ref[:, g] * alpha[n] + sums[n]
            acc[:, g] = acc[:, g] * alpha[n] + pv[n]

    late = 2 * NBLK - 2

    def pair_step(yy, xx, half):
        chunk = (yy * 4 + xx) * 4 + half
        cases = pair_cases(chunk, lo, hi)
        early = chunk + 2 < late

        def go(ids, masked):
            update(ids, kv_land[yy, xx, :, half].reshape(2 * HALF, 2 * HD), chunk, masked)

        for case, ids, masked in zip(
            cases[:4], ((0, 1), (0,), (1,), (0, 1)), (False, False, False, True)
        ):

            @pl.when(case & early)
            def _():
                go(ids, masked)

    def stage(n, carried):
        d = turn(n)
        yy, xx = lax.rem(y + 4 - d, 4), lax.rem(x + 4 - d, 4)
        net.arrived(crossed_y + d, kv_land.at[yy, whole, 1 - c, 0])
        net.arrived(crossed_x + d, kv_land.at[whole, xx, 1 - c, 1])

        def step(t, carried):
            half = t // 4
            pair_step(jnp.where(half == 0, yy, t - 4), jnp.where(half == 0, t, xx), half)
            return carried

        lax.fori_loop(0, 8, step, 0)
        return carried

    lax.fori_loop(0, 1, stage, 0)
    for e in (1, 3):
        near_y, near_x = lax.rem(y + 4 - e, 4), lax.rem(x + 4 - e, 4)
        part = pl.ds(e - 1, 2)
        net.arrived(from_y + e, row)
        line = kv_land.at[near_y, part, c, 0]
        net.put_at(relay_y + e, line, line, device(y + e, x, c, z))
        net.arrived(from_x + e, column)
        line = kv_land.at[part, near_x, c, 1]
        net.put_at(relay_x + e, line, line, device(y, x + e, c, z))
    for e in (1, 3):
        near_y, near_x = lax.rem(y + 4 - e, 4), lax.rem(x + 4 - e, 4)
        line = kv_land.at[near_y, whole, c, 0]
        net.put_at(crossed_y + e, line, line, sibling(pos))
        line = kv_land.at[whole, near_x, c, 1]
        net.put_at(crossed_x + e, line, line, sibling(pos))
    pump(we_job)
    lax.fori_loop(1, 2, stage, 0)
    pump(we_job)
    far_y, far_x = lax.rem(y + 2, 4), lax.rem(x + 2, 4)
    for e in (1, 3):
        part = pl.ds(e - 1, 2)
        net.arrived(relay_y + e, kv_land.at[far_y, part, c, 0])
        net.arrived(relay_x + e, kv_land.at[part, far_x, c, 1])
    line = kv_land.at[far_y, whole, c, 0]
    net.put_at(crossed_y + 2, line, line, sibling(pos))
    line = kv_land.at[whole, far_x, c, 1]
    net.put_at(crossed_x + 2, line, line, sibling(pos))
    lax.fori_loop(2, 4, stage, 0)
    for n in range(4):
        for k in (crossed_y, crossed_x):
            net.left(k + n, row)
    for n in (1, 3):
        net.left(from_y + n, row)
        net.left(from_x + n, column)
        net.left(relay_y + n, kv_land.at[y, pl.ds(0, 2), c, 0])
        net.left(relay_x + n, kv_land.at[pl.ds(0, 2), x, c, 1])
    kv_saved = net.keep(kv_land, kv_out)

    def last_chunk(i, chunk_at):
        block = kv_land[3, 3, chunk_at // 2, lax.rem(chunk_at, 2)]
        update((i,), block, late - 2 + chunk_at, True)

    for i, chunk in enumerate((lo, hi)):

        @pl.when(chunk >= late - 2)
        def _():
            lax.fori_loop(0, 2, lambda n, _: last_chunk(i, n), None)

        @pl.when(chunk >= late)
        def _():
            lanes = LANES[(i,)]
            third = at[:, lanes] >= bounds[1]
            m_ref[:, lanes] = jnp.where(third, FLOOR, m_ref[:, lanes])
            l_ref[:, lanes] = jnp.where(third, 0.0, l_ref[:, lanes])
            acc[:, lanes] = jnp.where(third, 0.0, acc[:, lanes])
            lax.fori_loop(2, 4, lambda n, _: last_chunk(i, n), None)

    start, wait_mixed = exchange_heads(
        True, pos, lambda k: o_out.at[k], lambda g: mixed.at[:, pl.ds(mult(g * QW, QW), QW)], hs, hr
    )
    for i in range(2):
        for h in range(QPG):
            lanes = slice(i * PAIR + h * HALF, i * PAIR + (h + 1) * HALF)
            total = l_ref[:, lanes]
            lse_out[:, lanes] = m_ref[:, lanes] * EXP_SCALE + jnp.log(total) * LOG2E
            value = jnp.transpose(acc[:, lanes] / total, (1, 0)).astype(BF)
            o_out[2 * i, :, h * HD : (h + 1) * HD] = value[:ROWS]
            o_out[2 * i + 1, :, h * HD : (h + 1) * HD] = value[ROWS:]
        start(2 * i)
        start(2 * i + 1)

    pump(wo_job)
    pump(wo_job)
    wo_saved = net.keep(wo_land, wo_out)
    wait_mixed()
    pump(we_job)

    def add_hidden(i, carried):
        columns = pl.ds(mult(i * QW, QW), QW)
        hidden_out[:, columns] = tok[:, columns].astype(F32) + lax.dot_general(
            mixed[...], wo_land[i].reshape(QW, D), ROW_ROW, preferred_element_type=F32
        )
        return carried

    lax.fori_loop(0, 4, add_hidden, 0)
    hidden = hidden_out[...]
    unit = hidden * lax.rsqrt(jnp.mean(hidden * hidden, axis=-1, keepdims=True) + epsilon)
    low = (unit * gains_out[EXPERTS : EXPERTS + 1, :]).astype(BF)
    own_rows[:, :D] = low
    small_weights = wq_land[:, :, :, :, GROUP_W:].reshape(D, SMALL)
    logits = jnp.dot(low, small_weights, preferred_element_type=F32)
    is_used = used[...] > 0.0
    top = jnp.max(jnp.where(is_used, logits, LOW), axis=-1, keepdims=True)
    raised = jnp.where(is_used, jnp.exp(logits - top), 0.0)
    route = raised / jnp.sum(raised, axis=-1, keepdims=True)
    coarse = route.astype(BF).astype(F32)
    own_rows[:, D:] = (coarse + pltpu.roll(route - coarse, EXPERTS, 1)).astype(BF)

    mine = rows_all.at[z, c]
    rows_kept = net.keep(own_rows, mine)
    from_z, crossed_z = net.reserve(4), net.reserve(4)
    relay_z = net.reserve(4)
    for d in (1, 3):
        net.put_at(from_z + d, own_rows, mine, device(y, x, c, z + d))
    net.put_at(crossed_z, own_rows, mine, sibling(pos))
    for job in (gy_job, we_job, wo_job, wq_job):
        for _ in job:
            pass
    rows_kept.wait()
    to_core, to_z = net.reserve(4), net.reserve(4)
    me = c * 4 + z
    gate_columns, up_columns, down_columns = (slice(i * UP, (i + 1) * UP) for i in range(3))

    def weights(columns):
        return we_land[:, :, :, columns].reshape(D, UP)

    def finish_block(n):
        d, slot = turn(n), lax.rem(n, 2)
        zz = lax.rem(z + 4 - d, 4)
        net.arrived(to_core + n, core_land.at[n])
        both[n] = (parts[slot, c].astype(F32) + core_land[n].astype(F32)).astype(BF)
        net.left(to_core + n, parts.at[slot, 1 - c])

        @pl.when(n > 0)
        def _():
            net.put_at(to_z + d, both.at[n], z_land.at[d], device(y, x, c, zz))

    def expert_block(n, carried):
        d, slot = turn(n), lax.rem(n, 2)
        zz = lax.rem(z + 4 - d, 4)
        got = rows_all.at[zz, c]

        @pl.when(n == 1)
        def _():
            for e in (1, 3):
                near = rows_all.at[lax.rem(z + 4 - e, 4), c]
                net.arrived(from_z + e, near)
                part = near.at[pl.ds((e - 1) * 32, 64)]
                net.put_at(relay_z + e, part, part, device(y, x, c, z + e))
                net.put_at(crossed_z + e, near, near, sibling(pos))

        @pl.when(n == 3)
        def _():
            for e in (1, 3):
                net.arrived(relay_z + e, got.at[pl.ds((e - 1) * 32, 64)])
            net.put_at(crossed_z + 2, got, got, sibling(pos))

        net.arrived(crossed_z + d, rows_all.at[zz, 1 - c])

        @pl.when(n > 1)
        def _():
            pltpu.make_async_copy(out_stage.at[slot], out_stage.at[slot], gs.at[slot]).wait()

        rows = rows_all[zz].reshape(2 * ROWS, RW)
        x_rows, lanes = rows[:, :D], rows[:, D:].astype(F32)
        lane = lax.broadcasted_iota(jnp.int32, lanes.shape, 1)
        route = jnp.sum(
            jnp.where((lane == me) | (lane == me + EXPERTS), lanes, 0.0), axis=-1, keepdims=True
        )
        gy_rows = gy_all[zz].reshape(2 * ROWS, D)
        gate = jnp.dot(x_rows, weights(gate_columns), preferred_element_type=F32)
        up = jnp.dot(x_rows, weights(up_columns), preferred_element_type=F32)
        raw = jnp.dot(gy_rows, weights(down_columns), preferred_element_type=F32)
        unit_lane = lax.broadcasted_iota(jnp.int32, gate.shape, 1)
        share = jnp.where(unit_lane < FE, route, 1.0)
        sig = 1.0 / (1.0 + jnp.exp(-gate))
        silu = gate * sig
        inner = silu * up
        scaled = (inner * share).astype(BF)
        inner_all[zz] = scaled
        route_grad = jnp.sum(inner[:, :FE] * raw[:, :FE], axis=-1, keepdims=True)
        inner_grad = raw * share
        pre_grad = jnp.concatenate(
            [inner_grad * up * (sig + silu * (1.0 - sig)), inner_grad * silu], axis=-1
        ).astype(BF)
        pre_all[zz] = pre_grad
        out_stage[slot] = (
            lax.dot_general(scaled, weights(down_columns), ROW_ROW, preferred_element_type=F32)
            .astype(BF)
            .reshape(2, ROWS, D)
        )
        pltpu.make_async_copy(out_stage.at[slot], out_parts.at[zz], gs.at[slot]).start()
        rows_grad = lax.dot_general(
            pre_grad[:, :UP], weights(gate_columns), ROW_ROW, preferred_element_type=F32
        ) + lax.dot_general(
            pre_grad[:, UP:], weights(up_columns), ROW_ROW, preferred_element_type=F32
        )
        parts[slot, :, :, :D] = rows_grad.astype(BF).reshape(2, ROWS, D)
        high = route_grad.astype(BF).astype(F32)
        parts[slot, :, :, D:] = (
            jnp.where(lane == me, high, 0.0) + jnp.where(lane == me + EXPERTS, route_grad - high, 0.0)
        ).astype(BF).reshape(2, ROWS, SMALL)
        net.put_at(to_core + n, parts.at[slot, 1 - c], core_land.at[n], sibling(pos))

        @pl.when(n > 0)
        def _():
            finish_block(n - 1)

        return carried

    lax.fori_loop(0, 4, expert_block, 0)
    finish_block(3)
    for slot in range(2):
        pltpu.make_async_copy(out_stage.at[slot], out_stage.at[slot], gs.at[slot]).wait()

    def weight_grads(t, carried):
        slot = lax.rem(t, 2)

        @pl.when(t > 1)
        def _():
            pltpu.make_async_copy(dwe_stage.at[slot], dwe_stage.at[slot], gr.at[slot]).wait()

        columns = pl.ds(mult(t * QW, QW), QW)
        for i in range(3):
            value = jnp.zeros((QW, UP), F32)
            for k in range(4):
                left = (rows_all if i < 2 else gy_all)[k, :, :, columns].reshape(2 * ROWS, QW)
                right = pre_all[k, :, i * UP : (i + 1) * UP] if i < 2 else inner_all[k]
                value = value + lax.dot_general(left, right, COL_COL, preferred_element_type=F32)
            dwe_stage[slot, :, :, i * UP : (i + 1) * UP] = value.astype(BF).reshape(4, 96, UP)
        pltpu.make_async_copy(dwe_stage.at[slot], dwe_out.at[t], gr.at[slot]).start()
        return carried

    lax.fori_loop(0, 4, weight_grads, 0)

    for d in (1, 2, 3):
        net.arrived(to_z + d, z_land.at[d])

    def total(columns):
        value = both[0, :, columns].astype(F32)
        for d in (1, 2, 3):
            value = value + z_land[d, :, columns].astype(F32)
        return value

    lane = lax.broadcasted_iota(jnp.int32, (ROWS, SMALL), 1)
    route_grads = total(slice(D, RW))
    route_grads = route_grads + pltpu.roll(route_grads, SMALL - EXPERTS, 1)
    logits_grad = (
        route * (route_grads - jnp.sum(route * route_grads, axis=-1, keepdims=True))
    ).astype(BF)
    normed_grad = total(slice(0, D)) + lax.dot_general(
        logits_grad, small_weights, ROW_ROW, preferred_element_type=F32
    )
    hidden = hidden_out[...]
    scale = lax.rsqrt(jnp.mean(hidden * hidden, axis=-1, keepdims=True) + epsilon)
    unit = hidden * scale
    dn = normed_grad * gains_out[EXPERTS : EXPERTS + 1, :]
    hidden_grad = gy_all[z, c].astype(F32) + scale * (
        dn - unit * jnp.mean(dn * unit, axis=-1, keepdims=True)
    )
    hidden_grad_out[...] = hidden_grad
    hidden_low = hidden_grad.astype(BF)
    hidden_low_out[...] = hidden_low
    total_grad = jnp.zeros((ROWS, D), F32)
    for i in range(4):
        total_grad = total_grad + jnp.dot(
            hidden_low[:, i * QW : (i + 1) * QW],
            wo_land[i].reshape(QW, D),
            preferred_element_type=F32,
        )
    start, wait_heads = exchange_heads(
        False, pos, lambda g: mixed_grad.at[g], lambda k: do_in.at[k], hs2, hr2
    )
    for g in range(4):
        mixed_grad[g] = total_grad[:, g * QW : (g + 1) * QW].astype(BF)
        start(g)
    gain_column = jnp.where(lane == EXPERTS, 1.0, 0.0).astype(BF)
    small_out[...] = (
        lax.dot_general(own_rows[:, :D], logits_grad, COL_COL, preferred_element_type=F32)
        + lax.dot_general(
            (normed_grad * unit).astype(BF), gain_column, COL_COL, preferred_element_type=F32
        )
    ).astype(BF)
    for n in range(4):
        net.left(crossed_z + n, own_rows)
        if n:
            net.left(to_z + n, both.at[n])
    for n in (1, 3):
        net.left(from_z + n, own_rows)
        net.left(relay_z + n, own_rows.at[pl.ds(0, 64)])
    for slot in range(2):
        pltpu.make_async_copy(dwe_stage.at[slot], dwe_stage.at[slot], gr.at[slot]).wait()
    wait_heads()
    do_out[...] = do_in[...]
    for copy in (wq_saved, tok_saved, kv_saved, wo_saved):
        copy.wait()
    net.finish()


def forward(bounds, tok, wq, wo, we, gy, used):
    outs = {
        "wo": ((4, 4, 2, 48, D), BF, ANY),
        "wq": ((4, 4, 2, 48, WQ), BF, ANY),
        "kv": ((4, 4, 2, 2, HALF, 2 * HD), BF, ANY),
        "q": ((3, HALF, QW), BF, VM),
        "o": ((4, ROWS, QW), BF, VM),
        "lse": ((1, 2 * PAIR), F32, VM),
        "tok": ((4, ROWS, D), BF, ANY),
        "hidden": ((ROWS, D), F32, VM),
        "hidden_grad": ((ROWS, D), F32, VM),
        "hidden_low": ((ROWS, D), BF, VM),
        "gains": ((16, D), F32, VM),
        "small": ((D, SMALL), BF, VM),
        "do": ((4, ROWS, QW), BF, VM),
        "out_parts": ((4, 2, ROWS, D), BF, ANY),
        "dwe": ((4, 4, 96, WE), BF, ANY),
    }
    values = pl.pallas_call(
        forward_kernel,
        name="forward",
        out_shape=tuple(jax.ShapeDtypeStruct(s, t) for s, t, _ in outs.values()),
        in_specs=[SM, VM, ANY, ANY, ANY, ANY, VM],
        out_specs=tuple(m for _, _, m in outs.values()),
        scratch_shapes=[
            pltpu.VMEM((4, 16, WQ), BF),
            pltpu.VMEM((48, WQ), BF),
            pltpu.VMEM((4, 4, 2, 48, WQ), BF),
            pltpu.VMEM((4, 16, D), BF),
            pltpu.VMEM((48, D), BF),
            pltpu.VMEM((4, 4, 2, 48, D), BF),
            pltpu.VMEM((8, 16, WE), BF),
            pltpu.VMEM((96, WE), BF),
            pltpu.VMEM((4, 4, 96, WE), BF),
            pltpu.VMEM((4, ROWS, D), BF),
            pltpu.VMEM((4, 4, 2, 2, HALF, 2 * HD), BF),
            pltpu.VMEM((HALF, QW), BF),
            pltpu.VMEM((HD, 2 * PAIR), BF),
            pltpu.VMEM((1, 2 * PAIR), F32),
            pltpu.VMEM((1, 2 * PAIR), F32),
            pltpu.VMEM((HD, 2 * PAIR), F32),
            pltpu.VMEM((ROWS, D), BF),
            pltpu.VMEM((ROWS, RW), BF),
            pltpu.VMEM((4, 2, ROWS, RW), BF),
            pltpu.VMEM((4, 2, ROWS, D), BF),
            pltpu.VMEM((4, 2 * ROWS, UP), BF),
            pltpu.VMEM((4, 2 * ROWS, 2 * UP), BF),
            pltpu.VMEM((2, 2, ROWS, RW), BF),
            pltpu.VMEM((2, 2, ROWS, D), BF),
            pltpu.VMEM((4, ROWS, RW), BF),
            pltpu.VMEM((4, ROWS, RW), BF),
            pltpu.VMEM((4, ROWS, RW), BF),
            pltpu.VMEM((2, 4, 96, WE), BF),
            pltpu.VMEM((4, ROWS, QW), BF),
            pltpu.VMEM((4, ROWS, QW), BF),
        ]
        + sems(144, 32)
        + [pltpu.SemaphoreType.DMA((4,))] * 6,
        compiler_params=pltpu.CompilerParams(
            collective_id=1, has_side_effects=True, vmem_limit_bytes=VMEM_LIMIT
        ),
    )(bounds, tok, wq, wo, we, gy, used)
    return dict(zip(outs, values))


def add_into(dst, left, right, rows):
    step = 32

    def body(i, carried):
        place = pl.ds(mult(i * step, step), step)
        dst[place, :] = (left[place, :].astype(F32) + right[place, :].astype(F32)).astype(
            dst.dtype
        )
        return carried

    lax.fori_loop(0, rows // step, body, 0)


def add_four(dst, parts, rows, step):
    def body(i, carried):
        place = pl.ds(mult(i * step, step), step)
        total = parts[0][place, :].astype(F32)
        for part in parts[1:]:
            total = total + part[place, :].astype(F32)
        dst[place, :] = total.astype(dst.dtype)
        return carried

    lax.fori_loop(0, rows // step, body, 0)


def sum_group(net, parts, pos, core_land, own, both, z_land, out):
    y, x, c, z = pos
    order = (0, 1, 3, 2)
    crossing, kept = [], []
    for d in order:
        zz = lax.rem(z + d, 4)
        crossing.append(net.put(parts.at[zz, 1 - c], core_land.at[zz], sibling(pos)))
        kept.append(net.keep(parts.at[zz, c], own.at[zz]))
    yield
    arriving = []
    for n, d in enumerate(order):
        zz = lax.rem(z + d, 4)
        crossing[n].wait_recv()
        kept[n].wait()
        add_into(both.at[zz], own.at[zz], core_land.at[zz], ROWS)
        if d:
            arriving.append(net.put(both.at[zz], z_land.at[d - 1], device(y, x, c, zz)))
    yield
    for copy in arriving:
        copy.wait_recv()
    add_four(out, [both.at[z]] + [z_land.at[d] for d in range(3)], ROWS, 32)


def group_scratch(width):
    return [
        pltpu.VMEM((4, ROWS, width), BF),
        pltpu.VMEM((4, ROWS, width), BF),
        pltpu.VMEM((4, ROWS, width), BF),
        pltpu.VMEM((3, ROWS, width), BF),
    ]


def fold_parts(own, land, total, rows):
    step = 16

    def body(i, carried):
        q = i // (rows // step)
        place = pl.ds(mult(lax.rem(i, rows // step) * step, step), step)
        value = own[q, place, :].astype(F32)
        for d in range(3):
            value = value + land[d, q, place, :].astype(F32)
        total[q, place, :] = value.astype(BF)
        return carried

    lax.fori_loop(0, 4 * (rows // step), body, 0)


def scatter_first(net, src, pos, cut, a_own, a_land, b_own, b_land, a_sum, b_sum):
    y, x, c, z = pos
    rows, width = src.shape[2], src.shape[3]
    first, second = pl.ds(0, cut), pl.ds(cut, width - cut)
    whole = slice(None)
    keep_a = net.keep(src.at[whole, x, whole, first], a_own)
    keep_b = net.keep(src.at[y, whole, whole, second], b_own)
    to_x, to_y = [], []
    for d in (1, 3, 2):
        xx, yy = lax.rem(x + d, 4), lax.rem(y + d, 4)
        to_x.append(
            net.put(src.at[whole, xx, whole, first], a_land.at[d - 1], device(y, xx, c, z))
        )
        to_y.append(
            net.put(src.at[yy, whole, whole, second], b_land.at[d - 1], device(yy, x, c, z))
        )
    yield
    keep_a.wait()
    for copy in to_x:
        copy.wait_recv()
    fold_parts(a_own, a_land, a_sum, rows)
    keep_b.wait()
    for copy in to_y:
        copy.wait_recv()
    fold_parts(b_own, b_land, b_sum, rows)


def scatter_second(net, pos, cut, a_sum, a_last, b_sum, b_last, out):
    y, x, c, z = pos
    rows, width = out.shape
    last_y, last_x = [], []
    for d in (1, 3, 2):
        yy, xx = lax.rem(y + d, 4), lax.rem(x + d, 4)
        last_y.append(net.put(a_sum.at[yy], a_last.at[d - 1], device(yy, x, c, z)))
        last_x.append(net.put(b_sum.at[xx], b_last.at[d - 1], device(y, xx, c, z)))
    yield
    for copy in last_y:
        copy.wait_recv()
    for copy in last_x:
        copy.wait_recv()
    step = 16
    first, second = slice(0, cut), slice(cut, width)

    def final(i, carried):
        place = pl.ds(mult(i * step, step), step)
        for at, own, last, columns in ((y, a_sum, a_last, first), (x, b_sum, b_last, second)):
            value = own[at, place, :].astype(F32)
            for d in range(3):
                value = value + last[d, place, :].astype(F32)
            out[place, columns] = value.astype(BF)
        return carried

    lax.fori_loop(0, rows // step, final, 0)


def first_scratch(rows, width, cut):
    shapes = []
    for w in (cut, width - cut):
        shapes += [pltpu.VMEM((4, rows, w), BF), pltpu.VMEM((3, 4, rows, w), BF)]
    return shapes


def second_scratch(rows, width, cut):
    return [pltpu.VMEM((3, rows, cut), BF), pltpu.VMEM((3, rows, width - cut), BF)]


def backward_kernel(
    bounds, q, o, do, lse, kv_in, dwe, hg, out_parts,
    dkv_out, dq_out, o_out, we_a, we_b, hg_all, out_sum,
    kv, o_in, dq_own, dq_in, q_rows, do_rows, qt, dot_t, delta, late_lse, dqt, part, core_land, both, a_land, b_land,
    a_sum, b_sum, a_last, b_last, *scratch,
):
    we_s = scratch[:4]
    group_s = scratch[4:8]
    ss, rs, ls = scratch[8:]
    pos = position()
    y, x, c, z = pos
    b = (y * 4 + x) * 2 + c
    net = Net(ss, rs, ls)
    kv_kept = net.keep(kv_in, kv)
    greet(z_peers(pos) + xy_peers(pos) + [device(*mirror(pos))] + other_column(pos))
    o_swap = net.put(o.at[pl.ds(2, 2)], o_in, device(*mirror(pos)))
    whole = slice(None)

    def experts():
        yield from scatter_first(net, dwe, pos, 1024, *we_s, we_a, we_b)

    def rows_of_group():
        mine = hg_all.at[z]
        kept = net.keep(hg, mine)
        copies = [net.put(hg, mine, device(y, x, c, z + d)) for d in (1, 3, 2)]
        yield
        kept.wait()
        for copy in copies:
            copy.wait_recv()

    def pump(job):
        try:
            next(job)
        except StopIteration:
            pass

    we_job = experts()
    out_job = sum_group(net, out_parts, pos, *group_s, out_sum)
    hg_job = rows_of_group()
    pump(out_job)
    pump(we_job)
    pump(hg_job)

    lo, hi = 2 * b, 2 * (NBLK - b) - 1
    at, first = query_places(bounds, lo, hi)
    for i in range(2):
        for h in range(QPG):
            columns = slice(h * HD, (h + 1) * HD)
            lanes = slice(i * PAIR + h * HALF, i * PAIR + (h + 1) * HALF)
            q_rows[lanes, :] = q[2 * i, :, columns]
            qt[:, lanes] = transposed(q[2 * i, :, columns])
            rows = do[2 * i : 2 * i + 2, :, columns].reshape(HALF, HD)
            do_rows[lanes, :] = rows
            do_t = jnp.transpose(rows.astype(F32), (1, 0))
            o_t = jnp.transpose(
                o[2 * i : 2 * i + 2, :, columns].reshape(HALF, HD).astype(F32), (1, 0)
            )
            dot_t[:, lanes] = do_t.astype(BF)
            delta[:, lanes] = jnp.sum(do_t * o_t, axis=0, keepdims=True)
    late_lse[...] = jnp.where(at >= bounds[1], -LOW, lse[...])
    dqt[...] = jnp.zeros_like(dqt)
    kv_kept.wait()
    pump(out_job)

    def pairs(ids, yy, xx, half, slot, chunk, masked):
        block = kv[yy, xx, :, half].reshape(2 * HALF, 2 * HD)
        k_rows, v_rows = block[:, :HD], block[:, HD:]
        groups = head_lanes(ids)
        scores = [jnp.dot(k_rows, qt[:, g], preferred_element_type=F32) for g in groups]
        dp = [jnp.dot(v_rows, dot_t[:, g], preferred_element_type=F32) for g in groups]
        if masked:
            key_at = pair_places(chunk, 2 * HALF, HALF)
            p = [
                jnp.where(
                    (key_at >= first[:, g]) & (key_at <= at[:, g]),
                    jnp.exp2(s * EXP_SCALE - lse[:, g]),
                    0.0,
                )
                for g, s in zip(groups, scores)
            ]
        else:
            p = [jnp.exp2(s * EXP_SCALE - late_lse[:, g]) for g, s in zip(groups, scores)]
        ds = [(w * (t - delta[:, g])).astype(BF) for g, w, t in zip(groups, p, dp)]
        dv = jnp.zeros((2 * HALF, HD), F32)
        dk = jnp.zeros((2 * HALF, HD), F32)
        for g, w, t in zip(groups, p, ds):
            dv = dv + jnp.dot(w.astype(BF), do_rows[g, :], preferred_element_type=F32)
            dk = dk + jnp.dot(t, q_rows[g, :], preferred_element_type=F32)
        dq = [lax.dot_general(k_rows, t, COL_COL, preferred_element_type=F32) for t in ds]
        for g, t in zip(groups, dq):
            dqt[:, g] += t
        part[slot, :, half, :, :HD] = (dk * SCALE).astype(BF).reshape(2, HALF, HD)
        part[slot, :, half, :, HD:] = dv.astype(BF).reshape(2, HALF, HD)

    def pair_step(yy, xx, half, slot):
        chunk = (yy * 4 + xx) * 4 + half
        cases = pair_cases(chunk, lo, hi)
        for case, ids, masked in zip(
            cases[:4], ((0, 1), (0,), (1,), (0, 1)), (False, False, False, True)
        ):

            @pl.when(case)
            def _():
                pairs(ids, yy, xx, half, slot, chunk, masked)

        @pl.when(cases[4])
        def _():
            part[slot, :, half] = jnp.zeros((2, HALF, 2 * HD), BF)

    def chip(t):
        dy = jnp.where(
            t < 4,
            t,
            jnp.where(
                t < 7,
                1,
                jnp.where(
                    t < 10,
                    jnp.where(t == 7, 0, t - 6),
                    jnp.where(
                        t < 12, 3, jnp.where(t < 14, 2 * (t - 12), 2 * (15 - t))
                    ),
                ),
            ),
        )
        dx = jnp.where(
            t < 4,
            1,
            jnp.where(
                t < 7,
                jnp.where(t == 4, 0, t - 3),
                jnp.where(
                    t < 10,
                    3,
                    jnp.where(t < 12, 2 * (t - 10), jnp.where(t < 14, 2, 0)),
                ),
            ),
        )
        return lax.rem(y + dy, 4), lax.rem(x + dx, 4)

    to_core, to_x, to_y = net.reserve(16), net.reserve(4), net.reserve(4)

    def fold_chip(t):
        yy, xx = chip(t)
        slot = lax.rem(t, 2)
        net.arrived(to_core + t, core_land.at[yy, xx])
        both[yy, xx] = (part[slot, c].astype(F32) + core_land[yy, xx].astype(F32)).astype(BF)
        net.left(to_core + t, part.at[slot, 1 - c])

    def send_lines(d):
        xx, yy = lax.rem(x + d, 4), lax.rem(y + d, 4)
        net.put_at(to_x + d, both.at[whole, xx, 0], a_land.at[d], device(y, xx, c, z))
        net.put_at(to_y + d, both.at[yy, whole, 1], b_land.at[d], device(yy, x, c, z))

    far_x, far_y = net.reserve(4), net.reserve(4)

    def send_far(odd):
        xx, yy = lax.rem(x + 2, 4), lax.rem(y + 2, 4)
        for e in (odd, odd + 2):
            ye, xe = lax.rem(y + e, 4), lax.rem(x + e, 4)
            net.put_at(far_x + e, both.at[ye, xx, 0], a_land.at[2, ye], device(y, xx, c, z))
            net.put_at(far_y + e, both.at[yy, xe, 1], b_land.at[2, xe], device(yy, x, c, z))

    def chip_step(t, carried):
        yy, xx = chip(t)
        slot = lax.rem(t, 2)

        def step(n, carried):
            pair_step(yy, xx, n, slot)
            return carried

        lax.fori_loop(0, 2, step, 0)
        net.put_at(to_core + t, part.at[slot, 1 - c], core_land.at[yy, xx], sibling(pos))

        @pl.when(t > 0)
        def _():
            fold_chip(t - 1)

        for at_chip, send in (
            (7, lambda: send_lines(1)),
            (12, lambda: (send_lines(3), send_far(1))),
            (15, lambda: send_far(0)),
        ):

            @pl.when(t == at_chip)
            def _():
                send()

        return carried

    lax.fori_loop(0, 16, chip_step, 0)
    for i in range(2):
        for h in range(QPG):
            lanes = slice(i * PAIR + h * HALF, i * PAIR + (h + 1) * HALF)
            dq_own[i, :, h * HD : (h + 1) * HD] = jnp.transpose(
                dqt[:, lanes] * SCALE, (1, 0)
            ).astype(BF)
    dq_swap = net.put(dq_own.at[1], dq_in, device(*mirror(pos)))
    lax.fori_loop(15, 16, lambda t, _: fold_chip(t), None)

    def fold_lines(own_at, land, total):
        def body(n, carried):
            q_at, place = n // 8, pl.ds(mult(lax.rem(n, 8) * 32, 32), 32)
            value = own_at(q_at, place).astype(F32)
            for d in (1, 2, 3):
                value = value + land[d, q_at, place, :].astype(F32)
            total[q_at, place, :] = value.astype(BF)
            return carried

        lax.fori_loop(0, 32, body, 0)

    for d in (1, 3):
        net.arrived(to_x + d, a_land.at[d])
    for e in range(4):
        net.arrived(far_x + e, a_land.at[2, e])
    fold_lines(lambda n, place: both[n, x, 0, place, :], a_land, a_sum)
    last_y = []
    for d in (1, 3, 2):
        yy = lax.rem(y + d, 4)
        last_y.append(net.put(a_sum.at[yy], a_last.at[d], device(yy, x, c, z)))
    for d in (1, 3):
        net.arrived(to_y + d, b_land.at[d])
    for e in range(4):
        net.arrived(far_y + e, b_land.at[2, e])
    fold_lines(lambda n, place: both[y, n, 1, place, :], b_land, b_sum)
    last_x = []
    for d in (1, 3, 2):
        xx = lax.rem(x + d, 4)
        last_x.append(net.put(b_sum.at[xx], b_last.at[d], device(y, xx, c, z)))
    pump(we_job)
    pump(out_job)
    o_swap.wait_recv()
    o_out[0] = o[0]
    o_out[1] = o[1]
    o_out[2] = o_in[0]
    o_out[3] = o_in[1]
    dq_swap.wait_recv()
    dq_out[0] = dq_own[0]
    dq_out[1] = dq_in[...]
    for copies, total, last, at, half in (
        (last_y, a_sum, a_last, y, 0),
        (last_x, b_sum, b_last, x, 1),
    ):
        for copy in copies:
            copy.wait_recv()
        value = total[at].astype(F32)
        for d in (1, 2, 3):
            value = value + last[d].astype(F32)
        dkv_out[half] = value.astype(BF)
    for job in (hg_job, out_job, we_job):
        for _ in job:
            pass
    for d in (1, 3):
        net.left(to_x + d, a_land.at[d])
        net.left(to_y + d, b_land.at[d])
    for e in range(4):
        net.left(far_x + e, a_land.at[2, e])
        net.left(far_y + e, b_land.at[2, e])
    net.finish()


def backward(bounds, q, o, do, lse, kv, dwe, hg, out_parts):
    return pl.pallas_call(
        backward_kernel,
        name="backward",
        out_shape=(
            jax.ShapeDtypeStruct((2, HALF, 2 * HD), BF),
            jax.ShapeDtypeStruct((2, HALF, QW), BF),
            jax.ShapeDtypeStruct((4, ROWS, QW), BF),
            jax.ShapeDtypeStruct((4, 96, 1024), BF),
            jax.ShapeDtypeStruct((4, 96, WE - 1024), BF),
            jax.ShapeDtypeStruct((4, ROWS, D), BF),
            jax.ShapeDtypeStruct((ROWS, D), F32),
        ),
        in_specs=[SM] + [VM] * 4 + [ANY] * 4,
        out_specs=(VM, VM, VM, VM, VM, ANY, VM),
        scratch_shapes=[
            pltpu.VMEM((4, 4, 2, 2, HALF, 2 * HD), BF),
            pltpu.VMEM((2, ROWS, QW), BF),
            pltpu.VMEM((2, HALF, QW), BF),
            pltpu.VMEM((HALF, QW), BF),
            pltpu.VMEM((2 * PAIR, HD), BF),
            pltpu.VMEM((2 * PAIR, HD), BF),
            pltpu.VMEM((HD, 2 * PAIR), BF),
            pltpu.VMEM((HD, 2 * PAIR), BF),
            pltpu.VMEM((1, 2 * PAIR), F32),
            pltpu.VMEM((1, 2 * PAIR), F32),
            pltpu.VMEM((HD, 2 * PAIR), F32),
            pltpu.VMEM((2, 2, 2, HALF, 2 * HD), BF),
            pltpu.VMEM((4, 4, 2, HALF, 2 * HD), BF),
            pltpu.VMEM((4, 4, 2, HALF, 2 * HD), BF),
            pltpu.VMEM((4, 4, HALF, 2 * HD), BF),
            pltpu.VMEM((4, 4, HALF, 2 * HD), BF),
            pltpu.VMEM((4, HALF, 2 * HD), BF),
            pltpu.VMEM((4, HALF, 2 * HD), BF),
            pltpu.VMEM((4, HALF, 2 * HD), BF),
            pltpu.VMEM((4, HALF, 2 * HD), BF),
        ]
        + first_scratch(96, WE, 1024)
        + group_scratch(D)
        + sems(72, 16),
        compiler_params=pltpu.CompilerParams(
            collective_id=7, has_side_effects=True, vmem_limit_bytes=VMEM_LIMIT
        ),
    )(bounds, q, o, do, lse, kv, dwe, hg, out_parts)


def close_kernel(
    dq, dkv, o, hg_in, tok_in, wq_in, gains, small, we_a_in, we_b_in,
    norm_grad, dwq_out, dwe_out, hg, tok, wq, we_a, we_b,
    joined, unit_all, n_part, n_land, dwq, w_land, w_both, *scratch,
):
    w_first, w_second, we_last = scratch[:4], scratch[4:6], scratch[6:8]
    w_a, w_b, w_rows, w_pieces, we_rows, we_pieces = scratch[8:14]
    ss, rs, ls = scratch[14:]
    pos = position()
    y, x, c, z = pos
    net = Net(ss, rs, ls)
    loads = [
        net.keep(src, dst)
        for src, dst in (
            (tok_in, tok), (hg_in, hg), (wq_in, wq), (we_a_in, we_a), (we_b_in, we_b)
        )
    ]
    greet(z_peers(pos) + xy_peers(pos) + other_column(pos))
    for copy in loads:
        copy.wait()
    experts_job = scatter_second(net, pos, 1024, we_a, we_last[0], we_b, we_last[1], we_rows)
    next(experts_job)
    joined[:, :, :QW] = dq[...].reshape(4, ROWS, QW)
    joined[:, :, QW:] = dkv[...].reshape(4, ROWS, 2 * HD)
    gain_attn = gains[EXPERTS + 1 : EXPERTS + 2, :]
    to_z, to_core = net.reserve(4), net.reserve(4)

    def normalise(k, carried):
        rows = tok[k].astype(F32)
        scale = lax.rsqrt(jnp.mean(rows * rows, axis=-1, keepdims=True) + epsilon)
        unit_all[k] = (rows * scale).astype(BF)
        return carried

    lax.fori_loop(0, 4, normalise, 0)

    def fold(t):
        net.arrived(to_core + t, w_land.at[t])

        def body(i, inner):
            xx, place = i // 3, pl.ds(mult(lax.rem(i, 3) * 16, 16), 16)
            w_both[t, xx, place, :] = (
                dwq[t, xx, c, place, :].astype(F32) + w_land[t, xx, place, :].astype(F32)
            ).astype(BF)
            return inner

        lax.fori_loop(0, 12, body, 0)
        net.left(to_core + t, w_land.at[t])

    def weight_grads(t, carried):
        columns = pl.ds(mult(t * QW, QW), QW)
        unit_grad = jnp.zeros((QW, GROUP_W), F32)
        wo_grad = jnp.zeros((QW, QW), F32)
        for k in range(4):
            unit_grad = unit_grad + lax.dot_general(
                unit_all[k, :, columns], joined[k], COL_COL, preferred_element_type=F32
            )
            wo_grad = wo_grad + lax.dot_general(
                hg[k, :, columns], o[k], COL_COL, preferred_element_type=F32
            )
        weights = wq[t].reshape(QW, WQ).astype(F32)
        lane = lax.broadcasted_iota(jnp.int32, (QW, SMALL), 1)
        here = lane == EXPERTS + 1
        small_weights = weights[:, GROUP_W:]
        gain = jnp.sum(jnp.where(here, small_weights, 0.0), axis=-1, keepdims=True)
        gain_grad = jnp.sum(unit_grad * weights[:, :GROUP_W], axis=-1, keepdims=True)
        small_grad = small[pl.ds(mult(t * QW, QW), QW), :].astype(F32)
        small_grad = jnp.where(here, gain_grad, small_grad)
        dwq[t, :, :, :, :GROUP_W] = (unit_grad * gain).astype(BF).reshape(4, 2, 48, GROUP_W)
        dwq[t, :, :, :, GROUP_W : GROUP_W + QW] = wo_grad.astype(BF).reshape(4, 2, 48, QW)
        dwq[t, :, :, :, GROUP_W + QW :] = small_grad.astype(BF).reshape(4, 2, 48, SMALL)
        net.put_at(to_core + t, dwq.at[t, :, 1 - c], w_land.at[t], sibling(pos))

        @pl.when(t > 0)
        def _():
            fold(t - 1)

        return carried

    lax.fori_loop(0, 4, weight_grads, 0)
    fold(3)
    weights_job = scatter_first(net, w_both, pos, GROUP_W, *w_first, w_a, w_b)
    next(weights_job)

    normed_grads = lax.dot_general(
        joined[...].reshape(BLK, GROUP_W),
        wq[...].reshape(D, WQ)[:, :GROUP_W],
        ROW_ROW,
        preferred_element_type=F32,
    )
    n_part[...] = normed_grads.astype(BF).reshape(4, ROWS, D)
    for d in (1, 3, 2):
        zz = lax.rem(z + d, 4)
        net.put_at(to_z + d, n_part.at[zz], n_land.at[d], device(y, x, c, zz))
    for _ in experts_job:
        pass
    we_pieces[...] = spread_rows(we_rows[...], 8)
    me = c * 4 + z
    expert_pieces = []
    for dc in (0, 1):
        for d in (0, 1, 3, 2):
            if (dc, d) == (0, 0):
                continue
            cc, zz = lax.rem(c + dc, 2), lax.rem(z + d, 4)
            expert_pieces.append(
                net.put(we_pieces.at[cc * 4 + zz], dwe_out.at[me], device(y, x, cc, zz))
            )
    expert_kept = net.keep(we_pieces.at[me], dwe_out.at[me])
    for _ in weights_job:
        pass
    weights_job = scatter_second(net, pos, GROUP_W, w_a, w_second[0], w_b, w_second[1], w_rows)
    next(weights_job)
    for d in (1, 2, 3):
        net.arrived(to_z + d, n_land.at[d])
    normed_grad = n_part[z].astype(F32)
    for d in (1, 2, 3):
        normed_grad = normed_grad + n_land[d].astype(F32)
    rows = tok[z].astype(F32)
    scale = lax.rsqrt(jnp.mean(rows * rows, axis=-1, keepdims=True) + epsilon)
    unit = rows * scale
    dn = normed_grad * gain_attn
    norm_grad[...] = scale * (
        dn - unit * jnp.mean(dn * unit, axis=-1, keepdims=True)
    )
    for _ in weights_job:
        pass
    w_pieces[...] = spread_rows(w_rows[...], 4)
    kept = net.keep(w_pieces.at[z], dwq_out.at[z])
    pieces = [
        net.put(w_pieces.at[lax.rem(z + d, 4)], dwq_out.at[z], device(y, x, c, z + d))
        for d in (1, 3, 2)
    ]
    expert_kept.wait()
    for copy in expert_pieces:
        copy.wait_recv()
    kept.wait()
    for copy in pieces:
        copy.wait_recv()
    for d in (1, 2, 3):
        net.left(to_z + d, n_land.at[d])
    net.finish()


def closing(dq, dkv, o, hg, tok, wq, gains, small, we_a, we_b):
    return pl.pallas_call(
        close_kernel,
        name="closing",
        out_shape=(
            jax.ShapeDtypeStruct((ROWS, D), F32),
            jax.ShapeDtypeStruct((4, 16, GQ), BF),
            jax.ShapeDtypeStruct((8, 16, WE), BF),
        ),
        in_specs=[VM] * 3 + [ANY] * 3 + [VM] * 2 + [ANY] * 2,
        out_specs=(VM, ANY, ANY),
        scratch_shapes=[
            pltpu.VMEM((4, ROWS, D), BF),
            pltpu.VMEM((4, ROWS, D), BF),
            pltpu.VMEM((4, 4, 2, 48, WQ), BF),
            pltpu.VMEM((4, 96, 1024), BF),
            pltpu.VMEM((4, 96, WE - 1024), BF),
            pltpu.VMEM((4, ROWS, GROUP_W), BF),
            pltpu.VMEM((4, ROWS, D), BF),
            pltpu.VMEM((4, ROWS, D), BF),
            pltpu.VMEM((4, ROWS, D), BF),
            pltpu.VMEM((4, 4, 2, 48, GQ), BF),
            pltpu.VMEM((4, 4, 48, GQ), BF),
            pltpu.VMEM((4, 4, 48, GQ), BF),
        ]
        + first_scratch(48, GQ, GROUP_W)
        + second_scratch(48, GQ, GROUP_W)
        + second_scratch(96, WE, 1024)
        + [
            pltpu.VMEM((4, 48, GROUP_W), BF),
            pltpu.VMEM((4, 48, GQ - GROUP_W), BF),
            pltpu.VMEM((48, GQ), BF),
            pltpu.VMEM((4, 16, GQ), BF),
            pltpu.VMEM((96, WE), BF),
            pltpu.VMEM((8, 16, WE), BF),
        ]
        + sems(48, 12),
        compiler_params=pltpu.CompilerParams(
            collective_id=8, has_side_effects=True, vmem_limit_bytes=VMEM_LIMIT
        ),
    )(dq, dkv, o, hg, tok, wq, gains, small, we_a, we_b)


def row_pad():
    at = lax.broadcasted_iota(jnp.int32, (16, 12), 0)
    return jnp.where(at == lax.broadcasted_iota(jnp.int32, (16, 12), 1), 1.0, 0.0)


def lane_pick(rows, lane):
    return jnp.where(lax.broadcasted_iota(jnp.int32, (rows, SMALL), 1) == lane, 1.0, 0.0)


def pack_kernel(
    qkv, out_w, router, gain_mlp, gain_attn, gate_up, down, shared_up, shared_down, ids,
    wq, wo, we, used,
):
    pad = row_pad()
    low = pad.astype(BF)

    def padded(value):
        return jnp.dot(low, value.astype(BF), preferred_element_type=F32).astype(BF)

    same = lane_equal(EXPERTS)
    wide = lax.dot_general(router[...].astype(BF), same, COL_COL, preferred_element_type=F32)
    small = jnp.dot(low, wide.astype(BF), preferred_element_type=F32)
    for lane, gain in ((EXPERTS, gain_mlp), (EXPERTS + 1, gain_attn)):
        small = small + jnp.dot(
            (pad * gain[...]).astype(BF),
            lane_pick(12, lane).astype(BF),
            preferred_element_type=F32,
        )
    for g in range(HK):
        wq[g, :, :GROUP_W] = padded(qkv[:, g * GROUP_W : (g + 1) * GROUP_W])
        wq[g, :, GROUP_W:] = small.astype(BF)
    wo[...] = padded(out_w[...])
    for e in range(EXPERTS):
        share = slice(e * FSL, (e + 1) * FSL)
        we[e, :, :FE] = padded(gate_up[:, e, :FE])
        we[e, :, FE:UP] = padded(shared_up[:, share])
        we[e, :, UP : UP + FE] = padded(gate_up[:, e, FE:])
        we[e, :, UP + FE : 2 * UP] = padded(shared_up[:, FS + e * FSL : FS + (e + 1) * FSL])
        we[e, :, 2 * UP : 2 * UP + FE] = padded(down[:, e, :])
        we[e, :, 2 * UP + FE :] = padded(shared_down[:, share])
    expert = lax.broadcasted_iota(jnp.int32, (EXPERTS, ROWS), 0)
    named = expert == ids[0:1, :]
    for k in range(1, 6):
        named = named | (expert == ids[k : k + 1, :])
    used[...] = lax.dot_general(
        jnp.where(named, 1.0, 0.0).astype(BF), same, COL_COL, preferred_element_type=F32
    )


def lane_equal(rows):
    at = lax.broadcasted_iota(jnp.int32, (rows, SMALL), 0)
    return jnp.where(at == lax.broadcasted_iota(jnp.int32, (rows, SMALL), 1), 1.0, 0.0).astype(BF)


def packing(*shards):
    return pl.pallas_call(
        pack_kernel,
        name="pack_shards",
        out_shape=(
            jax.ShapeDtypeStruct((4, 16, WQ), BF),
            jax.ShapeDtypeStruct((16, D), BF),
            jax.ShapeDtypeStruct((8, 16, WE), BF),
            jax.ShapeDtypeStruct((ROWS, SMALL), F32),
        ),
        in_specs=[VM] * 10,
        out_specs=(VM,) * 4,
        compiler_params=pltpu.CompilerParams(vmem_limit_bytes=VMEM_LIMIT),
    )(*shards)


def unpack_kernel(
    dwq, dwe, hidden, out_sum, hidden_grad, norm_grad,
    output, tokens_grad, gain_attn, qkv, out_w, gain_mlp, router, gate_up, down, shared_up,
    shared_down,
):
    output[...] = (hidden[...] + out_sum[...]).astype(BF)
    tokens_grad[...] = hidden_grad[...] + norm_grad[...]
    total = jnp.zeros((16, 16), F32)
    pick = lane_equal(16)
    for g in range(HK):
        qkv[:, g * GROUP_W : (g + 1) * GROUP_W] = dwq[g, :, :GROUP_W].astype(F32)[:12]
        out_w[:, g * QW : (g + 1) * QW] = dwq[g, :, GROUP_W : GROUP_W + QW].astype(F32)[:12]
        total = total + lax.dot_general(
            pick, dwq[g, :, GROUP_W + QW :], ROW_ROW, preferred_element_type=F32
        )
    router[...] = total[:EXPERTS, :12]
    gain_mlp[...] = total[EXPERTS : EXPERTS + 1, :12]
    gain_attn[...] = total[EXPERTS + 1 : EXPERTS + 2, :12]
    for e in range(EXPERTS):
        share = slice(e * FSL, (e + 1) * FSL)
        gate_up[:, e, :FE] = dwe[e, :, :FE].astype(F32)[:12]
        gate_up[:, e, FE:] = dwe[e, :, UP : UP + FE].astype(F32)[:12]
        shared_up[:, share] = dwe[e, :, FE:UP].astype(F32)[:12]
        shared_up[:, FS + e * FSL : FS + (e + 1) * FSL] = (
            dwe[e, :, UP + FE : 2 * UP].astype(F32)[:12]
        )
        down[:, e, :] = dwe[e, :, 2 * UP : 2 * UP + FE].astype(F32)[:12]
        shared_down[:, share] = dwe[e, :, 2 * UP + FE :].astype(F32)[:12]


def unpacking(*values):
    return pl.pallas_call(
        unpack_kernel,
        name="unpack_shards",
        out_shape=(
            jax.ShapeDtypeStruct((ROWS, D), BF),
            jax.ShapeDtypeStruct((ROWS, D), F32),
            jax.ShapeDtypeStruct((1, 12), F32),
            jax.ShapeDtypeStruct((12, QKV), F32),
            jax.ShapeDtypeStruct((12, D), F32),
            jax.ShapeDtypeStruct((1, 12), F32),
            jax.ShapeDtypeStruct((EXPERTS, 12), F32),
            jax.ShapeDtypeStruct((12, EXPERTS, 2 * FE), F32),
            jax.ShapeDtypeStruct((12, EXPERTS, FE), F32),
            jax.ShapeDtypeStruct((12, 2 * FS), F32),
            jax.ShapeDtypeStruct((12, FS), F32),
        ),
        in_specs=[VM] * 6,
        out_specs=(VM,) * 11,
        compiler_params=pltpu.CompilerParams(vmem_limit_bytes=VMEM_LIMIT),
    )(*values)


def per_device(
    tokens,
    seq_bounds,
    expert_ids,
    attn_gain,
    qkv_weight,
    out_weight,
    mlp_gain,
    router_weight,
    expert_gate_up,
    expert_down,
    shared_gate_up,
    shared_down,
    out_cotangent,
):
    wq_pieces, wo_piece, we_pieces, used = packing(
        qkv_weight,
        out_weight.T,
        router_weight.T,
        mlp_gain[None],
        attn_gain[None],
        jnp.transpose(expert_gate_up, (1, 0, 2)),
        jnp.transpose(expert_down, (2, 0, 1)),
        shared_gate_up,
        shared_down.T,
        expert_ids.T,
    )
    fwd = forward(seq_bounds, tokens, wq_pieces, wo_piece, we_pieces, out_cotangent, used)
    dkv_own, dq_all, attn_all, we_a, we_b, hidden_group, out_sum = backward(
        seq_bounds,
        *(fwd[k] for k in ("q", "o", "do", "lse", "kv", "dwe", "hidden_low", "out_parts")),
    )
    norm_grad, dwq_pieces, dwe_pieces = closing(
        dq_all,
        dkv_own,
        attn_all,
        hidden_group,
        *(fwd[k] for k in ("tok", "wq", "gains", "small")),
        we_a,
        we_b,
    )
    (
        output, tokens_grad, attn_gain_out, qkv_out, wo_out, mlp_gain_out, router_out,
        gate_up_out, down_out, shared_out, shared_down_out,
    ) = unpacking(
        dwq_pieces, dwe_pieces, fwd["hidden"], out_sum, fwd["hidden_grad"], norm_grad
    )
    return (
        output,
        tokens_grad,
        attn_gain_out.reshape(12),
        qkv_out,
        wo_out.T,
        mlp_gain_out.reshape(12),
        router_out.T,
        jnp.transpose(gate_up_out, (1, 0, 2)),
        jnp.transpose(down_out, (1, 2, 0)),
        shared_out,
        shared_down_out.T,
    )


def solution(mesh):
    both = ("blk", "head")
    in_specs = (
        P(both, None),
        P(),
        P(both, None),
        P(both),
        P(both, None),
        P(None, both),
        P(both),
        P(both, None),
        P(None, both, None),
        P(None, None, both),
        P(both, None),
        P(None, both),
        P(both, None),
    )
    out_specs = (
        P(both, None),
        P(both, None),
        P(both),
        P(both, None),
        P(None, both),
        P(both),
        P(both, None),
        P(None, both, None),
        P(None, None, both),
        P(both, None),
        P(None, both),
    )
    return jax.shard_map(
        per_device, mesh=mesh, in_specs=in_specs, out_specs=out_specs, check_vma=False
    )
```

```python
import functools

import jax
import jax.numpy as jnp
from jax import lax
from jax.experimental import pallas as pl
from jax.experimental.pallas import tpu as pltpu
from jax.sharding import PartitionSpec as P

D = 1536
HQ = 12
HK = 4
HD = 128
FE = 512
FS = 1024
EXPERTS = 8
QPG = 3
GROUP_W = 640
QKV = 2560
ROWS = 128
BLK = 512
HALF = 256
QW = 384
SMALL = 128
WQ = GROUP_W + SMALL
GQ = GROUP_W + QW + SMALL
PAIR = QPG * HALF
LANES = {(0, 1): slice(0, 2 * PAIR), (0,): slice(0, PAIR), (1,): slice(PAIR, 2 * PAIR)}


def head_lanes(ids):
    lanes = LANES[ids]
    return [slice(k, k + HALF) for k in range(lanes.start, lanes.stop, HALF)]


def pair_places(chunk, keys, queries):
    row = lax.broadcasted_iota(jnp.int32, (keys, queries), 0)
    return chunk * HALF + row + jnp.where(row >= HALF, HALF, 0)


def pair_cases(chunk, lo, hi):
    other = chunk + 2
    full_lo, full_hi, out_lo, out_hi = other < lo, other < hi, chunk > lo, chunk > hi
    plain = (chunk > 1) & (other < 2 * NBLK - 2) & (full_lo | out_lo) & (full_hi | out_hi)
    none = out_lo & out_hi
    return (
        plain & full_lo & full_hi,
        plain & full_lo & out_hi,
        plain & out_lo & full_hi,
        jnp.logical_not(plain) & jnp.logical_not(none),
        none,
    )

FSL = FS // 8
UP = FE + FSL
WE = 3 * UP
NBLK = 32
MESH = pl.DeviceIdType.MESH
BF = jnp.bfloat16
F32 = jnp.float32
epsilon = 1e-05
LOW = -1e30
LOG2E = 1.4426950408889634
SCALE = HD**-0.5
VMEM_LIMIT = 60 * 1024 * 1024

ANY = pl.BlockSpec(memory_space=pl.ANY)
VM = pl.BlockSpec(memory_space=pltpu.VMEM)


def position():
    b = lax.axis_index("blk")
    z = lax.axis_index("head")
    return b // 8, lax.rem(b // 2, 4), lax.rem(b, 2), z


def device(y, x, c, z):
    return ((lax.rem(y, 4) * 4 + lax.rem(x, 4)) * 2 + lax.rem(c, 2), lax.rem(z, 4))


def mirror(pos):
    y, x, c, z = pos
    return 3 - y, 3 - x, 1 - c, z


def announce(targets):
    barrier = pltpu.get_barrier_semaphore()
    for target in targets:
        pl.semaphore_signal(barrier, inc=1, device_id=target, device_id_type=MESH)
    return lambda: pl.semaphore_wait(barrier, len(targets))


def greet(targets):
    announce(targets)()


def z_peers(pos):
    y, x, c, z = pos
    return [device(y, x, c, z + d) for d in (1, 2, 3)]


def xy_peers(pos):
    y, x, c, z = pos
    return [device(y, x + d, c, z) for d in (1, 2, 3)] + [
        device(y + d, x, c, z) for d in (1, 2, 3)
    ]


def sibling(pos):
    y, x, c, z = pos
    return device(y, x, c + 1, z)


def other_column(pos):
    y, x, c, z = pos
    return [device(y, x, c + 1, z + d) for d in (0, 1, 2, 3)]


class Net:
    def __init__(self, send_sems, recv_sems, local_sems):
        self.send_sems, self.recv_sems, self.local_sems = send_sems, recv_sems, local_sems
        self.count = 0
        self.locals = 0
        self.started = []

    def put(self, src, dst, target):
        k = self.count
        self.count += 1
        copy = pltpu.make_async_remote_copy(
            src_ref=src,
            dst_ref=dst,
            send_sem=self.send_sems.at[k],
            recv_sem=self.recv_sems.at[k],
            device_id=target,
            device_id_type=MESH,
        )
        copy.start()
        self.started.append(copy)
        return copy

    def reserve(self, count):
        k = self.count
        self.count += count
        return k

    def put_at(self, k, src, dst, target):
        copy = self.copy_at(k, src, dst, target)
        copy.start()

    def copy_at(self, k, src, dst, target):
        return pltpu.make_async_remote_copy(
            src_ref=src,
            dst_ref=dst,
            send_sem=self.send_sems.at[k],
            recv_sem=self.recv_sems.at[k],
            device_id=target,
            device_id_type=MESH,
        )

    def arrived(self, k, ref):
        pltpu.make_async_copy(ref, ref, self.recv_sems.at[k]).wait()

    def left(self, k, ref):
        pltpu.make_async_copy(ref, ref, self.send_sems.at[k]).wait()

    def keep(self, src, dst):
        k = self.locals
        self.locals += 1
        copy = pltpu.make_async_copy(src, dst, self.local_sems.at[k])
        copy.start()
        return copy

    def finish(self):
        for copy in self.started:
            copy.wait_send()


def sems(remote, local):
    return [
        pltpu.SemaphoreType.DMA((remote,)),
        pltpu.SemaphoreType.DMA((remote,)),
        pltpu.SemaphoreType.DMA((local,)),
    ]


def run_jobs(jobs):
    live = list(jobs)
    while live:
        still = []
        for job in live:
            try:
                next(job)
                still.append(job)
            except StopIteration:
                pass
        live = still


def all_of(start, length):
    return pl.ds(start, length)


def gather_xy(net, land, own, cut, pos, with_core):
    y, x, c, z = pos
    width = own.shape[-1]
    first, second = pl.ds(0, cut), pl.ds(cut, width - cut)

    def place(yy, xx, columns):
        if with_core:
            return land.at[yy, xx, c, :, columns]
        return land.at[yy, xx, :, columns]

    whole = slice(None)
    mine = land.at[y, x, c] if with_core else land.at[y, x]
    kept = net.keep(own, mine)
    along_x = [
        net.put(own.at[:, first], place(y, x, first), device(y, x + d, c, z)) for d in (1, 3, 2)
    ]
    along_y = [
        net.put(own.at[:, second], place(y, x, second), device(y + d, x, c, z)) for d in (1, 3, 2)
    ]
    yield
    kept.wait()
    for copy in along_x:
        copy.wait_recv()
    row = place(y, whole, first)
    then_y = [net.put(row, row, device(y + d, x, c, z)) for d in (1, 3)]
    passed = []
    if with_core:
        passed.append(net.put(row, row, sibling(pos)))
    for copy in along_y:
        copy.wait_recv()
    column = place(whole, x, second)
    then_x = [net.put(column, column, device(y, x + d, c, z)) for d in (1, 3)]
    if with_core:
        passed.append(net.put(column, column, sibling(pos)))
    yield
    relays = []
    for d, half in ((1, pl.ds(0, 2)), (3, pl.ds(2, 2))):
        yy, xx = lax.rem(y + 4 - d, 4), lax.rem(x + 4 - d, 4)
        then_y[d // 2].wait_recv()
        part = place(yy, half, first)
        relays.append(net.put(part, part, device(y + d, x, c, z)))
        then_x[d // 2].wait_recv()
        part = place(half, xx, second)
        relays.append(net.put(part, part, device(y, x + d, c, z)))
        if with_core:
            for got in (place(yy, whole, first), place(whole, xx, second)):
                passed.append(net.put(got, got, sibling(pos)))
    yield
    for copy in relays:
        copy.wait_recv()
    if with_core:
        yy, xx = lax.rem(y + 2, 4), lax.rem(x + 2, 4)
        for got in (place(yy, whole, first), place(whole, xx, second)):
            passed.append(net.put(got, got, sibling(pos)))
    yield
    for copy in passed:
        copy.wait_recv()


def pick_rows(groups):
    rows = lax.broadcasted_iota(jnp.int32, (12 * groups, 16 * groups), 0)
    cols = lax.broadcasted_iota(jnp.int32, (12 * groups, 16 * groups), 1)
    piece = cols // 16
    within = cols - piece * 16
    return jnp.where((rows == piece * 12 + within) & (within < 12), 1.0, 0.0).astype(BF)


def squeeze_rows(pieces, groups):
    flat = pieces.reshape(groups * 16, pieces.shape[-1])
    return jnp.dot(pick_rows(groups), flat, preferred_element_type=F32).astype(BF)


def spread_rows(rows, groups):
    wide = lax.dot_general(
        pick_rows(groups), rows, (((0,), (0,)), ((), ())), preferred_element_type=F32
    )
    return wide.astype(BF).reshape(groups, 16, rows.shape[-1])


def mult(value, of):
    return pl.multiple_of(value, of)


def transposed(value):
    return jnp.transpose(value.astype(F32), (1, 0)).astype(BF)


SM = pl.BlockSpec(memory_space=pltpu.SMEM)


def home_block(pos, z):
    y, x, c, _ = pos
    b = (y * 4 + x) * 2 + c
    return jnp.where(z < 2, b, NBLK - 1 - b)


RW = D + SMALL
FLOOR = -1e29
ROW_ROW = (((1,), (1,)), ((), ()))
COL_COL = (((0,), (0,)), ((), ()))
EXP_SCALE = SCALE * LOG2E


def exchange_heads(to_tokens, pos, src_at, dst_at, ss, rs):
    y, x, c, z = pos
    b = (y * 4 + x) * 2 + c

    def ends(k):
        target = (home_block(pos, k if to_tokens else z), k)
        return src_at(k), dst_at(z), target, (target[0] == b) & (k == z)

    def remote(k):
        part, slot, target, _ = ends(k)
        return pltpu.make_async_remote_copy(
            src_ref=part,
            dst_ref=slot,
            send_sem=ss.at[k],
            recv_sem=rs.at[z],
            device_id=target,
            device_id_type=MESH,
        )

    def start(k):
        part, slot, _, stays = ends(k)

        @pl.when(stays)
        def _():
            pltpu.make_async_copy(part, slot, rs.at[z]).start()

        @pl.when(jnp.logical_not(stays))
        def _():
            remote(k).start()

    def wait():
        for k in range(4):
            pltpu.make_async_copy(dst_at(k), dst_at(k), rs.at[k]).wait()
        for k in range(4):

            @pl.when(jnp.logical_not(ends(k)[3]))
            def _():
                remote(k).wait_send()

    return start, wait


def query_places(bounds, lo, hi):
    lane = lax.broadcasted_iota(jnp.int32, (1, 2 * PAIR), 1)
    at = jnp.where(lane < PAIR, lo, hi) * HALF + lax.rem(lane, HALF)
    first = jnp.where(at >= bounds[1], bounds[1], jnp.where(at >= bounds[0], bounds[0], 0))
    return at, first


def turn(n):
    return jnp.where(n == 2, 3, jnp.where(n == 3, 2, n))


def forward_kernel(
    bounds, tok, wq, wo, we, gy, used,
    wo_out, wq_out, kv_out, q_out, o_out, lse_out, tok_out,
    hidden_out, hidden_grad_out, hidden_low_out, gains_out, small_out, do_out, out_parts, dwe_out,
    wq_z, wq_slab, wq_land, wo_z, wo_slab, wo_land, we_z, we_slab, we_land, tok_all, kv_land, q_in,
    qt, m_ref, l_ref, acc, mixed, own_rows, rows_all, gy_all, inner_all, pre_all, parts, out_stage,
    core_land, both, z_land, dwe_stage, mixed_grad, do_in, ss, rs, ls, hs, hr, gs, gr, hs2, hr2,
):
    pos = position()
    y, x, c, z = pos
    b = (y * 4 + x) * 2 + c
    my, mx, mc, _ = mirror(pos)
    greet(
        z_peers(pos)
        + xy_peers(pos)
        + [device(my, mx, mc, d) for d in range(4)]
        + other_column(pos)
    )
    net = Net(ss, rs, ls)

    wq_pieces = [
        net.put(wq.at[lax.rem(z + d, 4)], wq_z.at[z], device(y, x, c, z + d)) for d in (1, 3, 2)
    ]
    wq_kept = net.keep(wq.at[z], wq_z.at[z])

    def out_weights():
        pieces = [net.put(wo, wo_z.at[z], device(y, x, c, z + d)) for d in (1, 3, 2)]
        kept = net.keep(wo, wo_z.at[z])
        yield
        kept.wait()
        for copy in pieces:
            copy.wait_recv()
        wo_slab[...] = squeeze_rows(wo_z[...], 4)
        yield from gather_xy(net, wo_land, wo_slab, D // 2, pos, True)

    def expert_weights():
        me = c * 4 + z
        pieces = []
        for dc in (0, 1):
            for d in (0, 1, 3, 2):
                if (dc, d) == (0, 0):
                    continue
                cc, zz = lax.rem(c + dc, 2), lax.rem(z + d, 4)
                pieces.append(net.put(we.at[cc * 4 + zz], we_z.at[me], device(y, x, cc, zz)))
        kept = net.keep(we.at[me], we_z.at[me])
        yield
        kept.wait()
        for copy in pieces:
            copy.wait_recv()
        we_slab[...] = squeeze_rows(we_z[...], 8)
        yield from gather_xy(net, we_land, we_slab, 1024, pos, False)

    def cotangent():
        mine = gy_all.at[z, c]
        kept = net.keep(gy, mine)
        copies = [(d, net.put(gy, mine, device(y, x, c, z + d))) for d in (1, 3, 2)]
        passed = [net.put(gy, mine, sibling(pos))]
        yield
        for d, copy in copies:
            copy.wait_recv()
            got = gy_all.at[lax.rem(z + 4 - d, 4), c]
            passed.append(net.put(got, got, sibling(pos)))
        yield
        kept.wait()
        for copy in passed:
            copy.wait_recv()

    def pump(job):
        try:
            next(job)
        except StopIteration:
            pass

    wo_job, we_job, gy_job = out_weights(), expert_weights(), cotangent()
    pump(wo_job)
    tok_copies = [net.put(tok, tok_all.at[z], device(y, x, c, z + d)) for d in (1, 3, 2)]
    tok_kept = net.keep(tok, tok_all.at[z])
    pump(we_job)
    pump(gy_job)

    wq_kept.wait()
    for copy in wq_pieces:
        copy.wait_recv()
    wq_slab[...] = squeeze_rows(wq_z[...], 4)
    wq_job = gather_xy(net, wq_land, wq_slab, QW, pos, True)
    pump(wq_job)
    pump(wo_job)
    pump(wq_job)
    pump(wo_job)
    pump(wq_job)
    pump(wq_job)
    pump(wq_job)
    wq_saved = net.keep(wq_land, wq_out)

    for i in range(4):
        part = wq_land[i, :, :, :, GROUP_W:].reshape(QW, SMALL)
        one_hot = (
            lax.broadcasted_iota(jnp.int32, (16, SMALL), 0)
            == lax.broadcasted_iota(jnp.int32, (16, SMALL), 1)
        ).astype(BF)
        gains_out[:, i * QW : (i + 1) * QW] = lax.dot_general(
            one_hot, part, (((1,), (1,)), ((), ())), preferred_element_type=F32
        )
    tok_kept.wait()
    for copy in tok_copies:
        copy.wait_recv()
    tok_saved = net.keep(tok_all, tok_out)
    gain_attn = gains_out[EXPERTS + 1 : EXPERTS + 2, :]

    def normalise(i, carried):
        rows = tok_all[i].astype(F32)
        unit = rows * lax.rsqrt(jnp.mean(rows * rows, axis=-1, keepdims=True) + epsilon)
        out_stage[i // 2, lax.rem(i, 2)] = (unit * gain_attn).astype(BF)
        return carried

    lax.fori_loop(0, 4, normalise, 0)
    joined = jnp.dot(
        out_stage[...].reshape(BLK, D),
        wq_land[...].reshape(D, WQ)[:, :GROUP_W],
        preferred_element_type=F32,
    ).astype(BF)
    for half in range(2):
        rows = joined[half * HALF : (half + 1) * HALF]
        q_out[half] = rows[:, :QW]
        kv_land[y, x, c, half] = rows[:, QW:]

    swapped = net.put(q_out.at[1], q_in, device(my, mx, mc, z))
    whole = slice(None)
    along_x, along_y = [], []
    even, odd = kv_land.at[y, x, c, 0], kv_land.at[y, x, c, 1]
    for d in (1, 3, 2):
        along_x.append(net.put(even, even, device(y, x + d, c, z)))
        along_y.append(net.put(odd, odd, device(y + d, x, c, z)))
    m_ref[...] = jnp.full_like(m_ref, FLOOR)
    l_ref[...] = jnp.zeros_like(l_ref)
    acc[...] = jnp.zeros_like(acc)
    lo, hi = 2 * b, 2 * (NBLK - b) - 1
    at, first = query_places(bounds, lo, hi)
    for copy in along_x:
        copy.wait_recv()
    row = kv_land.at[y, whole, c, 0]
    from_y, crossed_y, crossed_x = net.reserve(4), net.reserve(4), net.reserve(4)
    for d in (1, 3):
        net.put_at(from_y + d, row, row, device(y + d, x, c, z))
    net.put_at(crossed_y, row, row, sibling(pos))
    for copy in along_y:
        copy.wait_recv()
    column = kv_land.at[whole, x, c, 1]
    from_x = net.reserve(4)
    for d in (1, 3):
        net.put_at(from_x + d, column, column, device(y, x + d, c, z))
    relay_y, relay_x = net.reserve(4), net.reserve(4)
    net.put_at(crossed_x, column, column, sibling(pos))
    pump(wo_job)
    pump(wo_job)
    swapped.wait_recv()
    for h in range(QPG):
        for i, rows in enumerate((q_out.at[0], q_in)):
            lanes = slice(i * PAIR + h * HALF, i * PAIR + (h + 1) * HALF)
            qt[:, lanes] = transposed(rows[:, h * HD : (h + 1) * HD])
    q_out[2] = q_in[...]

    def update(ids, block, chunk, masked):
        k_rows, v_rows = block[:, :HD], block[:, HD:]
        groups = head_lanes(ids)
        scores = [jnp.dot(k_rows, qt[:, g], preferred_element_type=F32) for g in groups]
        if masked:
            key_at = pair_places(chunk, block.shape[0], HALF)
            scores = [
                jnp.where((key_at >= first[:, g]) & (key_at <= at[:, g]), s, LOW)
                for g, s in zip(groups, scores)
            ]
        m_old = [m_ref[:, g] for g in groups]
        m_new = [jnp.maximum(m, jnp.max(s, axis=0, keepdims=True)) for m, s in zip(m_old, scores)]
        p = [jnp.exp2((s - m) * EXP_SCALE) for s, m in zip(scores, m_new)]
        alpha = [jnp.exp2((m - n) * EXP_SCALE) for m, n in zip(m_old, m_new)]
        pv = [
            lax.dot_general(v_rows, w.astype(BF), COL_COL, preferred_element_type=F32) for w in p
        ]
        sums = [jnp.sum(w, axis=0, keepdims=True) for w in p]
        for n, g in enumerate(groups):
            m_ref[:, g] = m_new[n]
            l_ref[:, g] = l_ref[:, g] * alpha[n] + sums[n]
            acc[:, g] = acc[:, g] * alpha[n] + pv[n]

    late = 2 * NBLK - 2

    def pair_step(yy, xx, half):
        chunk = (yy * 4 + xx) * 4 + half
        cases = pair_cases(chunk, lo, hi)
        early = chunk + 2 < late

        def go(ids, masked):
            update(ids, kv_land[yy, xx, :, half].reshape(2 * HALF, 2 * HD), chunk, masked)

        for case, ids, masked in zip(
            cases[:4], ((0, 1), (0,), (1,), (0, 1)), (False, False, False, True)
        ):

            @pl.when(case & early)
            def _():
                go(ids, masked)

    def stage(n, carried):
        d = turn(n)
        yy, xx = lax.rem(y + 4 - d, 4), lax.rem(x + 4 - d, 4)
        net.arrived(crossed_y + d, kv_land.at[yy, whole, 1 - c, 0])

        def step(t, carried):
            half = t // 4

            @pl.when(t == 4)
            def _():
                net.arrived(crossed_x + d, kv_land.at[whole, xx, 1 - c, 1])

            pair_step(jnp.where(half == 0, yy, t - 4), jnp.where(half == 0, t, xx), half)
            return carried

        lax.fori_loop(0, 8, step, 0)
        return carried

    lax.fori_loop(0, 1, stage, 0)
    for e in (1, 3):
        near_y, near_x = lax.rem(y + 4 - e, 4), lax.rem(x + 4 - e, 4)
        part = pl.ds(e - 1, 2)
        net.arrived(from_y + e, row)
        line = kv_land.at[near_y, part, c, 0]
        net.put_at(relay_y + e, line, line, device(y + e, x, c, z))
        net.arrived(from_x + e, column)
        line = kv_land.at[part, near_x, c, 1]
        net.put_at(relay_x + e, line, line, device(y, x + e, c, z))
    for e in (1, 3):
        near_y, near_x = lax.rem(y + 4 - e, 4), lax.rem(x + 4 - e, 4)
        line = kv_land.at[near_y, whole, c, 0]
        net.put_at(crossed_y + e, line, line, sibling(pos))
        line = kv_land.at[whole, near_x, c, 1]
        net.put_at(crossed_x + e, line, line, sibling(pos))
    pump(we_job)
    lax.fori_loop(1, 2, stage, 0)
    pump(we_job)
    far_y, far_x = lax.rem(y + 2, 4), lax.rem(x + 2, 4)
    for e in (1, 3):
        part = pl.ds(e - 1, 2)
        net.arrived(relay_y + e, kv_land.at[far_y, part, c, 0])
        net.arrived(relay_x + e, kv_land.at[part, far_x, c, 1])
    line = kv_land.at[far_y, whole, c, 0]
    net.put_at(crossed_y + 2, line, line, sibling(pos))
    line = kv_land.at[whole, far_x, c, 1]
    net.put_at(crossed_x + 2, line, line, sibling(pos))
    lax.fori_loop(2, 4, stage, 0)
    for n in range(4):
        for k in (crossed_y, crossed_x):
            net.left(k + n, row)
    for n in (1, 3):
        net.left(from_y + n, row)
        net.left(from_x + n, column)
        net.left(relay_y + n, kv_land.at[y, pl.ds(0, 2), c, 0])
        net.left(relay_x + n, kv_land.at[pl.ds(0, 2), x, c, 1])
    kv_saved = net.keep(kv_land, kv_out)

    def last_chunk(i, chunk_at):
        block = kv_land[3, 3, chunk_at // 2, lax.rem(chunk_at, 2)]
        update((i,), block, late - 2 + chunk_at, True)

    for i, chunk in enumerate((lo, hi)):

        @pl.when(chunk >= late - 2)
        def _():
            lax.fori_loop(0, 2, lambda n, _: last_chunk(i, n), None)

        @pl.when(chunk >= late)
        def _():
            lanes = LANES[(i,)]
            third = at[:, lanes] >= bounds[1]
            m_ref[:, lanes] = jnp.where(third, FLOOR, m_ref[:, lanes])
            l_ref[:, lanes] = jnp.where(third, 0.0, l_ref[:, lanes])
            acc[:, lanes] = jnp.where(third, 0.0, acc[:, lanes])
            lax.fori_loop(2, 4, lambda n, _: last_chunk(i, n), None)

    start, wait_mixed = exchange_heads(
        True, pos, lambda k: o_out.at[k], lambda g: mixed.at[:, pl.ds(mult(g * QW, QW), QW)], hs, hr
    )
    for i in range(2):
        for h in range(QPG):
            lanes = slice(i * PAIR + h * HALF, i * PAIR + (h + 1) * HALF)
            total = l_ref[:, lanes]
            lse_out[:, lanes] = m_ref[:, lanes] * EXP_SCALE + jnp.log(total) * LOG2E
            value = jnp.transpose(acc[:, lanes] / total, (1, 0)).astype(BF)
            o_out[2 * i, :, h * HD : (h + 1) * HD] = value[:ROWS]
            o_out[2 * i + 1, :, h * HD : (h + 1) * HD] = value[ROWS:]
        start(2 * i)
        start(2 * i + 1)

    pump(wo_job)
    pump(wo_job)
    wo_saved = net.keep(wo_land, wo_out)
    wait_mixed()
    pump(we_job)

    def add_hidden(i, carried):
        columns = pl.ds(mult(i * QW, QW), QW)
        hidden_out[:, columns] = tok[:, columns].astype(F32) + lax.dot_general(
            mixed[...], wo_land[i].reshape(QW, D), ROW_ROW, preferred_element_type=F32
        )
        return carried

    lax.fori_loop(0, 4, add_hidden, 0)
    hidden = hidden_out[...]
    unit = hidden * lax.rsqrt(jnp.mean(hidden * hidden, axis=-1, keepdims=True) + epsilon)
    low = (unit * gains_out[EXPERTS : EXPERTS + 1, :]).astype(BF)
    own_rows[:, :D] = low
    small_weights = wq_land[:, :, :, :, GROUP_W:].reshape(D, SMALL)
    logits = jnp.dot(low, small_weights, preferred_element_type=F32)
    is_used = used[...] > 0.0
    top = jnp.max(jnp.where(is_used, logits, LOW), axis=-1, keepdims=True)
    raised = jnp.where(is_used, jnp.exp(logits - top), 0.0)
    route = raised / jnp.sum(raised, axis=-1, keepdims=True)
    coarse = route.astype(BF).astype(F32)
    own_rows[:, D:] = (coarse + pltpu.roll(route - coarse, EXPERTS, 1)).astype(BF)

    mine = rows_all.at[z, c]
    rows_kept = net.keep(own_rows, mine)
    from_z, crossed_z = net.reserve(4), net.reserve(4)
    relay_z = net.reserve(4)
    for d in (1, 3):
        net.put_at(from_z + d, own_rows, mine, device(y, x, c, z + d))
    net.put_at(crossed_z, own_rows, mine, sibling(pos))
    for job in (gy_job, we_job, wo_job, wq_job):
        for _ in job:
            pass
    rows_kept.wait()
    to_core, to_z = net.reserve(4), net.reserve(4)
    me = c * 4 + z
    gate_columns, up_columns, down_columns = (slice(i * UP, (i + 1) * UP) for i in range(3))

    def weights(columns):
        return we_land[:, :, :, columns].reshape(D, UP)

    def finish_block(n):
        d, slot = turn(n), lax.rem(n, 2)
        zz = lax.rem(z + 4 - d, 4)
        net.arrived(to_core + n, core_land.at[n])
        both[n] = (parts[slot, c].astype(F32) + core_land[n].astype(F32)).astype(BF)
        net.left(to_core + n, parts.at[slot, 1 - c])

        @pl.when(n > 0)
        def _():
            net.put_at(to_z + d, both.at[n], z_land.at[d], device(y, x, c, zz))

    def expert_block(n, carried):
        d, slot = turn(n), lax.rem(n, 2)
        zz = lax.rem(z + 4 - d, 4)
        got = rows_all.at[zz, c]

        @pl.when(n == 1)
        def _():
            for e in (1, 3):
                near = rows_all.at[lax.rem(z + 4 - e, 4), c]
                net.arrived(from_z + e, near)
                part = near.at[pl.ds((e - 1) * 32, 64)]
                net.put_at(relay_z + e, part, part, device(y, x, c, z + e))
                net.put_at(crossed_z + e, near, near, sibling(pos))

        @pl.when(n == 3)
        def _():
            for e in (1, 3):
                net.arrived(relay_z + e, got.at[pl.ds((e - 1) * 32, 64)])
            net.put_at(crossed_z + 2, got, got, sibling(pos))

        net.arrived(crossed_z + d, rows_all.at[zz, 1 - c])

        @pl.when(n > 1)
        def _():
            pltpu.make_async_copy(out_stage.at[slot], out_stage.at[slot], gs.at[slot]).wait()

        rows = rows_all[zz].reshape(2 * ROWS, RW)
        x_rows, lanes = rows[:, :D], rows[:, D:].astype(F32)
        lane = lax.broadcasted_iota(jnp.int32, lanes.shape, 1)
        route = jnp.sum(
            jnp.where((lane == me) | (lane == me + EXPERTS), lanes, 0.0), axis=-1, keepdims=True
        )
        gy_rows = gy_all[zz].reshape(2 * ROWS, D)
        gate = jnp.dot(x_rows, weights(gate_columns), preferred_element_type=F32)
        up = jnp.dot(x_rows, weights(up_columns), preferred_element_type=F32)
        raw = jnp.dot(gy_rows, weights(down_columns), preferred_element_type=F32)
        unit_lane = lax.broadcasted_iota(jnp.int32, gate.shape, 1)
        share = jnp.where(unit_lane < FE, route, 1.0)
        sig = 1.0 / (1.0 + jnp.exp(-gate))
        silu = gate * sig
        inner = silu * up
        scaled = (inner * share).astype(BF)
        inner_all[zz] = scaled
        route_grad = jnp.sum(inner[:, :FE] * raw[:, :FE], axis=-1, keepdims=True)
        inner_grad = raw * share
        pre_grad = jnp.concatenate(
            [inner_grad * up * (sig + silu * (1.0 - sig)), inner_grad * silu], axis=-1
        ).astype(BF)
        pre_all[zz] = pre_grad
        out_stage[slot] = (
            lax.dot_general(scaled, weights(down_columns), ROW_ROW, preferred_element_type=F32)
            .astype(BF)
            .reshape(2, ROWS, D)
        )
        pltpu.make_async_copy(out_stage.at[slot], out_parts.at[zz], gs.at[slot]).start()
        rows_grad = lax.dot_general(
            pre_grad[:, :UP], weights(gate_columns), ROW_ROW, preferred_element_type=F32
        ) + lax.dot_general(
            pre_grad[:, UP:], weights(up_columns), ROW_ROW, preferred_element_type=F32
        )
        parts[slot, :, :, :D] = rows_grad.astype(BF).reshape(2, ROWS, D)
        high = route_grad.astype(BF).astype(F32)
        parts[slot, :, :, D:] = (
            jnp.where(lane == me, high, 0.0) + jnp.where(lane == me + EXPERTS, route_grad - high, 0.0)
        ).astype(BF).reshape(2, ROWS, SMALL)
        net.put_at(to_core + n, parts.at[slot, 1 - c], core_land.at[n], sibling(pos))

        @pl.when(n > 0)
        def _():
            finish_block(n - 1)

        return carried

    lax.fori_loop(0, 4, expert_block, 0)
    finish_block(3)
    for slot in range(2):
        pltpu.make_async_copy(out_stage.at[slot], out_stage.at[slot], gs.at[slot]).wait()

    def weight_grads(t, carried):
        slot = lax.rem(t, 2)

        @pl.when(t > 1)
        def _():
            pltpu.make_async_copy(dwe_stage.at[slot], dwe_stage.at[slot], gr.at[slot]).wait()

        columns = pl.ds(mult(t * QW, QW), QW)
        for i in range(3):
            value = jnp.zeros((QW, UP), F32)
            for k in range(4):
                left = (rows_all if i < 2 else gy_all)[k, :, :, columns].reshape(2 * ROWS, QW)
                right = pre_all[k, :, i * UP : (i + 1) * UP] if i < 2 else inner_all[k]
                value = value + lax.dot_general(left, right, COL_COL, preferred_element_type=F32)
            dwe_stage[slot, :, :, i * UP : (i + 1) * UP] = value.astype(BF).reshape(4, 96, UP)
        pltpu.make_async_copy(dwe_stage.at[slot], dwe_out.at[t], gr.at[slot]).start()
        return carried

    lax.fori_loop(0, 4, weight_grads, 0)

    for d in (1, 2, 3):
        net.arrived(to_z + d, z_land.at[d])

    def total(columns):
        value = both[0, :, columns].astype(F32)
        for d in (1, 2, 3):
            value = value + z_land[d, :, columns].astype(F32)
        return value

    lane = lax.broadcasted_iota(jnp.int32, (ROWS, SMALL), 1)
    route_grads = total(slice(D, RW))
    route_grads = route_grads + pltpu.roll(route_grads, SMALL - EXPERTS, 1)
    logits_grad = (
        route * (route_grads - jnp.sum(route * route_grads, axis=-1, keepdims=True))
    ).astype(BF)
    normed_grad = total(slice(0, D)) + lax.dot_general(
        logits_grad, small_weights, ROW_ROW, preferred_element_type=F32
    )
    hidden = hidden_out[...]
    scale = lax.rsqrt(jnp.mean(hidden * hidden, axis=-1, keepdims=True) + epsilon)
    unit = hidden * scale
    dn = normed_grad * gains_out[EXPERTS : EXPERTS + 1, :]
    hidden_grad = gy_all[z, c].astype(F32) + scale * (
        dn - unit * jnp.mean(dn * unit, axis=-1, keepdims=True)
    )
    hidden_grad_out[...] = hidden_grad
    hidden_low = hidden_grad.astype(BF)
    hidden_low_out[...] = hidden_low
    total_grad = jnp.zeros((ROWS, D), F32)
    for i in range(4):
        total_grad = total_grad + jnp.dot(
            hidden_low[:, i * QW : (i + 1) * QW],
            wo_land[i].reshape(QW, D),
            preferred_element_type=F32,
        )
    start, wait_heads = exchange_heads(
        False, pos, lambda g: mixed_grad.at[g], lambda k: do_in.at[k], hs2, hr2
    )
    for g in range(4):
        mixed_grad[g] = total_grad[:, g * QW : (g + 1) * QW].astype(BF)
        start(g)
    gain_column = jnp.where(lane == EXPERTS, 1.0, 0.0).astype(BF)
    small_out[...] = (
        lax.dot_general(own_rows[:, :D], logits_grad, COL_COL, preferred_element_type=F32)
        + lax.dot_general(
            (normed_grad * unit).astype(BF), gain_column, COL_COL, preferred_element_type=F32
        )
    ).astype(BF)
    for n in range(4):
        net.left(crossed_z + n, own_rows)
        if n:
            net.left(to_z + n, both.at[n])
    for n in (1, 3):
        net.left(from_z + n, own_rows)
        net.left(relay_z + n, own_rows.at[pl.ds(0, 64)])
    for slot in range(2):
        pltpu.make_async_copy(dwe_stage.at[slot], dwe_stage.at[slot], gr.at[slot]).wait()
    wait_heads()
    do_out[...] = do_in[...]
    for copy in (wq_saved, tok_saved, kv_saved, wo_saved):
        copy.wait()
    net.finish()


def forward(bounds, tok, wq, wo, we, gy, used):
    outs = {
        "wo": ((4, 4, 2, 48, D), BF, ANY),
        "wq": ((4, 4, 2, 48, WQ), BF, ANY),
        "kv": ((4, 4, 2, 2, HALF, 2 * HD), BF, ANY),
        "q": ((3, HALF, QW), BF, VM),
        "o": ((4, ROWS, QW), BF, VM),
        "lse": ((1, 2 * PAIR), F32, VM),
        "tok": ((4, ROWS, D), BF, ANY),
        "hidden": ((ROWS, D), F32, VM),
        "hidden_grad": ((ROWS, D), F32, VM),
        "hidden_low": ((ROWS, D), BF, VM),
        "gains": ((16, D), F32, VM),
        "small": ((D, SMALL), BF, VM),
        "do": ((4, ROWS, QW), BF, VM),
        "out_parts": ((4, 2, ROWS, D), BF, ANY),
        "dwe": ((4, 4, 96, WE), BF, ANY),
    }
    values = pl.pallas_call(
        forward_kernel,
        name="forward",
        out_shape=tuple(jax.ShapeDtypeStruct(s, t) for s, t, _ in outs.values()),
        in_specs=[SM, VM, ANY, ANY, ANY, ANY, VM],
        out_specs=tuple(m for _, _, m in outs.values()),
        scratch_shapes=[
            pltpu.VMEM((4, 16, WQ), BF),
            pltpu.VMEM((48, WQ), BF),
            pltpu.VMEM((4, 4, 2, 48, WQ), BF),
            pltpu.VMEM((4, 16, D), BF),
            pltpu.VMEM((48, D), BF),
            pltpu.VMEM((4, 4, 2, 48, D), BF),
            pltpu.VMEM((8, 16, WE), BF),
            pltpu.VMEM((96, WE), BF),
            pltpu.VMEM((4, 4, 96, WE), BF),
            pltpu.VMEM((4, ROWS, D), BF),
            pltpu.VMEM((4, 4, 2, 2, HALF, 2 * HD), BF),
            pltpu.VMEM((HALF, QW), BF),
            pltpu.VMEM((HD, 2 * PAIR), BF),
            pltpu.VMEM((1, 2 * PAIR), F32),
            pltpu.VMEM((1, 2 * PAIR), F32),
            pltpu.VMEM((HD, 2 * PAIR), F32),
            pltpu.VMEM((ROWS, D), BF),
            pltpu.VMEM((ROWS, RW), BF),
            pltpu.VMEM((4, 2, ROWS, RW), BF),
            pltpu.VMEM((4, 2, ROWS, D), BF),
            pltpu.VMEM((4, 2 * ROWS, UP), BF),
            pltpu.VMEM((4, 2 * ROWS, 2 * UP), BF),
            pltpu.VMEM((2, 2, ROWS, RW), BF),
            pltpu.VMEM((2, 2, ROWS, D), BF),
            pltpu.VMEM((4, ROWS, RW), BF),
            pltpu.VMEM((4, ROWS, RW), BF),
            pltpu.VMEM((4, ROWS, RW), BF),
            pltpu.VMEM((2, 4, 96, WE), BF),
            pltpu.VMEM((4, ROWS, QW), BF),
            pltpu.VMEM((4, ROWS, QW), BF),
        ]
        + sems(144, 32)
        + [pltpu.SemaphoreType.DMA((4,))] * 6,
        compiler_params=pltpu.CompilerParams(
            collective_id=1, has_side_effects=True, vmem_limit_bytes=VMEM_LIMIT
        ),
    )(bounds, tok, wq, wo, we, gy, used)
    return dict(zip(outs, values))


def add_into(dst, left, right, rows):
    step = 32

    def body(i, carried):
        place = pl.ds(mult(i * step, step), step)
        dst[place, :] = (left[place, :].astype(F32) + right[place, :].astype(F32)).astype(
            dst.dtype
        )
        return carried

    lax.fori_loop(0, rows // step, body, 0)


def add_four(dst, parts, rows, step):
    def body(i, carried):
        place = pl.ds(mult(i * step, step), step)
        total = parts[0][place, :].astype(F32)
        for part in parts[1:]:
            total = total + part[place, :].astype(F32)
        dst[place, :] = total.astype(dst.dtype)
        return carried

    lax.fori_loop(0, rows // step, body, 0)


def sum_group(net, parts, pos, core_land, own, both, z_land, out):
    y, x, c, z = pos
    order = (0, 1, 3, 2)
    crossing, kept = [], []
    for d in order:
        zz = lax.rem(z + d, 4)
        crossing.append(net.put(parts.at[zz, 1 - c], core_land.at[zz], sibling(pos)))
        kept.append(net.keep(parts.at[zz, c], own.at[zz]))
    yield
    arriving = []
    for n, d in enumerate(order):
        zz = lax.rem(z + d, 4)
        crossing[n].wait_recv()
        kept[n].wait()
        add_into(both.at[zz], own.at[zz], core_land.at[zz], ROWS)
        if d:
            arriving.append(net.put(both.at[zz], z_land.at[d - 1], device(y, x, c, zz)))
    yield
    for copy in arriving:
        copy.wait_recv()
    add_four(out, [both.at[z]] + [z_land.at[d] for d in range(3)], ROWS, 32)


def group_scratch(width):
    return [
        pltpu.VMEM((4, ROWS, width), BF),
        pltpu.VMEM((4, ROWS, width), BF),
        pltpu.VMEM((4, ROWS, width), BF),
        pltpu.VMEM((3, ROWS, width), BF),
    ]


def fold_parts(own, land, total, rows):
    step = 16

    def body(i, carried):
        q = i // (rows // step)
        place = pl.ds(mult(lax.rem(i, rows // step) * step, step), step)
        value = own[q, place, :].astype(F32)
        for d in range(3):
            value = value + land[d, q, place, :].astype(F32)
        total[q, place, :] = value.astype(BF)
        return carried

    lax.fori_loop(0, 4 * (rows // step), body, 0)


def scatter_first(net, src, pos, cut, a_own, a_land, b_own, b_land, a_sum, b_sum):
    y, x, c, z = pos
    rows, width = src.shape[2], src.shape[3]
    first, second = pl.ds(0, cut), pl.ds(cut, width - cut)
    whole = slice(None)
    keep_a = net.keep(src.at[whole, x, whole, first], a_own)
    keep_b = net.keep(src.at[y, whole, whole, second], b_own)
    to_x, to_y = [], []
    for d in (1, 3, 2):
        xx, yy = lax.rem(x + d, 4), lax.rem(y + d, 4)
        to_x.append(
            net.put(src.at[whole, xx, whole, first], a_land.at[d - 1], device(y, xx, c, z))
        )
        to_y.append(
            net.put(src.at[yy, whole, whole, second], b_land.at[d - 1], device(yy, x, c, z))
        )
    yield
    keep_a.wait()
    for copy in to_x:
        copy.wait_recv()
    fold_parts(a_own, a_land, a_sum, rows)
    keep_b.wait()
    for copy in to_y:
        copy.wait_recv()
    fold_parts(b_own, b_land, b_sum, rows)


def scatter_second(net, pos, cut, a_sum, a_last, b_sum, b_last, out):
    y, x, c, z = pos
    rows, width = out.shape
    last_y, last_x = [], []
    for d in (1, 3, 2):
        yy, xx = lax.rem(y + d, 4), lax.rem(x + d, 4)
        last_y.append(net.put(a_sum.at[yy], a_last.at[d - 1], device(yy, x, c, z)))
        last_x.append(net.put(b_sum.at[xx], b_last.at[d - 1], device(y, xx, c, z)))
    yield
    for copy in last_y:
        copy.wait_recv()
    for copy in last_x:
        copy.wait_recv()
    step = 16
    first, second = slice(0, cut), slice(cut, width)

    def final(i, carried):
        place = pl.ds(mult(i * step, step), step)
        for at, own, last, columns in ((y, a_sum, a_last, first), (x, b_sum, b_last, second)):
            value = own[at, place, :].astype(F32)
            for d in range(3):
                value = value + last[d, place, :].astype(F32)
            out[place, columns] = value.astype(BF)
        return carried

    lax.fori_loop(0, rows // step, final, 0)


def first_scratch(rows, width, cut):
    shapes = []
    for w in (cut, width - cut):
        shapes += [pltpu.VMEM((4, rows, w), BF), pltpu.VMEM((3, 4, rows, w), BF)]
    return shapes


def second_scratch(rows, width, cut):
    return [pltpu.VMEM((3, rows, cut), BF), pltpu.VMEM((3, rows, width - cut), BF)]


def backward_kernel(
    bounds, q, o, do, lse, kv_in, dwe, hg, out_parts,
    dkv_out, dq_out, o_out, we_a, we_b, hg_all, out_sum,
    kv, o_in, dq_own, dq_in, q_rows, do_rows, qt, dot_t, delta, late_lse, dqt, part, core_land, both, a_land, b_land,
    a_sum, b_sum, a_last, b_last, *scratch,
):
    we_s = scratch[:4]
    group_s = scratch[4:8]
    ss, rs, ls = scratch[8:]
    pos = position()
    y, x, c, z = pos
    b = (y * 4 + x) * 2 + c
    net = Net(ss, rs, ls)
    kv_kept = [net.keep(kv_in.at[i], kv.at[i]) for i in range(4)]
    everyone_here = announce(
        z_peers(pos) + xy_peers(pos) + [device(*mirror(pos))] + other_column(pos)
    )
    lo, hi = 2 * b, 2 * (NBLK - b) - 1
    at, first = query_places(bounds, lo, hi)
    for i in range(2):
        for h in range(QPG):
            columns = slice(h * HD, (h + 1) * HD)
            lanes = slice(i * PAIR + h * HALF, i * PAIR + (h + 1) * HALF)
            q_rows[lanes, :] = q[2 * i, :, columns]
            qt[:, lanes] = transposed(q[2 * i, :, columns])
            rows = do[2 * i : 2 * i + 2, :, columns].reshape(HALF, HD)
            do_rows[lanes, :] = rows
            do_t = jnp.transpose(rows.astype(F32), (1, 0))
            o_t = jnp.transpose(
                o[2 * i : 2 * i + 2, :, columns].reshape(HALF, HD).astype(F32), (1, 0)
            )
            dot_t[:, lanes] = do_t.astype(BF)
            delta[:, lanes] = jnp.sum(do_t * o_t, axis=0, keepdims=True)
    late_lse[...] = jnp.where(at >= bounds[1], -LOW, lse[...])
    dqt[...] = jnp.zeros_like(dqt)
    everyone_here()
    o_swap = net.put(o.at[pl.ds(2, 2)], o_in, device(*mirror(pos)))
    whole = slice(None)

    def experts():
        yield from scatter_first(net, dwe, pos, 1024, *we_s, we_a, we_b)

    def rows_of_group():
        mine = hg_all.at[z]
        kept = net.keep(hg, mine)
        copies = [net.put(hg, mine, device(y, x, c, z + d)) for d in (1, 3, 2)]
        yield
        kept.wait()
        for copy in copies:
            copy.wait_recv()

    def pump(job):
        try:
            next(job)
        except StopIteration:
            pass

    we_job = experts()
    out_job = sum_group(net, out_parts, pos, *group_s, out_sum)
    hg_job = rows_of_group()
    pump(out_job)
    pump(we_job)
    pump(hg_job)

    for copy in kv_kept:
        copy.wait()
    pump(out_job)

    def pairs(ids, yy, xx, half, slot, chunk, masked):
        block = kv[yy, xx, :, half].reshape(2 * HALF, 2 * HD)
        k_rows, v_rows = block[:, :HD], block[:, HD:]
        groups = head_lanes(ids)
        scores = [jnp.dot(k_rows, qt[:, g], preferred_element_type=F32) for g in groups]
        dp = [jnp.dot(v_rows, dot_t[:, g], preferred_element_type=F32) for g in groups]
        if masked:
            key_at = pair_places(chunk, 2 * HALF, HALF)
            p = [
                jnp.where(
                    (key_at >= first[:, g]) & (key_at <= at[:, g]),
                    jnp.exp2(s * EXP_SCALE - lse[:, g]),
                    0.0,
                )
                for g, s in zip(groups, scores)
            ]
        else:
            p = [jnp.exp2(s * EXP_SCALE - late_lse[:, g]) for g, s in zip(groups, scores)]
        ds = [(w * (t - delta[:, g])).astype(BF) for g, w, t in zip(groups, p, dp)]
        dv = jnp.zeros((2 * HALF, HD), F32)
        dk = jnp.zeros((2 * HALF, HD), F32)
        for g, w, t in zip(groups, p, ds):
            dv = dv + jnp.dot(w.astype(BF), do_rows[g, :], preferred_element_type=F32)
            dk = dk + jnp.dot(t, q_rows[g, :], preferred_element_type=F32)
        dq = [lax.dot_general(k_rows, t, COL_COL, preferred_element_type=F32) for t in ds]
        for g, t in zip(groups, dq):
            dqt[:, g] += t
        part[slot, :, half, :, :HD] = (dk * SCALE).astype(BF).reshape(2, HALF, HD)
        part[slot, :, half, :, HD:] = dv.astype(BF).reshape(2, HALF, HD)

    def pair_step(yy, xx, half, slot):
        chunk = (yy * 4 + xx) * 4 + half
        cases = pair_cases(chunk, lo, hi)
        for case, ids, masked in zip(
            cases[:4], ((0, 1), (0,), (1,), (0, 1)), (False, False, False, True)
        ):

            @pl.when(case)
            def _():
                pairs(ids, yy, xx, half, slot, chunk, masked)

        @pl.when(cases[4])
        def _():
            part[slot, :, half] = jnp.zeros((2, HALF, 2 * HD), BF)

    def chip(t):
        dy = jnp.where(
            t < 4,
            t,
            jnp.where(
                t < 7,
                1,
                jnp.where(
                    t < 10,
                    jnp.where(t == 7, 0, t - 6),
                    jnp.where(
                        t < 12, 3, jnp.where(t < 14, 2 * (t - 12), 2 * (15 - t))
                    ),
                ),
            ),
        )
        dx = jnp.where(
            t < 4,
            1,
            jnp.where(
                t < 7,
                jnp.where(t == 4, 0, t - 3),
                jnp.where(
                    t < 10,
                    3,
                    jnp.where(t < 12, 2 * (t - 10), jnp.where(t < 14, 2, 0)),
                ),
            ),
        )
        return lax.rem(y + dy, 4), lax.rem(x + dx, 4)

    to_core, to_x, to_y = net.reserve(16), net.reserve(4), net.reserve(4)

    def fold_chip(t):
        yy, xx = chip(t)
        slot = lax.rem(t, 2)
        net.arrived(to_core + t, core_land.at[yy, xx])
        both[yy, xx] = (part[slot, c].astype(F32) + core_land[yy, xx].astype(F32)).astype(BF)
        net.left(to_core + t, part.at[slot, 1 - c])

    def send_lines(d):
        xx, yy = lax.rem(x + d, 4), lax.rem(y + d, 4)
        net.put_at(to_x + d, both.at[whole, xx, 0], a_land.at[d], device(y, xx, c, z))
        net.put_at(to_y + d, both.at[yy, whole, 1], b_land.at[d], device(yy, x, c, z))

    far_x, far_y = net.reserve(4), net.reserve(4)

    def send_far(odd):
        xx, yy = lax.rem(x + 2, 4), lax.rem(y + 2, 4)
        for e in (odd, odd + 2):
            ye, xe = lax.rem(y + e, 4), lax.rem(x + e, 4)
            net.put_at(far_x + e, both.at[ye, xx, 0], a_land.at[2, ye], device(y, xx, c, z))
            net.put_at(far_y + e, both.at[yy, xe, 1], b_land.at[2, xe], device(yy, x, c, z))

    def chip_step(t, carried):
        yy, xx = chip(t)
        slot = lax.rem(t, 2)

        def step(n, carried):
            pair_step(yy, xx, n, slot)
            return carried

        lax.fori_loop(0, 2, step, 0)
        net.put_at(to_core + t, part.at[slot, 1 - c], core_land.at[yy, xx], sibling(pos))

        @pl.when(t > 0)
        def _():
            fold_chip(t - 1)

        for at_chip, send in (
            (7, lambda: send_lines(1)),
            (12, lambda: (send_lines(3), send_far(1))),
            (15, lambda: send_far(0)),
        ):

            @pl.when(t == at_chip)
            def _():
                send()

        return carried

    lax.fori_loop(0, 16, chip_step, 0)
    for i in range(2):
        for h in range(QPG):
            lanes = slice(i * PAIR + h * HALF, i * PAIR + (h + 1) * HALF)
            dq_own[i, :, h * HD : (h + 1) * HD] = jnp.transpose(
                dqt[:, lanes] * SCALE, (1, 0)
            ).astype(BF)
    dq_swap = net.put(dq_own.at[1], dq_in, device(*mirror(pos)))
    lax.fori_loop(15, 16, lambda t, _: fold_chip(t), None)

    def fold_lines(own_at, land, total):
        def body(n, carried):
            q_at, place = n // 8, pl.ds(mult(lax.rem(n, 8) * 32, 32), 32)
            value = own_at(q_at, place).astype(F32)
            for d in (1, 2, 3):
                value = value + land[d, q_at, place, :].astype(F32)
            total[q_at, place, :] = value.astype(BF)
            return carried

        lax.fori_loop(0, 32, body, 0)

    for d in (1, 3):
        net.arrived(to_x + d, a_land.at[d])
    for e in range(4):
        net.arrived(far_x + e, a_land.at[2, e])
    fold_lines(lambda n, place: both[n, x, 0, place, :], a_land, a_sum)
    last_y = []
    for d in (1, 3, 2):
        yy = lax.rem(y + d, 4)
        last_y.append(net.put(a_sum.at[yy], a_last.at[d], device(yy, x, c, z)))
    for d in (1, 3):
        net.arrived(to_y + d, b_land.at[d])
    for e in range(4):
        net.arrived(far_y + e, b_land.at[2, e])
    fold_lines(lambda n, place: both[y, n, 1, place, :], b_land, b_sum)
    last_x = []
    for d in (1, 3, 2):
        xx = lax.rem(x + d, 4)
        last_x.append(net.put(b_sum.at[xx], b_last.at[d], device(y, xx, c, z)))
    pump(we_job)
    pump(out_job)
    o_swap.wait_recv()
    o_out[0] = o[0]
    o_out[1] = o[1]
    o_out[2] = o_in[0]
    o_out[3] = o_in[1]
    dq_swap.wait_recv()
    dq_out[0] = dq_own[0]
    dq_out[1] = dq_in[...]
    for copies, total, last, at, half in (
        (last_y, a_sum, a_last, y, 0),
        (last_x, b_sum, b_last, x, 1),
    ):
        for copy in copies:
            copy.wait_recv()
        value = total[at].astype(F32)
        for d in (1, 2, 3):
            value = value + last[d].astype(F32)
        dkv_out[half] = value.astype(BF)
    for job in (hg_job, out_job, we_job):
        for _ in job:
            pass
    for d in (1, 3):
        net.left(to_x + d, a_land.at[d])
        net.left(to_y + d, b_land.at[d])
    for e in range(4):
        net.left(far_x + e, a_land.at[2, e])
        net.left(far_y + e, b_land.at[2, e])
    net.finish()


def backward(bounds, q, o, do, lse, kv, dwe, hg, out_parts):
    return pl.pallas_call(
        backward_kernel,
        name="backward",
        out_shape=(
            jax.ShapeDtypeStruct((2, HALF, 2 * HD), BF),
            jax.ShapeDtypeStruct((2, HALF, QW), BF),
            jax.ShapeDtypeStruct((4, ROWS, QW), BF),
            jax.ShapeDtypeStruct((4, 96, 1024), BF),
            jax.ShapeDtypeStruct((4, 96, WE - 1024), BF),
            jax.ShapeDtypeStruct((4, ROWS, D), BF),
            jax.ShapeDtypeStruct((ROWS, D), F32),
        ),
        in_specs=[SM] + [VM] * 4 + [ANY] * 4,
        out_specs=(VM, VM, VM, VM, VM, ANY, VM),
        scratch_shapes=[
            pltpu.VMEM((4, 4, 2, 2, HALF, 2 * HD), BF),
            pltpu.VMEM((2, ROWS, QW), BF),
            pltpu.VMEM((2, HALF, QW), BF),
            pltpu.VMEM((HALF, QW), BF),
            pltpu.VMEM((2 * PAIR, HD), BF),
            pltpu.VMEM((2 * PAIR, HD), BF),
            pltpu.VMEM((HD, 2 * PAIR), BF),
            pltpu.VMEM((HD, 2 * PAIR), BF),
            pltpu.VMEM((1, 2 * PAIR), F32),
            pltpu.VMEM((1, 2 * PAIR), F32),
            pltpu.VMEM((HD, 2 * PAIR), F32),
            pltpu.VMEM((2, 2, 2, HALF, 2 * HD), BF),
            pltpu.VMEM((4, 4, 2, HALF, 2 * HD), BF),
            pltpu.VMEM((4, 4, 2, HALF, 2 * HD), BF),
            pltpu.VMEM((4, 4, HALF, 2 * HD), BF),
            pltpu.VMEM((4, 4, HALF, 2 * HD), BF),
            pltpu.VMEM((4, HALF, 2 * HD), BF),
            pltpu.VMEM((4, HALF, 2 * HD), BF),
            pltpu.VMEM((4, HALF, 2 * HD), BF),
            pltpu.VMEM((4, HALF, 2 * HD), BF),
        ]
        + first_scratch(96, WE, 1024)
        + group_scratch(D)
        + sems(72, 16),
        compiler_params=pltpu.CompilerParams(
            collective_id=7, has_side_effects=True, vmem_limit_bytes=VMEM_LIMIT
        ),
    )(bounds, q, o, do, lse, kv, dwe, hg, out_parts)


def close_kernel(
    dq, dkv, o, hg_in, tok_in, wq_in, gains, small, we_a_in, we_b_in,
    norm_grad, dwq_out, dwe_out, hg, tok, wq, we_a, we_b,
    joined, unit_all, n_part, n_land, dwq, w_land, w_both, *scratch,
):
    w_first, w_second, we_last = scratch[:4], scratch[4:6], scratch[6:8]
    w_a, w_b, w_rows, w_pieces, we_rows, we_pieces = scratch[8:14]
    ss, rs, ls = scratch[14:]
    pos = position()
    y, x, c, z = pos
    net = Net(ss, rs, ls)
    loads = [
        net.keep(src, dst)
        for src, dst in (
            (tok_in, tok), (hg_in, hg), (wq_in, wq), (we_a_in, we_a), (we_b_in, we_b)
        )
    ]
    everyone_here = announce(z_peers(pos) + xy_peers(pos) + other_column(pos))
    for copy in loads:
        copy.wait()
    joined[:, :, :QW] = dq[...].reshape(4, ROWS, QW)
    joined[:, :, QW:] = dkv[...].reshape(4, ROWS, 2 * HD)
    gain_attn = gains[EXPERTS + 1 : EXPERTS + 2, :]
    to_z, to_core = net.reserve(4), net.reserve(4)

    def normalise(k, carried):
        rows = tok[k].astype(F32)
        scale = lax.rsqrt(jnp.mean(rows * rows, axis=-1, keepdims=True) + epsilon)
        unit_all[k] = (rows * scale).astype(BF)
        return carried

    lax.fori_loop(0, 4, normalise, 0)

    everyone_here()
    experts_job = scatter_second(net, pos, 1024, we_a, we_last[0], we_b, we_last[1], we_rows)
    next(experts_job)

    def fold(t):
        net.arrived(to_core + t, w_land.at[t])

        def body(i, inner):
            xx, place = i // 3, pl.ds(mult(lax.rem(i, 3) * 16, 16), 16)
            w_both[t, xx, place, :] = (
                dwq[t, xx, c, place, :].astype(F32) + w_land[t, xx, place, :].astype(F32)
            ).astype(BF)
            return inner

        lax.fori_loop(0, 12, body, 0)
        net.left(to_core + t, w_land.at[t])

    def weight_grads(t, carried):
        columns = pl.ds(mult(t * QW, QW), QW)
        unit_grad = jnp.zeros((QW, GROUP_W), F32)
        wo_grad = jnp.zeros((QW, QW), F32)
        for k in range(4):
            unit_grad = unit_grad + lax.dot_general(
                unit_all[k, :, columns], joined[k], COL_COL, preferred_element_type=F32
            )
            wo_grad = wo_grad + lax.dot_general(
                hg[k, :, columns], o[k], COL_COL, preferred_element_type=F32
            )
        weights = wq[t].reshape(QW, WQ).astype(F32)
        lane = lax.broadcasted_iota(jnp.int32, (QW, SMALL), 1)
        here = lane == EXPERTS + 1
        small_weights = weights[:, GROUP_W:]
        gain = jnp.sum(jnp.where(here, small_weights, 0.0), axis=-1, keepdims=True)
        gain_grad = jnp.sum(unit_grad * weights[:, :GROUP_W], axis=-1, keepdims=True)
        small_grad = small[pl.ds(mult(t * QW, QW), QW), :].astype(F32)
        small_grad = jnp.where(here, gain_grad, small_grad)
        dwq[t, :, :, :, :GROUP_W] = (unit_grad * gain).astype(BF).reshape(4, 2, 48, GROUP_W)
        dwq[t, :, :, :, GROUP_W : GROUP_W + QW] = wo_grad.astype(BF).reshape(4, 2, 48, QW)
        dwq[t, :, :, :, GROUP_W + QW :] = small_grad.astype(BF).reshape(4, 2, 48, SMALL)
        net.put_at(to_core + t, dwq.at[t, :, 1 - c], w_land.at[t], sibling(pos))

        @pl.when(t > 0)
        def _():
            fold(t - 1)

        return carried

    lax.fori_loop(0, 4, weight_grads, 0)
    fold(3)
    weights_job = scatter_first(net, w_both, pos, GROUP_W, *w_first, w_a, w_b)
    next(weights_job)

    normed_grads = lax.dot_general(
        joined[...].reshape(BLK, GROUP_W),
        wq[...].reshape(D, WQ)[:, :GROUP_W],
        ROW_ROW,
        preferred_element_type=F32,
    )
    n_part[...] = normed_grads.astype(BF).reshape(4, ROWS, D)
    for d in (1, 3, 2):
        zz = lax.rem(z + d, 4)
        net.put_at(to_z + d, n_part.at[zz], n_land.at[d], device(y, x, c, zz))
    for _ in experts_job:
        pass
    we_pieces[...] = spread_rows(we_rows[...], 8)
    me = c * 4 + z
    expert_pieces = []
    for dc in (0, 1):
        for d in (0, 1, 3, 2):
            if (dc, d) == (0, 0):
                continue
            cc, zz = lax.rem(c + dc, 2), lax.rem(z + d, 4)
            expert_pieces.append(
                net.put(we_pieces.at[cc * 4 + zz], dwe_out.at[me], device(y, x, cc, zz))
            )
    expert_kept = net.keep(we_pieces.at[me], dwe_out.at[me])
    for _ in weights_job:
        pass
    weights_job = scatter_second(net, pos, GROUP_W, w_a, w_second[0], w_b, w_second[1], w_rows)
    next(weights_job)
    for d in (1, 2, 3):
        net.arrived(to_z + d, n_land.at[d])
    normed_grad = n_part[z].astype(F32)
    for d in (1, 2, 3):
        normed_grad = normed_grad + n_land[d].astype(F32)
    rows = tok[z].astype(F32)
    scale = lax.rsqrt(jnp.mean(rows * rows, axis=-1, keepdims=True) + epsilon)
    unit = rows * scale
    dn = normed_grad * gain_attn
    norm_grad[...] = scale * (
        dn - unit * jnp.mean(dn * unit, axis=-1, keepdims=True)
    )
    for _ in weights_job:
        pass
    w_pieces[...] = spread_rows(w_rows[...], 4)
    kept = net.keep(w_pieces.at[z], dwq_out.at[z])
    pieces = [
        net.put(w_pieces.at[lax.rem(z + d, 4)], dwq_out.at[z], device(y, x, c, z + d))
        for d in (1, 3, 2)
    ]
    expert_kept.wait()
    for copy in expert_pieces:
        copy.wait_recv()
    kept.wait()
    for copy in pieces:
        copy.wait_recv()
    for d in (1, 2, 3):
        net.left(to_z + d, n_land.at[d])
    net.finish()


def closing(dq, dkv, o, hg, tok, wq, gains, small, we_a, we_b):
    return pl.pallas_call(
        close_kernel,
        name="closing",
        out_shape=(
            jax.ShapeDtypeStruct((ROWS, D), F32),
            jax.ShapeDtypeStruct((4, 16, GQ), BF),
            jax.ShapeDtypeStruct((8, 16, WE), BF),
        ),
        in_specs=[VM] * 3 + [ANY] * 3 + [VM] * 2 + [ANY] * 2,
        out_specs=(VM, ANY, ANY),
        scratch_shapes=[
            pltpu.VMEM((4, ROWS, D), BF),
            pltpu.VMEM((4, ROWS, D), BF),
            pltpu.VMEM((4, 4, 2, 48, WQ), BF),
            pltpu.VMEM((4, 96, 1024), BF),
            pltpu.VMEM((4, 96, WE - 1024), BF),
            pltpu.VMEM((4, ROWS, GROUP_W), BF),
            pltpu.VMEM((4, ROWS, D), BF),
            pltpu.VMEM((4, ROWS, D), BF),
            pltpu.VMEM((4, ROWS, D), BF),
            pltpu.VMEM((4, 4, 2, 48, GQ), BF),
            pltpu.VMEM((4, 4, 48, GQ), BF),
            pltpu.VMEM((4, 4, 48, GQ), BF),
        ]
        + first_scratch(48, GQ, GROUP_W)
        + second_scratch(48, GQ, GROUP_W)
        + second_scratch(96, WE, 1024)
        + [
            pltpu.VMEM((4, 48, GROUP_W), BF),
            pltpu.VMEM((4, 48, GQ - GROUP_W), BF),
            pltpu.VMEM((48, GQ), BF),
            pltpu.VMEM((4, 16, GQ), BF),
            pltpu.VMEM((96, WE), BF),
            pltpu.VMEM((8, 16, WE), BF),
        ]
        + sems(48, 12),
        compiler_params=pltpu.CompilerParams(
            collective_id=8, has_side_effects=True, vmem_limit_bytes=VMEM_LIMIT
        ),
    )(dq, dkv, o, hg, tok, wq, gains, small, we_a, we_b)


def row_pad():
    at = lax.broadcasted_iota(jnp.int32, (16, 12), 0)
    return jnp.where(at == lax.broadcasted_iota(jnp.int32, (16, 12), 1), 1.0, 0.0)


def lane_pick(rows, lane):
    return jnp.where(lax.broadcasted_iota(jnp.int32, (rows, SMALL), 1) == lane, 1.0, 0.0)


def pack_kernel(
    qkv, out_w, router, gain_mlp, gain_attn, gate_up, down, shared_up, shared_down, ids,
    wq, wo, we, used,
):
    pad = row_pad()
    low = pad.astype(BF)

    def padded(value):
        return jnp.dot(low, value.astype(BF), preferred_element_type=F32).astype(BF)

    same = lane_equal(EXPERTS)
    wide = lax.dot_general(router[...].astype(BF), same, COL_COL, preferred_element_type=F32)
    small = jnp.dot(low, wide.astype(BF), preferred_element_type=F32)
    for lane, gain in ((EXPERTS, gain_mlp), (EXPERTS + 1, gain_attn)):
        small = small + jnp.dot(
            (pad * gain[...]).astype(BF),
            lane_pick(12, lane).astype(BF),
            preferred_element_type=F32,
        )
    for g in range(HK):
        wq[g, :, :GROUP_W] = padded(qkv[:, g * GROUP_W : (g + 1) * GROUP_W])
        wq[g, :, GROUP_W:] = small.astype(BF)
    wo[...] = padded(out_w[...])
    for e in range(EXPERTS):
        share = slice(e * FSL, (e + 1) * FSL)
        we[e, :, :FE] = padded(gate_up[:, e, :FE])
        we[e, :, FE:UP] = padded(shared_up[:, share])
        we[e, :, UP : UP + FE] = padded(gate_up[:, e, FE:])
        we[e, :, UP + FE : 2 * UP] = padded(shared_up[:, FS + e * FSL : FS + (e + 1) * FSL])
        we[e, :, 2 * UP : 2 * UP + FE] = padded(down[:, e, :])
        we[e, :, 2 * UP + FE :] = padded(shared_down[:, share])
    expert = lax.broadcasted_iota(jnp.int32, (EXPERTS, ROWS), 0)
    named = expert == ids[0:1, :]
    for k in range(1, 6):
        named = named | (expert == ids[k : k + 1, :])
    used[...] = lax.dot_general(
        jnp.where(named, 1.0, 0.0).astype(BF), same, COL_COL, preferred_element_type=F32
    )


def lane_equal(rows):
    at = lax.broadcasted_iota(jnp.int32, (rows, SMALL), 0)
    return jnp.where(at == lax.broadcasted_iota(jnp.int32, (rows, SMALL), 1), 1.0, 0.0).astype(BF)


def packing(*shards):
    return pl.pallas_call(
        pack_kernel,
        name="pack_shards",
        out_shape=(
            jax.ShapeDtypeStruct((4, 16, WQ), BF),
            jax.ShapeDtypeStruct((16, D), BF),
            jax.ShapeDtypeStruct((8, 16, WE), BF),
            jax.ShapeDtypeStruct((ROWS, SMALL), F32),
        ),
        in_specs=[VM] * 10,
        out_specs=(VM,) * 4,
        compiler_params=pltpu.CompilerParams(vmem_limit_bytes=VMEM_LIMIT),
    )(*shards)


def unpack_kernel(
    dwq, dwe, hidden, out_sum, hidden_grad, norm_grad,
    output, tokens_grad, gain_attn, qkv, out_w, gain_mlp, router, gate_up, down, shared_up,
    shared_down,
):
    output[...] = (hidden[...] + out_sum[...]).astype(BF)
    tokens_grad[...] = hidden_grad[...] + norm_grad[...]
    total = jnp.zeros((16, 16), F32)
    pick = lane_equal(16)
    for g in range(HK):
        qkv[:, g * GROUP_W : (g + 1) * GROUP_W] = dwq[g, :, :GROUP_W].astype(F32)[:12]
        out_w[:, g * QW : (g + 1) * QW] = dwq[g, :, GROUP_W : GROUP_W + QW].astype(F32)[:12]
        total = total + lax.dot_general(
            pick, dwq[g, :, GROUP_W + QW :], ROW_ROW, preferred_element_type=F32
        )
    router[...] = total[:EXPERTS, :12]
    gain_mlp[...] = total[EXPERTS : EXPERTS + 1, :12]
    gain_attn[...] = total[EXPERTS + 1 : EXPERTS + 2, :12]
    for e in range(EXPERTS):
        share = slice(e * FSL, (e + 1) * FSL)
        gate_up[:, e, :FE] = dwe[e, :, :FE].astype(F32)[:12]
        gate_up[:, e, FE:] = dwe[e, :, UP : UP + FE].astype(F32)[:12]
        shared_up[:, share] = dwe[e, :, FE:UP].astype(F32)[:12]
        shared_up[:, FS + e * FSL : FS + (e + 1) * FSL] = (
            dwe[e, :, UP + FE : 2 * UP].astype(F32)[:12]
        )
        down[:, e, :] = dwe[e, :, 2 * UP : 2 * UP + FE].astype(F32)[:12]
        shared_down[:, share] = dwe[e, :, 2 * UP + FE :].astype(F32)[:12]


def unpacking(*values):
    return pl.pallas_call(
        unpack_kernel,
        name="unpack_shards",
        out_shape=(
            jax.ShapeDtypeStruct((ROWS, D), BF),
            jax.ShapeDtypeStruct((ROWS, D), F32),
            jax.ShapeDtypeStruct((1, 12), F32),
            jax.ShapeDtypeStruct((12, QKV), F32),
            jax.ShapeDtypeStruct((12, D), F32),
            jax.ShapeDtypeStruct((1, 12), F32),
            jax.ShapeDtypeStruct((EXPERTS, 12), F32),
            jax.ShapeDtypeStruct((12, EXPERTS, 2 * FE), F32),
            jax.ShapeDtypeStruct((12, EXPERTS, FE), F32),
            jax.ShapeDtypeStruct((12, 2 * FS), F32),
            jax.ShapeDtypeStruct((12, FS), F32),
        ),
        in_specs=[VM] * 6,
        out_specs=(VM,) * 11,
        compiler_params=pltpu.CompilerParams(vmem_limit_bytes=VMEM_LIMIT),
    )(*values)


def per_device(
    tokens,
    seq_bounds,
    expert_ids,
    attn_gain,
    qkv_weight,
    out_weight,
    mlp_gain,
    router_weight,
    expert_gate_up,
    expert_down,
    shared_gate_up,
    shared_down,
    out_cotangent,
):
    wq_pieces, wo_piece, we_pieces, used = packing(
        qkv_weight,
        out_weight.T,
        router_weight.T,
        mlp_gain[None],
        attn_gain[None],
        jnp.transpose(expert_gate_up, (1, 0, 2)),
        jnp.transpose(expert_down, (2, 0, 1)),
        shared_gate_up,
        shared_down.T,
        expert_ids.T,
    )
    fwd = forward(seq_bounds, tokens, wq_pieces, wo_piece, we_pieces, out_cotangent, used)
    dkv_own, dq_all, attn_all, we_a, we_b, hidden_group, out_sum = backward(
        seq_bounds,
        *(fwd[k] for k in ("q", "o", "do", "lse", "kv", "dwe", "hidden_low", "out_parts")),
    )
    norm_grad, dwq_pieces, dwe_pieces = closing(
        dq_all,
        dkv_own,
        attn_all,
        hidden_group,
        *(fwd[k] for k in ("tok", "wq", "gains", "small")),
        we_a,
        we_b,
    )
    (
        output, tokens_grad, attn_gain_out, qkv_out, wo_out, mlp_gain_out, router_out,
        gate_up_out, down_out, shared_out, shared_down_out,
    ) = unpacking(
        dwq_pieces, dwe_pieces, fwd["hidden"], out_sum, fwd["hidden_grad"], norm_grad
    )
    return (
        output,
        tokens_grad,
        attn_gain_out.reshape(12),
        qkv_out,
        wo_out.T,
        mlp_gain_out.reshape(12),
        router_out.T,
        jnp.transpose(gate_up_out, (1, 0, 2)),
        jnp.transpose(down_out, (1, 2, 0)),
        shared_out,
        shared_down_out.T,
    )


def solution(mesh):
    both = ("blk", "head")
    in_specs = (
        P(both, None),
        P(),
        P(both, None),
        P(both),
        P(both, None),
        P(None, both),
        P(both),
        P(both, None),
        P(None, both, None),
        P(None, None, both),
        P(both, None),
        P(None, both),
        P(both, None),
    )
    out_specs = (
        P(both, None),
        P(both, None),
        P(both),
        P(both, None),
        P(None, both),
        P(both),
        P(both, None),
        P(None, both, None),
        P(None, None, both),
        P(both, None),
        P(None, both),
    )
    return jax.shard_map(
        per_device, mesh=mesh, in_specs=in_specs, out_specs=out_specs, check_vma=False
    )
```
